256 devices in a mesh: band: 64 (over x, z, core), wp: 4 (over y).
Axes of the slice: x: 4, y: 4, z: 8, core: 2. Of those that a mesh axis runs over, the one named last changes fastest.
Arguments:
- uv_tiles: bfloat16 [4, 4096, 2, 128, 128], P('wp', 'band'), may hold values from -6 to 6
- target_bands: int32 [4, 4096, 1], P('wp', 'band'), may hold values from 0 to 63; in each aligned block of 64 rows (0 to 63, 64 to 127, ..., all dimensions but the last counted through in order) at most 2 rows name the same one
- uv_offsets: int32 [4, 4096, 2], P('wp', 'band'), may hold values from 0 to 8064, as said below
- tile_counts: int32 [4, 64], P('wp', 'band'), may hold values from 48 to 64, as said below
- plane_w: float32 [4], P('wp'), may hold values from -8 to 8
Outputs:
- stacked_image: float32 [8192, 8192], P('wp', 'band')
The draws below stay inside these ranges and needn't reach their ends.
Inputs may be any that keep to these rules, and one draw needn't show every extreme that they name: `target_bands`: among the 64 slots of one device no band is named more than 2 times. `uv_offsets`: the first entry is at most 0, the second at most 8064; both bounds are reached. `tile_counts`: some device uses all 64 slots.
All inputs are finite; a program needn't handle non-finite values.
Results may differ from the reference program's by a relative error of at most 0.0029.
Values may be sent and summed in bfloat16 or wider, within the bound.
No kernel may reach another device: no remote copies, remote signals or barrier semaphores. Data moves between devices by JAX's collectives and lax.ppermute only.
A program may use at most 128 MiB of HBM per device.

```python
import math
import jax
import jax.numpy as jnp
import numpy as np
from jax import lax

N = 8192
TILE = 128
PLANES_DEV = 1
PLANES = 4
TILES_DEV = 64
TILES = 4096
CAP = 2
N_BAND = 64
N_WP = 4


def draw_uv_offsets(key, part):
    key = jax.random.fold_in(key, 11)
    row_key, col_key, pick_key = jax.random.split(key, 3)
    band_rows = N // N_BAND
    row_part = jax.random.randint(row_key, (N_WP, N_BAND * TILES_DEV), 0, band_rows - TILE + 1)
    col_part = jax.random.randint(col_key, (N_WP, N_BAND * TILES_DEV), 0, N - TILE + 1)
    picks = jax.random.randint(pick_key, (2,), 0, N_BAND) * TILES_DEV
    row_part = row_part.at[0, picks[0]].set(band_rows - TILE)
    col_part = col_part.at[0, picks[1]].set(N - TILE)
    return jnp.stack([row_part, col_part], axis=-1).astype(jnp.int32)


def draw_tile_counts(key, part):
    key = jax.random.fold_in(key, 37)
    count_key, pick_key = jax.random.split(key)
    counts_drawn = jax.random.randint(count_key, (N_WP, N_BAND), 3 * TILES_DEV // 4, TILES_DEV + 1)
    picks = jax.random.randint(pick_key, (2,), 0, N_BAND)
    counts_drawn = counts_drawn.at[picks[0] % N_WP, picks[1]].set(TILES_DEV)
    return counts_drawn.astype(jnp.int32)


def levels(stream_key, dims, pieces, least, top_value):
    loudness, own = 1.0, jax.random.fold_in(stream_key, 6)
    for dim, shards_of in pieces:
        draws = jnp.exp(jax.random.uniform(jax.random.fold_in(own, dim), (shards_of,), jnp.float32, least / len(pieces), top_value / len(pieces)))
        loudness = loudness * jnp.repeat(draws, dims[dim] // shards_of).reshape([-1 if axis == dim else 1 for axis in range(len(dims))])
    return loudness


def deal_out(own_key, own, number, rows, count, top, bound, skew):
    ranking = jax.random.permutation(own_key, count)
    crowded, usual = load_shares(count, rows * top, bound, skew, True), load_shares(count, rows * top, bound, skew, False)
    places = jnp.arange(count)

    def named(sizes, offset_by):
        used = int((sizes > 0).sum())
        fixed = max(1, used // 4)
        moved = fixed + (places - fixed + offset_by * (used - fixed)) % max(1, count - fixed)
        return jnp.zeros((count,), jnp.int32).at[ranking[jnp.where(places < fixed, places, moved)]].set(jnp.asarray(sizes, jnp.int32))

    sizes = jnp.where(number % 4 == 0, named(crowded, number // 4), named(usual, number - number // 4 - 1))
    mixed = jax.random.permutation(jax.random.fold_in(own, 3), count)
    donor, sink = mixed[0:count // 2 * 2:2], mixed[1:count // 2 * 2:2]
    slack = jnp.minimum(sizes[donor] - 1, bound - sizes[sink]) // 2
    slack = jnp.where((donor == ranking[0]) | (sink == ranking[0]) | (sizes[sink] == 0), 0, jnp.maximum(slack, 0))
    moved = jax.random.randint(jax.random.fold_in(own, 4), (count // 2,), 0, 1 << 20) % (slack + 1)
    sizes = sizes.at[donor].add(-moved).at[sink].add(moved)
    labels = jnp.searchsorted(jnp.cumsum(sizes), jnp.arange(rows * top), side="right").astype(jnp.int32)
    listing = labels.reshape(top, rows).T
    listing = listing[jax.random.permutation(jax.random.fold_in(own, 1), rows)]
    offset_by = jax.random.randint(jax.random.fold_in(own, 2), (rows, 1), 0, top)
    return jnp.take_along_axis(listing, (jnp.arange(top)[None, :] + offset_by) % top, axis=1)


def load_shares(amount, total, bound, skew, full):
    weights = [(1 << 20) // math.isqrt(standing ** skew) + 1 for standing in range(1, amount + 1)]
    largest = bound if full else min(bound, max(-(-total // amount), total * weights[0] // sum(weights)))
    least = 1 if total - largest >= amount - 1 else 0
    holding, surplus = [largest] + [least] * (amount - 1), total - largest - least * (amount - 1)
    while surplus > 0:
        free = [i for i in range(1, amount) if holding[i] < largest] or [i for i in range(1, amount) if holding[i] < bound]
        mass, left = sum([weights[i] for i in free]), surplus
        for i in free:
            addition = min(bound - holding[i], max(1, left * weights[i] // mass), surplus)
            holding[i] = holding[i] + addition
            surplus = surplus - addition
    return np.array(holding)


def noise(rng, extent, spread, reach, cuts=(), kind=jnp.bfloat16):
    result = spread * jax.random.normal(rng, extent, jnp.float32)
    if cuts:
        result = result * levels(rng, extent, cuts, -0.22, 0.18)
    return jnp.clip(result, -reach, reach).astype(kind)


def setup_inputs(seed: int = 0) -> dict:
    splits = jax.random.split(jax.random.key(seed), 6)
    uv_tiles = noise(splits[0], (N_WP, TILES, 2, TILE, TILE), 1.0, 6.0, ((0, 4), (1, 64)))
    target_bands_keys = jax.random.split(jax.random.fold_in(splits[1], 1), N_WP * TILES // TILES_DEV)
    target_bands_turns = jax.random.permutation(jax.random.fold_in(splits[1], 3), N_WP * TILES // TILES_DEV)
    target_bands = jax.vmap(lambda own, number: deal_out(jax.random.fold_in(splits[1], 2), own, number, TILES_DEV, N_BAND, 1, CAP, 2))(target_bands_keys, target_bands_turns).reshape((N_WP, TILES, 1))
    uv_offsets = draw_uv_offsets(jax.random.fold_in(splits[5], 71), 0)
    tile_counts = draw_tile_counts(jax.random.fold_in(splits[5], 71), 0)
    plane_w = jnp.clip(jax.random.uniform(splits[4], (PLANES,), jnp.float32, -8.0, 8.0) * levels(splits[4], (PLANES,), ((0, 4),), -0.4, 0.0), -8.0, 8.0)
    return dict(uv_tiles=uv_tiles, target_bands=target_bands, uv_offsets=uv_offsets, tile_counts=tile_counts, plane_w=plane_w)


def reference(uv_tiles, target_bands, uv_offsets, tile_counts, plane_w):
    band_rows = N // N_BAND
    position = jnp.arange(N_BAND * TILES_DEV, dtype=jnp.int32)
    owner = position // TILES_DEV
    in_use = (position % TILES_DEV)[None, :] < tile_counts[:, owner]
    row_start = (target_bands[:, :, 0] * band_rows + uv_offsets[:, :, 0]).astype(jnp.int32)
    col_start = uv_offsets[:, :, 1].astype(jnp.int32)
    centred = (jnp.arange(N, dtype=jnp.float32) - N // 2) / N
    radius = centred[:, None] ** 2 + centred[None, :] ** 2
    w_term = -radius / (1.0 + jnp.sqrt(1.0 - radius))

    def one_plane(stacked, plane_index):
        group = (plane_index // PLANES_DEV).astype(jnp.int32)
        group_tiles = lax.dynamic_index_in_dim(uv_tiles, group, 0, keepdims=False)
        group_use = lax.dynamic_index_in_dim(in_use, group, 0, keepdims=False)
        group_rows = lax.dynamic_index_in_dim(row_start, group, 0, keepdims=False)
        group_cols = lax.dynamic_index_in_dim(col_start, group, 0, keepdims=False)

        def add_tile(number, uv_grid):
            weight = group_use[number].astype(jnp.float32)
            addend = group_tiles[number].astype(jnp.float32) * weight
            corner = (jnp.int32(0), group_rows[number], group_cols[number])
            current = lax.dynamic_slice(uv_grid, corner, (2, TILE, TILE))
            return lax.dynamic_update_slice(uv_grid, current + addend, corner)
        uv_grid = lax.fori_loop(0, N_BAND * TILES_DEV, add_tile, jnp.zeros((2, N, N), jnp.float32))
        row_spectrum = jnp.fft.ifft(lax.complex(uv_grid[0], uv_grid[1]), axis=1) * N
        real_low = jnp.real(row_spectrum).astype(jnp.bfloat16)
        imag_low = jnp.imag(row_spectrum).astype(jnp.bfloat16)
        real_low, imag_low = lax.optimization_barrier((real_low, imag_low))
        rounded = lax.complex(real_low.astype(jnp.float32), imag_low.astype(jnp.float32))
        sky_image = jnp.fft.ifft(rounded, axis=0)
        phase_angle = 2.0 * math.pi * plane_w[plane_index] * w_term
        stacked = stacked + (jnp.real(sky_image) * jnp.cos(phase_angle) - jnp.imag(sky_image) * jnp.sin(phase_angle))
        return (stacked, None)
    stacked, _ = lax.scan(one_plane, jnp.zeros((N, N), jnp.float32), jnp.arange(PLANES, dtype=jnp.int32))
    return stacked
```

```python
import functools
import math

import jax
import jax.numpy as jnp
import ml_dtypes
import numpy as np
from jax import lax
from jax.experimental import pallas as pl
from jax.experimental.pallas import tpu as pltpu
from jax.sharding import PartitionSpec as P

N = 8192
BANDS = 64
EDGE = 128
SLOTS = 64
HALF = 64
ROWS = 8192
F32 = jnp.float32
BF16 = jnp.bfloat16
VMEM_LIMIT = 56 * 1024 * 1024


def circle(numerator, length):
    angle = 2.0 * np.pi * (np.asarray(numerator) % length) / length
    return np.cos(angle), np.sin(angle)


def split(table):
    high = table.astype(ml_dtypes.bfloat16)
    low = (table - high.astype(np.float64)).astype(ml_dtypes.bfloat16)
    return high, low


def row_first_table():
    cosine, sine = circle(np.arange(64)[:, None] * np.arange(64)[None, :], 64)
    table = np.zeros((2, 64, 64, 2))
    table[0, :, :, 0] = cosine
    table[0, :, :, 1] = -sine
    table[1, :, :, 0] = sine
    table[1, :, :, 1] = cosine
    high, low = split(table.reshape(128, 128))
    return np.concatenate([high, high, low], axis=1)


def row_twiddles():
    cosine, sine = circle(np.arange(128)[:, None] * np.arange(128)[None, :], N)
    return np.stack([cosine, sine]).astype(np.float32)


def row_second_table():
    cosine, sine = circle(np.arange(64)[:, None] * np.arange(128)[None, :], 64)
    table = np.block([[cosine, -sine], [sine, cosine]])
    high, low = split(table)
    return np.concatenate([high, low], axis=0)


def column_first_table():
    rows = np.arange(128)[:, None, None]
    k = np.arange(64)[None, :, None]
    band = np.arange(64)[None, None, :]
    cosine, sine = circle(k * (128 * band + rows), N)
    table = np.concatenate(
        [np.concatenate([cosine, -sine], axis=2), np.concatenate([sine, cosine], axis=2)], axis=1
    )
    high, low = split(table)
    return np.concatenate([high, low], axis=2)


def column_second_table():
    cosine, sine = circle(np.arange(128)[:, None] * np.arange(128)[None, :], 128)
    table = np.zeros((2, 128, 2, 2, 64))
    cosine = cosine.reshape(128, 2, 64) / N
    sine = sine.reshape(128, 2, 64) / N
    table[0, :, :, 0] = cosine
    table[0, :, :, 1] = -sine
    table[1, :, :, 0] = sine
    table[1, :, :, 1] = cosine
    high, low = split(table.reshape(256, 256))
    return np.concatenate([high, high, low], axis=1)


def pack_kernel(shift_ref, used_ref, tiles_ref, out_ref, rows_ref, *, per_step):
    step = pl.program_id(0)

    def one(index, carry):
        slot = step * per_step + index
        shift = shift_ref[slot]
        keep = used_ref[slot] > 0
        for part in range(2):
            block = tiles_ref[index, part].astype(F32)
            block = jnp.where(keep, pltpu.roll(block, shift, 1), 0.0)
            rows_ref[pl.ds(slot * 2 + part, HALF, stride=128), :] = block
        return carry

    lax.fori_loop(0, per_step, one, 0, unroll=2)

    @pl.when(step == pl.num_programs(0) - 1)
    def _():
        def cast(index, carry):
            where = pl.ds(pl.multiple_of(index * 128, 128), 128)
            out_ref[where, :] = rows_ref[where, :].astype(BF16)
            return carry

        lax.fori_loop(0, ROWS // 128, cast, 0)


def pack(shift, used, tiles, half):
    per_step = 8
    return pl.pallas_call(
        functools.partial(pack_kernel, per_step=per_step),
        grid=(SLOTS // per_step,),
        in_specs=[
            pl.BlockSpec(memory_space=pltpu.SMEM),
            pl.BlockSpec(memory_space=pltpu.SMEM),
            pl.BlockSpec((per_step, 2, HALF, 128), lambda i: (i, 0, half, 0)),
        ],
        out_specs=pl.BlockSpec((ROWS, 128), lambda i: (0, 0)),
        out_shape=jax.ShapeDtypeStruct((ROWS, 128), BF16),
        scratch_shapes=[pltpu.VMEM((ROWS, 128), F32)],
        compiler_params=pltpu.CompilerParams(vmem_limit_bytes=VMEM_LIMIT),
        cost_estimate=pl.CostEstimate(flops=8 * 1024 * 1024, bytes_accessed=4 << 20, transcendentals=0),
        name="pack_rows",
    )(shift, used, tiles)


def grid_kernel(
    place_ref, pieces_ref, first_ref, twiddle_ref, second_ref, out_ref, grid_a, grid_b, rows_ref
):
    def clear(index, carry):
        where = pl.ds(pl.multiple_of(index * 64, 64), 64)
        grid_a[where, :] = jnp.zeros((64, 128), F32)
        grid_b[where, :] = jnp.zeros((64, 128), F32)
        return carry

    lax.fori_loop(0, ROWS // 64, clear, 0)
    grid_a[pl.ds(ROWS, 8), :] = jnp.zeros((8, 128), F32)
    grid_b[pl.ds(ROWS, 8), :] = jnp.zeros((8, 128), F32)

    sublane = lax.broadcasted_iota(jnp.int32, (8, 128), 0)
    lane = lax.broadcasted_iota(jnp.int32, (8, 128), 1)
    position = lane + (sublane // 2) * 128
    upper = sublane < 2

    def place(index, carry):
        pieces = pieces_ref[pl.ds(pl.multiple_of(index * 16, 16), 16), :].astype(F32)
        for part in range(2):
            block = pieces[8 * part : 8 * part + 8]
            turned = [block] + [pltpu.roll(block, 8 - 2 * turn, 0) for turn in (1, 2, 3)]
            for piece in range(4):
                both = jnp.where(upper, turned[piece], turned[(piece + 3) % 4])
                packed = place_ref[index * 8 + part * 4 + piece]
                shift = packed & 127
                row = packed >> 7
                offset = position - shift
                inside = (offset >= 0) & (offset < 128)
                grid = grid_a if piece % 2 == 0 else grid_b
                window = pl.ds(row, 8)
                grid[window, :] = grid[window, :] + jnp.where(inside, both, 0.0)
        return carry

    lax.fori_loop(0, BANDS * SLOTS // 8, place, 0)

    first = first_ref[...]
    second = second_ref[...]
    cosine = twiddle_ref[0]
    sine = twiddle_ref[1]

    def band_step(band, carry):
        where = pl.ds(pl.multiple_of(band * 128, 128), 128)
        cells = grid_a[where, :] + grid_b[where, :]
        high = cells.astype(BF16)
        low = (cells - high.astype(F32)).astype(BF16)
        section = jnp.dot(
            first, jnp.concatenate([high, low, high], axis=0), preferred_element_type=F32
        )
        real = jnp.concatenate([section[:64], section[:64]], axis=0)
        imag = jnp.concatenate([section[64:], section[64:]], axis=0)
        turned = jnp.concatenate(
            [real * cosine - imag * sine, real * sine + imag * cosine], axis=1
        )
        high = turned.astype(BF16)
        low = (turned - high.astype(F32)).astype(BF16)
        contract = (((1,), (1,)), ((), ()))
        main = lax.dot_general(second, high, contract, preferred_element_type=F32)
        rest = lax.dot_general(second[:128], low, contract, preferred_element_type=F32)
        spectrum = main[:128] + main[128:] + rest
        rows_ref[pl.ds(band, 64, stride=128), :] = spectrum[:64]
        rows_ref[pl.ds(64 + band, 64, stride=128), :] = spectrum[64:]
        return carry

    lax.fori_loop(0, BANDS, band_step, 0, unroll=2)

    def cast(index, carry):
        where = pl.ds(pl.multiple_of(index * 128, 128), 128)
        out_ref[where, :] = rows_ref[where, :].astype(BF16)
        return carry

    lax.fori_loop(0, ROWS // 128, cast, 0)


def grid_and_rows(places, pieces, first, twiddle, second):
    vmem = pl.BlockSpec(memory_space=pltpu.VMEM)
    return pl.pallas_call(
        grid_kernel,
        in_specs=[pl.BlockSpec(memory_space=pltpu.SMEM), vmem, vmem, vmem, vmem],
        out_specs=vmem,
        out_shape=jax.ShapeDtypeStruct((ROWS, 128), BF16),
        scratch_shapes=[
            pltpu.VMEM((ROWS + 8, 128), F32),
            pltpu.VMEM((ROWS + 8, 128), F32),
            pltpu.VMEM((ROWS, 128), F32),
        ],
        compiler_params=pltpu.CompilerParams(vmem_limit_bytes=VMEM_LIMIT),
        cost_estimate=pl.CostEstimate(flops=20_000_000_000, bytes_accessed=4 << 20, transcendentals=0),
        name="place_and_row_transform",
    )(places, pieces, first, twiddle, second)


def column_first_kernel(rows_ref, table_ref, out_ref):
    for index in range(rows_ref.shape[0]):
        source = pl.program_id(0) * rows_ref.shape[0] + index
        rows = rows_ref[index]
        section = jnp.dot(
            table_ref[index], jnp.concatenate([rows, rows], axis=0), preferred_element_type=F32
        )
        out_ref[pl.ds(source, 64, stride=128), :] = section[:64]
        out_ref[pl.ds(64 + source, 64, stride=128), :] = section[64:]


def column_first(rows, table, half):
    per_step = 8
    steps = 64 // per_step
    return pl.pallas_call(
        column_first_kernel,
        grid=(steps,),
        in_specs=[
            pl.BlockSpec((per_step, 128, 128), lambda i: (i, 0, 0)),
            pl.BlockSpec((per_step, 128, 256), lambda i: (i + half * steps, 0, 0)),
        ],
        out_specs=pl.BlockSpec((ROWS, 128), lambda i: (0, 0)),
        out_shape=jax.ShapeDtypeStruct((ROWS, 128), F32),
        compiler_params=pltpu.CompilerParams(vmem_limit_bytes=VMEM_LIMIT),
        cost_estimate=pl.CostEstimate(flops=2_000_000_000, bytes_accessed=10 << 20, transcendentals=0),
        name="column_transform_over_bands",
    )(rows, table)


def column_second_kernel(first_ref, later_ref, table_ref, cosine_ref, sine_ref, out_ref):
    table = table_ref[...]
    for index in range(first_ref.shape[0]):
        cells = jnp.concatenate([first_ref[index], later_ref[index]], axis=0)
        high = cells.astype(BF16)
        low = (cells - high.astype(F32)).astype(BF16)
        sky = jnp.dot(
            table, jnp.concatenate([high, low, high], axis=0), preferred_element_type=F32
        )
        image = sky[:128] * cosine_ref[index] - sky[128:] * sine_ref[index]
        out_ref[:, index] = image.astype(BF16).reshape(4, 32, 128)


def column_second(first, later, table, cosine, sine, part, parts):
    per_step = 8
    count = 64 // parts
    steps = count // per_step
    block = pl.BlockSpec((per_step, 128, 128), lambda i: (i + part * steps, 0, 0))
    return pl.pallas_call(
        column_second_kernel,
        grid=(steps,),
        in_specs=[block, block, pl.BlockSpec((256, 768), lambda i: (0, 0)), block, block],
        out_specs=pl.BlockSpec((4, per_step, 32, 128), lambda i: (0, i, 0, 0)),
        out_shape=jax.ShapeDtypeStruct((4, count, 32, 128), BF16),
        compiler_params=pltpu.CompilerParams(vmem_limit_bytes=VMEM_LIMIT),
        cost_estimate=pl.CostEstimate(
            flops=6_000_000_000 // parts, bytes_accessed=(18 << 20) // parts, transcendentals=0
        ),
        name="column_transform_over_rows",
    )(first, later, table, cosine, sine)


def sum_kernel(*refs):
    out_ref = refs[-1]
    parts = len(refs) - 1
    count = 64 // parts
    for part in range(parts):

        def one(k, carry):
            total = refs[part][0, k].astype(F32)
            for plane in range(1, 4):
                total = total + refs[part][plane, k].astype(F32)
            out_ref[pl.ds(part * count + k, 32, stride=64), :] = total
            return carry

        lax.fori_loop(0, count, one, 0, unroll=2)


def window_sum(blocks):
    vmem = pl.BlockSpec(memory_space=pltpu.VMEM)
    return pl.pallas_call(
        sum_kernel,
        in_specs=[vmem] * len(blocks),
        out_specs=vmem,
        out_shape=jax.ShapeDtypeStruct((2048, 128), F32),
        compiler_params=pltpu.CompilerParams(vmem_limit_bytes=VMEM_LIMIT),
        cost_estimate=pl.CostEstimate(flops=1 << 20, bytes_accessed=3 << 20, transcendentals=0),
        name="window_sum",
    )(*blocks)


def w_phases(plane_w):
    k = jnp.arange(64, dtype=jnp.int32)[:, None, None]
    j = jnp.arange(128, dtype=jnp.int32)[None, :, None]
    column = lax.axis_index("band") * 128 + jnp.arange(128, dtype=jnp.int32)[None, None, :]
    x = ((64 * j + k).astype(F32) - N // 2) / N
    y = (column.astype(F32) - N // 2) / N
    radius = x**2 + y**2
    angle = 2.0 * math.pi * plane_w * (jnp.sqrt(1.0 - radius) - 1.0)
    return jnp.cos(angle), jnp.sin(angle)


def local(uv_tiles, target_bands, uv_offsets, tile_counts, plane_w):
    tiles = uv_tiles[0]
    used = (jnp.arange(SLOTS, dtype=jnp.int32) < tile_counts[0, 0]).astype(jnp.int32)
    column = uv_offsets[0, :, 1]
    shift = column % 128
    row = (target_bands[0, :, 0] * 64 + column // 128) * 2
    places = lax.all_gather(row * 128 + shift, "band", axis=0, tiled=True)

    first = jnp.asarray(row_first_table())
    twiddle = jnp.asarray(row_twiddles())
    second = jnp.asarray(row_second_table())
    column_table = jnp.asarray(column_first_table())
    last_table = jnp.asarray(column_second_table())

    sections = []
    for half in range(2):
        packed = pack(shift, used, tiles, half)
        arrived = lax.all_to_all(
            packed.reshape(64, 128, 128), "band", split_axis=0, concat_axis=0, tiled=True
        )
        spectrum = grid_and_rows(places, arrived.reshape(ROWS, 128), first, twiddle, second)
        columns = lax.all_to_all(
            spectrum.reshape(64, 128, 128), "band", split_axis=0, concat_axis=0, tiled=True
        )
        sections.append(column_first(columns, column_table, half).reshape(64, 128, 128))

    cosine, sine = w_phases(plane_w[0])
    parts = 2
    blocks = []
    for part in range(parts):
        image = column_second(sections[0], sections[1], last_table, cosine, sine, part, parts)
        blocks.append(lax.all_to_all(image, "wp", split_axis=0, concat_axis=0, tiled=True))
    return window_sum(blocks)


def solution(mesh):
    placed = (
        P("wp", "band", None, None, None),
        P("wp", "band", None),
        P("wp", "band", None),
        P("wp", "band"),
        P("wp"),
    )
    return jax.shard_map(
        local, mesh=mesh, in_specs=placed, out_specs=P("wp", "band"), check_vma=False
    )
```

```python
import functools
import math

import jax
import jax.numpy as jnp
import ml_dtypes
import numpy as np
from jax import lax
from jax.experimental import pallas as pl
from jax.experimental.pallas import tpu as pltpu
from jax.sharding import PartitionSpec as P

N = 8192
BANDS = 64
EDGE = 128
SLOTS = 64
ROWS = 8192
STRIDE = 129
F32 = jnp.float32
BF16 = jnp.bfloat16
VMEM_LIMIT = 56 * 1024 * 1024


def circle(numerator, length):
    angle = 2.0 * np.pi * (np.asarray(numerator) % length) / length
    return np.cos(angle), np.sin(angle)


def split(table):
    high = table.astype(ml_dtypes.bfloat16)
    low = (table - high.astype(np.float64)).astype(ml_dtypes.bfloat16)
    return high, low


def row_first_table():
    cosine, sine = circle(np.arange(64)[:, None] * np.arange(64)[None, :], 64)
    table = np.zeros((2, 64, 64, 2))
    table[0, :, :, 0] = cosine
    table[0, :, :, 1] = -sine
    table[1, :, :, 0] = sine
    table[1, :, :, 1] = cosine
    high, low = split(table.reshape(128, 128))
    return np.concatenate([high, high, low], axis=1)


def row_twiddles():
    cosine, sine = circle(np.arange(128)[:, None] * np.arange(128)[None, :], N)
    return np.stack([cosine, sine]).astype(np.float32)


def row_second_table():
    cosine, sine = circle(np.arange(64)[:, None] * np.arange(128)[None, :], 64)
    table = np.block([[cosine, -sine], [sine, cosine]])
    high, low = split(table)
    return np.concatenate([high, low], axis=0)


def column_second_table():
    cosine, sine = circle(np.arange(128)[:, None] * np.arange(128)[None, :], 128)
    table = np.zeros((2, 128, 2, 2, 64))
    cosine = cosine.reshape(128, 2, 64) / N
    sine = sine.reshape(128, 2, 64) / N
    table[0, :, :, 0] = cosine
    table[0, :, :, 1] = -sine
    table[1, :, :, 0] = sine
    table[1, :, :, 1] = cosine
    high, low = split(table.reshape(256, 256))
    return np.concatenate([high, low], axis=1)


def pack_kernel(count_ref, offset_ref, tiles_ref, out_ref, rows_ref, *, per_step):
    step = pl.program_id(0)

    def one(index, carry):
        slot = step * per_step + index
        shift = offset_ref[slot, 1] & 127
        keep = slot < count_ref[0, 0]
        for part in range(2):
            block = tiles_ref[index, part].astype(F32)
            block = jnp.where(keep, pltpu.roll(block, shift, 1), 0.0)
            rows_ref[pl.ds(slot * 2 + part, 64, stride=STRIDE), :] = block
        return carry

    lax.fori_loop(0, per_step, one, 0, unroll=4)

    @pl.when(step == pl.num_programs(0) - 1)
    def _():
        def cast(index, carry):
            rows = rows_ref[pl.ds(index * STRIDE, 128), :].astype(BF16)
            out_ref[pl.ds(pl.multiple_of(index * 128, 128), 128), :] = rows
            return carry

        lax.fori_loop(0, 64, cast, 0, unroll=2)


def pack(count, offsets, tiles, half):
    per_step = 8
    return pl.pallas_call(
        functools.partial(pack_kernel, per_step=per_step),
        grid=(SLOTS // per_step,),
        in_specs=[
            pl.BlockSpec(memory_space=pltpu.SMEM),
            pl.BlockSpec(memory_space=pltpu.SMEM),
            pl.BlockSpec((per_step, 2, 64, 128), lambda i: (i, 0, half, 0)),
        ],
        out_specs=pl.BlockSpec((ROWS, 128), lambda i: (0, 0)),
        out_shape=jax.ShapeDtypeStruct((ROWS, 128), BF16),
        scratch_shapes=[pltpu.VMEM((64 * STRIDE, 128), F32)],
        compiler_params=pltpu.CompilerParams(vmem_limit_bytes=VMEM_LIMIT),
        cost_estimate=pl.CostEstimate(flops=8 << 20, bytes_accessed=4 << 20, transcendentals=0),
        name="pack_rows",
    )(count, offsets, tiles)


def grid_kernel(
    place_ref, me_ref, pieces_ref, first_ref, twiddle_ref, second_ref, bands_ref, out_ref,
    grid_a, grid_b, rows_ref,
):
    def clear(index, carry):
        where = pl.ds(pl.multiple_of(index * 64, 64), 64)
        grid_a[where, :] = jnp.zeros((64, 128), F32)
        grid_b[where, :] = jnp.zeros((64, 128), F32)
        return carry

    lax.fori_loop(0, ROWS // 64, clear, 0)
    grid_a[pl.ds(ROWS, 8), :] = jnp.zeros((8, 128), F32)
    grid_b[pl.ds(ROWS, 8), :] = jnp.zeros((8, 128), F32)

    me = me_ref[0]
    sublane = lax.broadcasted_iota(jnp.int32, (8, 128), 0)
    lane = lax.broadcasted_iota(jnp.int32, (8, 128), 1)
    position = lane + (sublane // 2) * 128
    upper = sublane < 2

    def place(index, carry):
        pieces = pieces_ref[pl.ds(pl.multiple_of(index * 16, 16), 16), :].astype(F32)
        source = ((index // 8 - me) & 63) * 64 + (index & 7) * 8
        for part in range(2):
            block = pieces[8 * part : 8 * part + 8]
            turned = [block] + [pltpu.roll(block, 8 - 2 * turn, 0) for turn in (1, 2, 3)]
            for piece in range(4):
                both = jnp.where(upper, turned[piece], turned[(piece + 3) % 4])
                packed = place_ref[source + part * 4 + piece]
                shift = packed & 127
                row = packed >> 7
                offset = position - shift
                inside = (offset >= 0) & (offset < 128)
                grid = grid_a if piece % 2 == 0 else grid_b
                window = pl.ds(row, 8)
                grid[window, :] = grid[window, :] + jnp.where(inside, both, 0.0)
        return carry

    lax.fori_loop(0, BANDS * SLOTS // 8, place, 0)

    first = first_ref[...]
    second = second_ref[...]
    cosine = twiddle_ref[0]
    sine = twiddle_ref[1]

    def band_step(band, carry):
        where = pl.ds(pl.multiple_of(band * 128, 128), 128)
        cells = grid_a[where, :] + grid_b[where, :]
        high = cells.astype(BF16)
        low = (cells - high.astype(F32)).astype(BF16)
        section = jnp.dot(
            first, jnp.concatenate([high, low, high], axis=0), preferred_element_type=F32
        )
        real = jnp.concatenate([section[:64], section[:64]], axis=0)
        imag = jnp.concatenate([section[64:], section[64:]], axis=0)
        turned = jnp.concatenate(
            [real * cosine - imag * sine, real * sine + imag * cosine], axis=1
        )
        high = turned.astype(BF16)
        low = (turned - high.astype(F32)).astype(BF16)
        contract = (((1,), (1,)), ((), ()))
        main = lax.dot_general(second, high, contract, preferred_element_type=F32)
        rest = lax.dot_general(second[:128], low, contract, preferred_element_type=F32)
        spectrum = main[:128] + main[128:] + rest
        rows_ref[pl.ds(band, 64, stride=STRIDE), :] = spectrum[:64]
        rows_ref[pl.ds(64 + band, 64, stride=STRIDE), :] = spectrum[64:]
        return carry

    lax.fori_loop(0, BANDS, band_step, 0, unroll=2)

    table = bands_ref[...]

    def block_step(index, carry):
        rows = rows_ref[pl.ds(index * STRIDE, 128), :].astype(BF16)
        section = jnp.dot(table, jnp.concatenate([rows, rows], axis=0), preferred_element_type=F32)
        out_ref[pl.ds(pl.multiple_of(index * 128, 128), 128), :] = section.astype(BF16)
        return carry

    lax.fori_loop(0, 64, block_step, 0, unroll=2)


def grid_and_rows(places, me, pieces, first, twiddle, second, bands):
    vmem = pl.BlockSpec(memory_space=pltpu.VMEM)
    smem = pl.BlockSpec(memory_space=pltpu.SMEM)
    return pl.pallas_call(
        grid_kernel,
        in_specs=[smem, smem, vmem, vmem, vmem, vmem, vmem],
        out_specs=vmem,
        out_shape=jax.ShapeDtypeStruct((ROWS, 128), BF16),
        scratch_shapes=[
            pltpu.VMEM((ROWS + 8, 128), F32),
            pltpu.VMEM((ROWS + 8, 128), F32),
            pltpu.VMEM((64 * STRIDE, 128), F32),
        ],
        compiler_params=pltpu.CompilerParams(vmem_limit_bytes=VMEM_LIMIT),
        cost_estimate=pl.CostEstimate(flops=20_000_000_000, bytes_accessed=4 << 20, transcendentals=0),
        name="place_and_transform",
    )(places, me, pieces, first, twiddle, second, bands)


def column_kernel(early_ref, late_ref, table_ref, cosine_ref, sine_ref, own_ref, *sent):
    table = table_ref[...]
    count = early_ref.shape[0]
    late = jnp.swapaxes(late_ref[...], 0, 1).reshape(count, 128, 128)
    for index in range(count):
        cells = jnp.concatenate([early_ref[index], late[index]], axis=0)
        sky = jnp.dot(table, jnp.concatenate([cells, cells], axis=0), preferred_element_type=F32)
        image = sky[:128] * cosine_ref[index] - sky[128:] * sine_ref[index]
        own_ref[index] = image[:32]
        for step in range(3):
            sent[step][index] = image[32 * step + 32 : 32 * step + 64].astype(BF16)


def column_transform(early, late, table, cosine, sine, begin, count):
    per_step = 8
    skip = begin // per_step
    block = pl.BlockSpec((per_step, 128, 128), lambda i: (i + skip, 0, 0))
    result = pl.BlockSpec((per_step, 32, 128), lambda i: (i, 0, 0))
    return pl.pallas_call(
        column_kernel,
        grid=(count // per_step,),
        in_specs=[
            block,
            pl.BlockSpec((64, 2 * per_step, 128), lambda i: (0, i + skip, 0)),
            pl.BlockSpec((256, 512), lambda i: (0, 0)),
            block,
            block,
        ],
        out_specs=[result] * 4,
        out_shape=[jax.ShapeDtypeStruct((count, 32, 128), F32)]
        + [jax.ShapeDtypeStruct((count, 32, 128), BF16)] * 3,
        compiler_params=pltpu.CompilerParams(vmem_limit_bytes=VMEM_LIMIT),
        cost_estimate=pl.CostEstimate(
            flops=count * 70_000_000, bytes_accessed=count * (200 << 10), transcendentals=0
        ),
        name="column_transform",
    )(early, late, table, cosine, sine)


def sum_kernel(*refs, counts):
    out_ref = refs[-1]
    begin = 0
    for part, count in enumerate(counts):
        own, *others = refs[4 * part : 4 * part + 4]
        for group in range(0, count, 8):
            total = own[group : group + 8]
            for other in others:
                total = total + other[group : group + 8].astype(F32)
            out_ref[:, begin + group : begin + group + 8, :] = jnp.swapaxes(total, 0, 1)
        begin += count


def window_sum(parts, counts):
    vmem = pl.BlockSpec(memory_space=pltpu.VMEM)
    flat = [block for part in parts for block in part]
    return pl.pallas_call(
        functools.partial(sum_kernel, counts=counts),
        in_specs=[vmem] * len(flat),
        out_specs=vmem,
        out_shape=jax.ShapeDtypeStruct((32, 64, 128), F32),
        compiler_params=pltpu.CompilerParams(vmem_limit_bytes=VMEM_LIMIT),
        cost_estimate=pl.CostEstimate(flops=1 << 20, bytes_accessed=3 << 20, transcendentals=0),
        name="window_sum",
    )(*flat)


def w_phases(plane_w, turn):
    k = jnp.arange(64, dtype=jnp.int32)[:, None, None]
    j = (jnp.arange(128, dtype=jnp.int32)[None, :, None] + 32 * turn) % 128
    column = lax.axis_index("band") * 128 + jnp.arange(128, dtype=jnp.int32)[None, None, :]
    x = ((64 * j + k).astype(F32) - N // 2) / N
    y = (column.astype(F32) - N // 2) / N
    radius = x**2 + y**2
    angle = 2.0 * math.pi * plane_w * (jnp.sqrt(1.0 - radius) - 1.0)
    return jnp.cos(angle), jnp.sin(angle)


def band_table(row):
    k = jnp.arange(64, dtype=jnp.int32)[:, None]
    band = jnp.arange(64, dtype=jnp.int32)[None, :]
    angle = (2.0 * math.pi / N) * ((k * (128 * band + row)) % N).astype(F32)
    cosine = jnp.cos(angle)
    sine = jnp.sin(angle)
    real = jnp.concatenate([cosine, -sine], axis=1)
    imag = jnp.concatenate([sine, cosine], axis=1)
    table = jnp.stack([real, imag], axis=1).reshape(128, 128)
    high = table.astype(BF16)
    low = (table - high.astype(F32)).astype(BF16)
    return jnp.concatenate([high, low], axis=1)


def gather_places(place):
    held = place
    reach = 1
    while reach < BANDS:
        pairs = [(source, (source - reach) % BANDS) for source in range(BANDS)]
        held = jnp.concatenate([held, lax.ppermute(held, "band", pairs)])
        reach *= 2
    return held


def local(uv_tiles, target_bands, uv_offsets, tile_counts, plane_w):
    tiles = uv_tiles[0]
    offsets = uv_offsets[0]
    me = lax.axis_index("band")
    turn = lax.axis_index("wp")
    column = offsets[:, 1]
    place = (target_bands[0, :, 0] * 64 + column // 128) * 256 + column % 128
    places = gather_places(place)

    first = jnp.asarray(row_first_table())
    twiddle = jnp.asarray(row_twiddles())
    second = jnp.asarray(row_second_table())

    arrived = []
    for half in range(2):
        packed = pack(tile_counts, offsets, tiles, half)
        arrived.append(
            lax.all_to_all(
                packed.reshape(64, 128, 128), "band", split_axis=0, concat_axis=0, tiled=True
            ).reshape(ROWS, 128)
        )
    columns = []
    for half in range(2):
        spectrum = grid_and_rows(
            places, me[None], arrived[half], first, twiddle, second, band_table(me + 64 * half)
        )
        columns.append(
            lax.all_to_all(
                spectrum.reshape(64, 128, 128), "band", split_axis=0, concat_axis=0, tiled=True
            )
        )
    early = jnp.swapaxes(columns[0], 0, 1).reshape(64, 128, 128)

    cosine, sine = w_phases(plane_w[0], turn)
    table = jnp.roll(jnp.asarray(column_second_table()).reshape(2, 128, 512), -32 * turn, axis=1)
    table = table.reshape(256, 512)
    counts = (32, 32)
    parts = []
    begin = 0
    for count in counts:
        own, *sent = column_transform(early, columns[1], table, cosine, sine, begin, count)
        moved = [
            lax.ppermute(block, "wp", [(plane, (plane + step + 1) % 4) for plane in range(4)])
            for step, block in enumerate(sent)
        ]
        parts.append([own, *moved])
        begin += count
    return window_sum(parts, counts).reshape(2048, 128)


def solution(mesh):
    placed = (
        P("wp", "band", None, None, None),
        P("wp", "band", None),
        P("wp", "band", None),
        P("wp", "band"),
        P("wp"),
    )
    return jax.shard_map(
        local, mesh=mesh, in_specs=placed, out_specs=P("wp", "band"), check_vma=False
    )
```

```python
import functools
import math

import jax
import jax.numpy as jnp
import ml_dtypes
import numpy as np
from jax import lax
from jax.experimental import pallas as pl
from jax.experimental.pallas import tpu as pltpu
from jax.sharding import PartitionSpec as P

N = 8192
BANDS = 64
EDGE = 128
SLOTS = 64
ROWS = 8192
STRIDE = 129
F32 = jnp.float32
BF16 = jnp.bfloat16
MIB = 1 << 20


def circle(numerator, length):
    angle = 2.0 * np.pi * (np.asarray(numerator) % length) / length
    return np.cos(angle), np.sin(angle)


def split(table):
    high = table.astype(ml_dtypes.bfloat16)
    low = (table - high.astype(np.float64)).astype(ml_dtypes.bfloat16)
    return high, low


def row_first_table():
    cosine, sine = circle(np.arange(64)[:, None] * np.arange(64)[None, :], 64)
    table = np.zeros((2, 64, 64, 2))
    table[0, :, :, 0] = cosine
    table[0, :, :, 1] = -sine
    table[1, :, :, 0] = sine
    table[1, :, :, 1] = cosine
    high, low = split(table.reshape(128, 128))
    return np.concatenate([high, high, low], axis=1)


def row_twiddles():
    cosine, sine = circle(np.arange(128)[:, None] * np.arange(128)[None, :], N)
    return np.stack([cosine, sine]).astype(np.float32)


def row_second_table():
    cosine, sine = circle(np.arange(64)[:, None] * np.arange(128)[None, :], 64)
    table = np.block([[cosine, -sine], [sine, cosine]])
    high, low = split(table)
    return np.concatenate([high, low], axis=0)


def column_second_table():
    cosine, sine = circle(np.arange(128)[:, None] * np.arange(128)[None, :], 128)
    table = np.zeros((2, 128, 2, 2, 64))
    cosine = cosine.reshape(128, 2, 64) / N
    sine = sine.reshape(128, 2, 64) / N
    table[0, :, :, 0] = cosine
    table[0, :, :, 1] = -sine
    table[1, :, :, 0] = sine
    table[1, :, :, 1] = cosine
    high, low = split(table.reshape(256, 256))
    return np.concatenate([high, low], axis=1)


def pack_kernel(
    count_ref, band_ref, offset_ref, tiles_ref, out_ref, held_ref, rows_ref, done_ref, in_sems, out_sems,
    *, half
):
    groups = 8
    each = SLOTS // groups
    incoming = []
    for group in range(groups):
        where = pl.ds(each * group, each)
        copy = pltpu.make_async_copy(
            tiles_ref.at[where, :, pl.ds(64 * half, 64), :], held_ref.at[where], in_sems.at[group]
        )
        copy.start()
        incoming.append(copy)

    count = count_ref[0, 0]
    if half == 0:
        row = lax.broadcasted_iota(jnp.int32, (8, 128), 0)
        lane = lax.broadcasted_iota(jnp.int32, (8, 128), 1)

        def number(slot, values):
            column = offset_ref[1, slot]
            values = jnp.where((row == 0) & (lane == slot), band_ref[0, slot], values)
            values = jnp.where((row == 1) & (lane == slot), column >> 7, values)
            return jnp.where((row == 2) & (lane == slot), column & 127, values)

        values = lax.fori_loop(0, SLOTS, number, jnp.zeros((8, 128), jnp.int32), unroll=4)
        places = values.astype(F32).astype(BF16)

    def one(slot, carry):
        shift = offset_ref[1, slot] & 127
        keep = slot < count
        tile = pltpu.roll(held_ref[slot].astype(F32).reshape(128, 128), shift, 1)
        tile = jnp.where(keep, tile, 0.0)
        for part in range(2):
            where = pl.ds(slot * 2 + part, 64, stride=STRIDE)
            rows_ref[where, :] = tile[64 * part : 64 * part + 64]
        return carry

    for group in range(groups):
        incoming[group].wait()
        lax.fori_loop(each * group, each * group + each, one, 0, unroll=8)

    def cast(block, carry):
        done_ref[block, :128] = rows_ref[pl.ds(block * STRIDE, 128), :].astype(BF16)
        if half == 0:
            done_ref[block, 128:] = places
        return carry

    outgoing = []
    for group in range(4):
        lax.fori_loop(16 * group, 16 * group + 16, cast, 0, unroll=4)
        where = pl.ds(16 * group, 16)
        copy = pltpu.make_async_copy(done_ref.at[where], out_ref.at[where], out_sems.at[group])
        copy.start()
        outgoing.append(copy)
    for copy in outgoing:
        copy.wait()


def pack(count, bands, offsets, tiles, half):
    length = 128 if half else 136
    smem = pl.BlockSpec(memory_space=pltpu.SMEM)
    anywhere = pl.BlockSpec(memory_space=pl.ANY)
    return pl.pallas_call(
        functools.partial(pack_kernel, half=half),
        in_specs=[smem, smem, smem, anywhere],
        out_specs=anywhere,
        out_shape=jax.ShapeDtypeStruct((64, length, 128), BF16),
        scratch_shapes=[
            pltpu.VMEM((SLOTS, 2, 64, 128), BF16),
            pltpu.VMEM((64 * STRIDE, 128), F32),
            pltpu.VMEM((64, length, 128), BF16),
            pltpu.SemaphoreType.DMA((8,)),
            pltpu.SemaphoreType.DMA((4,)),
        ],
        compiler_params=pltpu.CompilerParams(vmem_limit_bytes=62 * MIB),
        cost_estimate=pl.CostEstimate(flops=8 << 20, bytes_accessed=4 << 20, transcendentals=0),
        name="pack_rows",
    )(count, bands, offsets, tiles)


def grid_kernel(
    place_ref, arrived_ref, first_ref, twiddle_ref, second_ref, bands_ref, out_ref,
    grid_a, grid_b, rows_ref, pieces_ref, done_ref, in_sem, out_sems,
):
    incoming = pltpu.make_async_copy(arrived_ref.at[:, pl.ds(0, 128), :], pieces_ref, in_sem)
    incoming.start()

    def clear(index, carry):
        where = pl.ds(pl.multiple_of(index * 64, 64), 64)
        grid_a[where, :] = jnp.zeros((64, 128), F32)
        grid_b[where, :] = jnp.zeros((64, 128), F32)
        return carry

    lax.fori_loop(0, ROWS // 64, clear, 0)
    grid_a[pl.ds(ROWS, 8), :] = jnp.zeros((8, 128), F32)
    grid_b[pl.ds(ROWS, 8), :] = jnp.zeros((8, 128), F32)

    incoming.wait()
    sublane = lax.broadcasted_iota(jnp.int32, (8, 128), 0)
    lane = lax.broadcasted_iota(jnp.int32, (8, 128), 1)
    position = lane + (sublane // 2) * 128
    upper = sublane < 2

    def place(index, carry):
        source = index >> 3
        slot = (index & 7) * 8
        pieces = pieces_ref[source, pl.ds(pl.multiple_of(slot * 2, 16), 16), :].astype(F32)
        for part in range(2):
            block = pieces[8 * part : 8 * part + 8]
            turned = [block] + [pltpu.roll(block, 8 - 2 * turn, 0) for turn in (1, 2, 3)]
            for piece in range(4):
                both = jnp.where(upper, turned[piece], turned[(piece + 3) % 4])
                packed = place_ref[source, slot + part * 4 + piece]
                shift = packed & 127
                row = packed >> 7
                offset = position - shift
                inside = (offset >= 0) & (offset < 128)
                grid = grid_a if piece % 2 == 0 else grid_b
                window = pl.ds(row, 8)
                grid[window, :] = grid[window, :] + jnp.where(inside, both, 0.0)
        return carry

    lax.fori_loop(0, BANDS * SLOTS // 8, place, 0, unroll=4)

    first = first_ref[...]
    second = second_ref[...]
    cosine = twiddle_ref[0]
    sine = twiddle_ref[1]

    def band_step(band, carry):
        where = pl.ds(pl.multiple_of(band * 128, 128), 128)
        cells = grid_a[where, :] + grid_b[where, :]
        high = cells.astype(BF16)
        low = (cells - high.astype(F32)).astype(BF16)
        section = jnp.dot(
            first, jnp.concatenate([high, low, high], axis=0), preferred_element_type=F32
        )
        real = jnp.concatenate([section[:64], section[:64]], axis=0)
        imag = jnp.concatenate([section[64:], section[64:]], axis=0)
        turned = jnp.concatenate(
            [real * cosine - imag * sine, real * sine + imag * cosine], axis=1
        )
        high = turned.astype(BF16)
        low = (turned - high.astype(F32)).astype(BF16)
        contract = (((1,), (1,)), ((), ()))
        main = lax.dot_general(second, high, contract, preferred_element_type=F32)
        rest = lax.dot_general(second[:128], low, contract, preferred_element_type=F32)
        spectrum = main[:128] + main[128:] + rest
        rows_ref[pl.ds(band, 64, stride=STRIDE), :] = spectrum[:64]
        rows_ref[pl.ds(64 + band, 64, stride=STRIDE), :] = spectrum[64:]
        return carry

    lax.fori_loop(0, BANDS, band_step, 0, unroll=4)

    table = bands_ref[...]

    def block_step(index, carry):
        rows = rows_ref[pl.ds(index * STRIDE, 128), :].astype(BF16)
        section = jnp.dot(table, jnp.concatenate([rows, rows], axis=0), preferred_element_type=F32)
        done_ref[index] = section.astype(BF16)
        return carry

    outgoing = []
    for group in range(4):
        lax.fori_loop(16 * group, 16 * group + 16, block_step, 0, unroll=4)
        where = pl.ds(16 * group, 16)
        copy = pltpu.make_async_copy(done_ref.at[where], out_ref.at[where], out_sems.at[group])
        copy.start()
        outgoing.append(copy)
    for copy in outgoing:
        copy.wait()


def grid_and_rows(places, arrived, first, twiddle, second, bands):
    vmem = pl.BlockSpec(memory_space=pltpu.VMEM)
    anywhere = pl.BlockSpec(memory_space=pl.ANY)
    return pl.pallas_call(
        grid_kernel,
        in_specs=[pl.BlockSpec(memory_space=pltpu.SMEM), anywhere, vmem, vmem, vmem, vmem],
        out_specs=anywhere,
        out_shape=jax.ShapeDtypeStruct((64, 128, 128), BF16),
        scratch_shapes=[
            pltpu.VMEM((ROWS + 8, 128), F32),
            pltpu.VMEM((ROWS + 8, 128), F32),
            pltpu.VMEM((64 * STRIDE, 128), F32),
            pltpu.VMEM((64, 128, 128), BF16),
            pltpu.VMEM((64, 128, 128), BF16),
            pltpu.SemaphoreType.DMA,
            pltpu.SemaphoreType.DMA((4,)),
        ],
        compiler_params=pltpu.CompilerParams(vmem_limit_bytes=62 * MIB),
        cost_estimate=pl.CostEstimate(flops=20_000_000_000, bytes_accessed=4 << 20, transcendentals=0),
        name="place_and_transform",
    )(places, arrived, first, twiddle, second, bands)


def column_kernel(early_ref, late_ref, table_ref, cosine_ref, sine_ref, own_ref, *sent):
    table = table_ref[...]
    count = early_ref.shape[0]
    late = jnp.swapaxes(late_ref[...], 0, 1).reshape(count, 128, 128)
    for pair in range(0, count, 2):
        cells = jnp.concatenate(
            [
                jnp.concatenate([early_ref[index], late[index]], axis=0)
                for index in (pair, pair + 1)
            ],
            axis=1,
        )
        both = jnp.dot(table, jnp.concatenate([cells, cells], axis=0), preferred_element_type=F32)
        for index in (pair, pair + 1):
            sky = both[:, 128 * (index - pair) : 128 * (index - pair) + 128]
            image = sky[:128] * cosine_ref[index] - sky[128:] * sine_ref[index]
            own_ref[index] = image[:32]
            for step in range(3):
                sent[step][index] = image[32 * step + 32 : 32 * step + 64].astype(BF16)


def column_transform(early, late, table, cosine, sine, begin, count):
    per_step = 8
    skip = begin // per_step
    block = pl.BlockSpec((per_step, 128, 128), lambda i: (i + skip, 0, 0))
    result = pl.BlockSpec((per_step, 32, 128), lambda i: (i, 0, 0))
    return pl.pallas_call(
        column_kernel,
        grid=(count // per_step,),
        in_specs=[
            block,
            pl.BlockSpec((64, 2 * per_step, 128), lambda i: (0, i + skip, 0)),
            pl.BlockSpec((256, 512), lambda i: (0, 0)),
            block,
            block,
        ],
        out_specs=[result] * 4,
        out_shape=[jax.ShapeDtypeStruct((count, 32, 128), F32)]
        + [jax.ShapeDtypeStruct((count, 32, 128), BF16)] * 3,
        compiler_params=pltpu.CompilerParams(vmem_limit_bytes=16 * MIB),
        cost_estimate=pl.CostEstimate(
            flops=count * 70_000_000, bytes_accessed=count * (200 << 10), transcendentals=0
        ),
        name="column_transform",
    )(early, late, table, cosine, sine)


def sum_kernel(*refs, counts):
    out_ref = refs[-1]
    begin = 0
    for part, count in enumerate(counts):
        own, *others = refs[4 * part : 4 * part + 4]
        for group in range(0, count, 8):
            total = own[group : group + 8]
            for other in others:
                total = total + other[group : group + 8].astype(F32)
            out_ref[:, begin + group : begin + group + 8, :] = jnp.swapaxes(total, 0, 1)
        begin += count


def window_sum(parts, counts):
    vmem = pl.BlockSpec(memory_space=pltpu.VMEM)
    flat = [block for part in parts for block in part]
    return pl.pallas_call(
        functools.partial(sum_kernel, counts=counts),
        in_specs=[vmem] * len(flat),
        out_specs=vmem,
        out_shape=jax.ShapeDtypeStruct((32, 64, 128), F32),
        compiler_params=pltpu.CompilerParams(vmem_limit_bytes=16 * MIB),
        cost_estimate=pl.CostEstimate(flops=1 << 20, bytes_accessed=3 << 20, transcendentals=0),
        name="window_sum",
    )(*flat)


def w_phases(plane_w, turn):
    k = jnp.arange(64, dtype=jnp.int32)[:, None, None]
    j = (jnp.arange(128, dtype=jnp.int32)[None, :, None] + 32 * turn) % 128
    column = lax.axis_index("band") * 128 + jnp.arange(128, dtype=jnp.int32)[None, None, :]
    x = ((64 * j + k).astype(F32) - N // 2) / N
    y = (column.astype(F32) - N // 2) / N
    radius = x**2 + y**2
    angle = 2.0 * math.pi * plane_w * (jnp.sqrt(1.0 - radius) - 1.0)
    return jnp.cos(angle), jnp.sin(angle)


def band_table(row):
    k = jnp.arange(64, dtype=jnp.int32)[:, None]
    band = jnp.arange(64, dtype=jnp.int32)[None, :]
    angle = (2.0 * math.pi / N) * ((k * (128 * band + row)) % N).astype(F32)
    cosine = jnp.cos(angle)
    sine = jnp.sin(angle)
    real = jnp.concatenate([cosine, -sine], axis=1)
    imag = jnp.concatenate([sine, cosine], axis=1)
    table = jnp.stack([real, imag], axis=1).reshape(128, 128)
    high = lax.reduce_precision(table, 8, 7)
    low = lax.reduce_precision(table - high, 8, 7)
    return jnp.concatenate([high, low], axis=1).astype(BF16)


def local(uv_tiles, target_bands, uv_offsets, tile_counts, plane_w):
    me = lax.axis_index("band")
    turn = lax.axis_index("wp")
    first = jnp.asarray(row_first_table())
    twiddle = jnp.asarray(row_twiddles())
    second = jnp.asarray(row_second_table())

    arrived = []
    for half in range(2):
        packed = pack(tile_counts, target_bands[0].T, uv_offsets[0].T, uv_tiles[0], half)
        arrived.append(
            lax.all_to_all(packed, "band", split_axis=0, concat_axis=0, tiled=True)
        )
    numbers = arrived[0][:, 128:131, :64].astype(jnp.int32)
    places = (numbers[:, 0] * 64 + numbers[:, 1]) * 256 + numbers[:, 2]
    columns = []
    for half in range(2):
        spectrum = grid_and_rows(
            places, arrived[half], first, twiddle, second, band_table(me + 64 * half)
        )
        columns.append(
            lax.all_to_all(spectrum, "band", split_axis=0, concat_axis=0, tiled=True)
        )
    early = jnp.swapaxes(columns[0], 0, 1).reshape(64, 128, 128)

    cosine, sine = w_phases(plane_w[0], turn)
    table = jnp.roll(jnp.asarray(column_second_table()).reshape(2, 128, 512), -32 * turn, axis=1)
    table = table.reshape(256, 512)
    counts = (24, 40)
    parts = []
    begin = 0
    late = columns[1]
    for count in counts:
        own, *sent = column_transform(early, late, table, cosine, sine, begin, count)
        late, own = lax.optimization_barrier((late, own))
        moved = [
            lax.ppermute(block, "wp", [(plane, (plane + step + 1) % 4) for plane in range(4)])
            for step, block in enumerate(sent)
        ]
        parts.append([own, *moved])
        begin += count
    return window_sum(parts, counts).reshape(2048, 128)


def solution(mesh):
    placed = (
        P("wp", "band", None, None, None),
        P("wp", "band", None),
        P("wp", "band", None),
        P("wp", "band"),
        P("wp"),
    )
    return jax.shard_map(
        local, mesh=mesh, in_specs=placed, out_specs=P("wp", "band"), check_vma=False
    )
```

```python
import functools
import math

import jax
import jax.numpy as jnp
import ml_dtypes
import numpy as np
from jax import lax
from jax.experimental import pallas as pl
from jax.experimental.pallas import tpu as pltpu
from jax.sharding import PartitionSpec as P

N = 8192
BANDS = 64
EDGE = 128
SLOTS = 64
ROWS = 8192
STRIDE = 129
F32 = jnp.float32
BF16 = jnp.bfloat16
MIB = 1 << 20


def circle(numerator, length):
    angle = 2.0 * np.pi * (np.asarray(numerator) % length) / length
    return np.cos(angle), np.sin(angle)


def split(table):
    high = table.astype(ml_dtypes.bfloat16)
    low = (table - high.astype(np.float64)).astype(ml_dtypes.bfloat16)
    return high, low


def row_first_table():
    cosine, sine = circle(np.arange(64)[:, None] * np.arange(64)[None, :], 64)
    table = np.zeros((2, 64, 64, 2))
    table[0, :, :, 0] = cosine
    table[0, :, :, 1] = -sine
    table[1, :, :, 0] = sine
    table[1, :, :, 1] = cosine
    high, low = split(table.reshape(128, 128))
    return np.concatenate([high, high, low], axis=1)


def row_twiddles():
    cosine, sine = circle(np.arange(128)[:, None] * np.arange(128)[None, :], N)
    return np.stack([cosine, sine]).astype(np.float32)


def row_second_table():
    cosine, sine = circle(np.arange(64)[:, None] * np.arange(128)[None, :], 64)
    table = np.block([[cosine, -sine], [sine, cosine]])
    high, low = split(table)
    return np.concatenate([high, low], axis=0)


def column_second_table():
    cosine, sine = circle(np.arange(128)[:, None] * np.arange(128)[None, :], 128)
    table = np.zeros((2, 128, 2, 2, 64))
    cosine = cosine.reshape(128, 2, 64) / N
    sine = sine.reshape(128, 2, 64) / N
    table[0, :, :, 0] = cosine
    table[0, :, :, 1] = -sine
    table[1, :, :, 0] = sine
    table[1, :, :, 1] = cosine
    high, low = split(table.reshape(256, 256))
    return np.concatenate([high, low], axis=1)


def pack_kernel(
    count_ref, band_ref, offset_ref, tiles_ref, out_ref, held_ref, rows_ref, done_ref, in_sems, out_sems,
    *, half
):
    groups = 8
    each = SLOTS // groups
    incoming = []
    for group in range(groups):
        where = pl.ds(each * group, each)
        copy = pltpu.make_async_copy(
            tiles_ref.at[where, :, pl.ds(64 * half, 64), :], held_ref.at[where], in_sems.at[group]
        )
        copy.start()
        incoming.append(copy)

    count = count_ref[0, 0]
    if half == 0:
        row = lax.broadcasted_iota(jnp.int32, (8, 128), 0)
        lane = lax.broadcasted_iota(jnp.int32, (8, 128), 1)

        def number(slot, values):
            column = offset_ref[1, slot]
            values = jnp.where((row == 0) & (lane == slot), band_ref[0, slot], values)
            values = jnp.where((row == 1) & (lane == slot), column >> 7, values)
            return jnp.where((row == 2) & (lane == slot), column & 127, values)

        values = lax.fori_loop(0, SLOTS, number, jnp.zeros((8, 128), jnp.int32), unroll=4)
        places = values.astype(F32).astype(BF16)

    def one(slot, carry):
        shift = offset_ref[1, slot] & 127
        keep = slot < count
        tile = pltpu.roll(held_ref[slot].astype(F32).reshape(128, 128), shift, 1)
        tile = jnp.where(keep, tile, 0.0)
        for part in range(2):
            where = pl.ds(slot * 2 + part, 64, stride=STRIDE)
            rows_ref[where, :] = tile[64 * part : 64 * part + 64]
        return carry

    for group in range(groups):
        incoming[group].wait()
        lax.fori_loop(each * group, each * group + each, one, 0, unroll=8)

    def cast(block, carry):
        done_ref[block, :128] = rows_ref[pl.ds(block * STRIDE, 128), :].astype(BF16)
        if half == 0:
            done_ref[block, 128:] = places
        return carry

    outgoing = []
    for group in range(4):
        lax.fori_loop(16 * group, 16 * group + 16, cast, 0, unroll=4)
        where = pl.ds(16 * group, 16)
        copy = pltpu.make_async_copy(done_ref.at[where], out_ref.at[where], out_sems.at[group])
        copy.start()
        outgoing.append(copy)
    for copy in outgoing:
        copy.wait()


def pack(count, bands, offsets, tiles, half):
    length = 128 if half else 136
    smem = pl.BlockSpec(memory_space=pltpu.SMEM)
    anywhere = pl.BlockSpec(memory_space=pl.ANY)
    return pl.pallas_call(
        functools.partial(pack_kernel, half=half),
        in_specs=[smem, smem, smem, anywhere],
        out_specs=anywhere,
        out_shape=jax.ShapeDtypeStruct((64, length, 128), BF16),
        scratch_shapes=[
            pltpu.VMEM((SLOTS, 2, 64, 128), BF16),
            pltpu.VMEM((64 * STRIDE, 128), F32),
            pltpu.VMEM((64, length, 128), BF16),
            pltpu.SemaphoreType.DMA((8,)),
            pltpu.SemaphoreType.DMA((4,)),
        ],
        compiler_params=pltpu.CompilerParams(vmem_limit_bytes=62 * MIB),
        cost_estimate=pl.CostEstimate(flops=8 << 20, bytes_accessed=4 << 20, transcendentals=0),
        name="pack_rows",
    )(count, bands, offsets, tiles)


def grid_kernel(
    place_ref, arrived_ref, first_ref, twiddle_ref, second_ref, bands_ref, out_ref,
    grid_a, grid_b, rows_ref, pieces_ref, done_ref, in_sem, out_sems,
):
    incoming = pltpu.make_async_copy(arrived_ref.at[:, pl.ds(0, 128), :], pieces_ref, in_sem)
    incoming.start()

    def clear(index, carry):
        where = pl.ds(pl.multiple_of(index * 64, 64), 64)
        grid_a[where, :] = jnp.zeros((64, 128), F32)
        grid_b[where, :] = jnp.zeros((64, 128), F32)
        return carry

    lax.fori_loop(0, ROWS // 64, clear, 0)
    grid_a[pl.ds(ROWS, 8), :] = jnp.zeros((8, 128), F32)
    grid_b[pl.ds(ROWS, 8), :] = jnp.zeros((8, 128), F32)

    incoming.wait()
    sublane = lax.broadcasted_iota(jnp.int32, (8, 128), 0)
    lane = lax.broadcasted_iota(jnp.int32, (8, 128), 1)
    position = lane + (sublane // 2) * 128
    upper = sublane < 2

    def place(index, carry):
        source = index >> 3
        slot = (index & 7) * 8
        pieces = pieces_ref[source, pl.ds(pl.multiple_of(slot * 2, 16), 16), :].astype(F32)
        for part in range(2):
            block = pieces[8 * part : 8 * part + 8]
            turned = [block] + [pltpu.roll(block, 8 - 2 * turn, 0) for turn in (1, 2, 3)]
            for piece in range(4):
                both = jnp.where(upper, turned[piece], turned[(piece + 3) % 4])
                packed = place_ref[source, slot + part * 4 + piece]
                shift = packed & 127
                row = packed >> 7
                offset = position - shift
                inside = (offset >= 0) & (offset < 128)
                grid = grid_a if piece % 2 == 0 else grid_b
                window = pl.ds(row, 8)
                grid[window, :] = grid[window, :] + jnp.where(inside, both, 0.0)
        return carry

    lax.fori_loop(0, BANDS * SLOTS // 8, place, 0, unroll=4)

    first = first_ref[...]
    second = second_ref[...]
    cosine = twiddle_ref[0]
    sine = twiddle_ref[1]

    def band_step(band, carry):
        where = pl.ds(pl.multiple_of(band * 128, 128), 128)
        cells = grid_a[where, :] + grid_b[where, :]
        high = cells.astype(BF16)
        low = (cells - high.astype(F32)).astype(BF16)
        section = jnp.dot(
            first, jnp.concatenate([high, low, high], axis=0), preferred_element_type=F32
        )
        real = jnp.concatenate([section[:64], section[:64]], axis=0)
        imag = jnp.concatenate([section[64:], section[64:]], axis=0)
        turned = jnp.concatenate(
            [real * cosine - imag * sine, real * sine + imag * cosine], axis=1
        )
        high = turned.astype(BF16)
        low = (turned - high.astype(F32)).astype(BF16)
        contract = (((1,), (1,)), ((), ()))
        main = lax.dot_general(second, high, contract, preferred_element_type=F32)
        rest = lax.dot_general(second[:128], low, contract, preferred_element_type=F32)
        spectrum = main[:128] + main[128:] + rest
        rows_ref[pl.ds(band, 64, stride=STRIDE), :] = spectrum[:64]
        rows_ref[pl.ds(64 + band, 64, stride=STRIDE), :] = spectrum[64:]
        return carry

    lax.fori_loop(0, BANDS, band_step, 0, unroll=4)

    table = bands_ref[...]

    def block_step(index, carry):
        rows = rows_ref[pl.ds(index * STRIDE, 128), :].astype(BF16)
        section = jnp.dot(table, jnp.concatenate([rows, rows], axis=0), preferred_element_type=F32)
        section = section.astype(BF16)
        parts, _, length, _ = done_ref.shape
        for part in range(parts):
            done_ref[part, index] = section[length * part : length * part + length]
        return carry

    outgoing = []
    for group in range(4):
        lax.fori_loop(16 * group, 16 * group + 16, block_step, 0, unroll=4)
        where = pl.ds(16 * group, 16)
        copy = pltpu.make_async_copy(
            done_ref.at[:, where], out_ref.at[:, where], out_sems.at[group]
        )
        copy.start()
        outgoing.append(copy)
    for copy in outgoing:
        copy.wait()


def grid_and_rows(places, arrived, first, twiddle, second, bands, parts):
    shape = (parts, 64, 128 // parts, 128)
    vmem = pl.BlockSpec(memory_space=pltpu.VMEM)
    anywhere = pl.BlockSpec(memory_space=pl.ANY)
    return pl.pallas_call(
        grid_kernel,
        in_specs=[pl.BlockSpec(memory_space=pltpu.SMEM), anywhere, vmem, vmem, vmem, vmem],
        out_specs=anywhere,
        out_shape=jax.ShapeDtypeStruct(shape, BF16),
        scratch_shapes=[
            pltpu.VMEM((ROWS + 8, 128), F32),
            pltpu.VMEM((ROWS + 8, 128), F32),
            pltpu.VMEM((64 * STRIDE, 128), F32),
            pltpu.VMEM((64, 128, 128), BF16),
            pltpu.VMEM(shape, BF16),
            pltpu.SemaphoreType.DMA,
            pltpu.SemaphoreType.DMA((4,)),
        ],
        compiler_params=pltpu.CompilerParams(vmem_limit_bytes=62 * MIB),
        cost_estimate=pl.CostEstimate(flops=20_000_000_000, bytes_accessed=4 << 20, transcendentals=0),
        name="place_and_transform",
    )(places, arrived, first, twiddle, second, bands)


def deal_kernel(turn_ref, columns_ref, *out_refs):
    for step, out_ref in enumerate(out_refs):
        begin = ((turn_ref[0] + step) & 3) * 32
        for group in range(2):
            where = pl.ds(pl.multiple_of(begin + 16 * group, 16), 16)
            rows = jnp.swapaxes(columns_ref[:, where, :], 0, 1).reshape(8, 128, 128)
            out_ref[8 * group : 8 * group + 8] = rows


def deal_rows(turn, columns):
    vmem = pl.BlockSpec(memory_space=pltpu.VMEM)
    return pl.pallas_call(
        deal_kernel,
        in_specs=[pl.BlockSpec(memory_space=pltpu.SMEM), vmem],
        out_specs=[vmem] * 4,
        out_shape=[jax.ShapeDtypeStruct((16, 128, 128), BF16)] * 4,
        compiler_params=pltpu.CompilerParams(vmem_limit_bytes=16 * MIB),
        cost_estimate=pl.CostEstimate(flops=1 << 20, bytes_accessed=4 << 20, transcendentals=0),
        name="deal_rows",
    )(turn, columns)


def phase_kernel(turn_ref, me_ref, w_ref, cosine_ref, sine_ref):
    turn = turn_ref[0]
    k = 16 * turn + pl.program_id(0)
    j = (lax.broadcasted_iota(jnp.int32, (128, 128), 0) + 32 * turn) & 127
    column = lax.broadcasted_iota(jnp.int32, (128, 128), 1) + 128 * me_ref[0]
    x = ((64 * j + k).astype(F32) - N // 2) / N
    y = (column.astype(F32) - N // 2) / N
    term = jnp.sqrt(1.0 - (x * x + y * y)) - 1.0
    for step in range(4):
        angle = (2.0 * math.pi * w_ref[step]) * term
        cosine_ref[step, 0] = jnp.cos(angle)
        sine_ref[step, 0] = jnp.sin(angle)


def phases(turn, me, w):
    smem = pl.BlockSpec(memory_space=pltpu.SMEM)
    block = pl.BlockSpec((4, 1, 128, 128), lambda i: (0, i, 0, 0))
    return pl.pallas_call(
        phase_kernel,
        grid=(16,),
        in_specs=[smem] * 3,
        out_specs=[block] * 2,
        out_shape=[jax.ShapeDtypeStruct((4, 16, 128, 128), F32)] * 2,
        compiler_params=pltpu.CompilerParams(vmem_limit_bytes=16 * MIB),
        cost_estimate=pl.CostEstimate(flops=200 << 20, bytes_accessed=8 << 20, transcendentals=2 << 20),
        name="w_phases",
    )(turn, me, w)


def column_kernel(
    turn_ref, early_0, early_1, early_2, early_3, late_ref, table_ref, cosine_ref, sine_ref,
    own_ref, *sent
):
    table = table_ref[...]
    early = (early_0, early_1, early_2, early_3)
    count = early_0.shape[0]
    late = [
        jnp.swapaxes(late_ref[(turn_ref[0] - step) & 3], 0, 1).reshape(count, 128, 128)
        for step in range(4)
    ]
    for index in range(count):
        image = jnp.zeros((128, 128), F32)
        for pair in (0, 2):
            cells = jnp.concatenate(
                [
                    jnp.concatenate([early[step][index], late[step][index]], axis=0)
                    for step in (pair, pair + 1)
                ],
                axis=1,
            )
            sky = jnp.dot(
                table, jnp.concatenate([cells, cells], axis=0), preferred_element_type=F32
            )
            for step in (pair, pair + 1):
                part = sky[:, 128 * (step - pair) : 128 * (step - pair) + 128]
                image += part[:128] * cosine_ref[step, index] - part[128:] * sine_ref[step, index]
        own_ref[index] = image[:32]
        for step in range(3):
            sent[step][index] = image[32 * step + 32 : 32 * step + 64].astype(BF16)


def column_transform(turn, early, late, table, cosine, sine):
    each = 8
    block = pl.BlockSpec((each, 128, 128), lambda i: (i, 0, 0))
    phase = pl.BlockSpec((4, each, 128, 128), lambda i: (0, i, 0, 0))
    result = pl.BlockSpec((each, 32, 128), lambda i: (i, 0, 0))
    return pl.pallas_call(
        column_kernel,
        grid=(16 // each,),
        in_specs=[pl.BlockSpec(memory_space=pltpu.SMEM)]
        + [block] * 4
        + [
            pl.BlockSpec((4, 64, 2 * each, 128), lambda i: (0, 0, i, 0)),
            pl.BlockSpec((256, 512), lambda i: (0, 0)),
            phase,
            phase,
        ],
        out_specs=[result] * 4,
        out_shape=[jax.ShapeDtypeStruct((16, 32, 128), F32)]
        + [jax.ShapeDtypeStruct((16, 32, 128), BF16)] * 3,
        compiler_params=pltpu.CompilerParams(vmem_limit_bytes=24 * MIB),
        cost_estimate=pl.CostEstimate(
            flops=4_300_000_000, bytes_accessed=13 << 20, transcendentals=0
        ),
        name="column_transform",
    )(turn, *early, late, table, cosine, sine)


def place_kernel(turn_ref, *refs):
    out_ref = refs[-1]
    for step, block_ref in enumerate(refs[:-1]):
        begin = ((turn_ref[0] - step) & 3) * 16
        for group in (0, 8):
            rows = jnp.swapaxes(block_ref[group : group + 8].astype(F32), 0, 1)
            out_ref[:, pl.ds(pl.multiple_of(begin + group, 8), 8), :] = rows


def place_rows(turn, blocks):
    vmem = pl.BlockSpec(memory_space=pltpu.VMEM)
    return pl.pallas_call(
        place_kernel,
        in_specs=[pl.BlockSpec(memory_space=pltpu.SMEM)] + [vmem] * 4,
        out_specs=vmem,
        out_shape=jax.ShapeDtypeStruct((32, 64, 128), F32),
        compiler_params=pltpu.CompilerParams(vmem_limit_bytes=16 * MIB),
        cost_estimate=pl.CostEstimate(flops=1 << 20, bytes_accessed=2 << 20, transcendentals=0),
        name="place_image_rows",
    )(turn, *blocks)


def along_wp(block, step):
    pairs = [(plane, (plane + step) % 4) for plane in range(4)]
    return lax.ppermute(block, "wp", pairs)


def band_table(row):
    k = jnp.arange(64, dtype=jnp.int32)[:, None]
    band = jnp.arange(64, dtype=jnp.int32)[None, :]
    angle = (2.0 * math.pi / N) * ((k * (128 * band + row)) % N).astype(F32)
    cosine = jnp.cos(angle)
    sine = jnp.sin(angle)
    real = jnp.concatenate([cosine, -sine], axis=1)
    imag = jnp.concatenate([sine, cosine], axis=1)
    table = jnp.stack([real, imag], axis=1).reshape(128, 128)
    high = lax.reduce_precision(table, 8, 7)
    low = lax.reduce_precision(table - high, 8, 7)
    return jnp.concatenate([high, low], axis=1).astype(BF16)


def local(uv_tiles, target_bands, uv_offsets, tile_counts, plane_w):
    me = lax.axis_index("band")
    turn = lax.axis_index("wp")
    first = jnp.asarray(row_first_table())
    twiddle = jnp.asarray(row_twiddles())
    second = jnp.asarray(row_second_table())

    arrived = []
    for half in range(2):
        packed = pack(tile_counts, target_bands[0].T, uv_offsets[0].T, uv_tiles[0], half)
        arrived.append(
            lax.all_to_all(packed, "band", split_axis=0, concat_axis=0, tiled=True)
        )
    numbers = arrived[0][:, 128:131, :64].astype(jnp.int32)
    places = (numbers[:, 0] * 64 + numbers[:, 1]) * 256 + numbers[:, 2]
    early = late = None
    for half in range(2):
        spectrum = grid_and_rows(
            places, arrived[half], first, twiddle, second, band_table(me + 64 * half), 4 if half else 1
        )
        if half == 0:
            early = lax.all_to_all(
                spectrum.reshape(64, 128, 128), "band", split_axis=0, concat_axis=0, tiled=True
            )
        else:
            late = lax.all_to_all(
                spectrum.reshape(256, 32, 128), ("wp", "band"), split_axis=0, concat_axis=0, tiled=True
            ).reshape(4, 64, 32, 128)

    early, w = lax.optimization_barrier((early, plane_w))
    w = jnp.concatenate([w, along_wp(w, 1)])
    w = jnp.concatenate([w, along_wp(w, 2)])
    turn = turn[None]
    cosine, sine = phases(turn, me[None], w)
    dealt = deal_rows(turn, early)
    dealt = [dealt[0]] + [along_wp(dealt[step], step) for step in (1, 2, 3)]
    table = jnp.roll(jnp.asarray(column_second_table()).reshape(2, 128, 512), -32 * turn[0], axis=1)
    own, *sent = column_transform(turn, dealt, late, table.reshape(256, 512), cosine, sine)
    blocks = [own] + [along_wp(block, step + 1) for step, block in enumerate(sent)]
    return place_rows(turn, blocks).reshape(2048, 128)


def solution(mesh):
    placed = (
        P("wp", "band", None, None, None),
        P("wp", "band", None),
        P("wp", "band", None),
        P("wp", "band"),
        P("wp"),
    )
    return jax.shard_map(
        local, mesh=mesh, in_specs=placed, out_specs=P("wp", "band"), check_vma=False
    )
```

```python
import functools
import math

import jax
import jax.numpy as jnp
import ml_dtypes
import numpy as np
from jax import lax
from jax.experimental import pallas as pl
from jax.experimental.pallas import tpu as pltpu
from jax.sharding import PartitionSpec as P

N = 8192
BANDS = 64
EDGE = 128
SLOTS = 64
ROWS = 8192
STRIDE = 129
F32 = jnp.float32
BF16 = jnp.bfloat16
MIB = 1 << 20


def circle(numerator, length):
    angle = 2.0 * np.pi * (np.asarray(numerator) % length) / length
    return np.cos(angle), np.sin(angle)


def split(table):
    high = table.astype(ml_dtypes.bfloat16)
    low = (table - high.astype(np.float64)).astype(ml_dtypes.bfloat16)
    return high, low


def row_first_table():
    cosine, sine = circle(np.arange(64)[:, None] * np.arange(64)[None, :], 64)
    table = np.zeros((2, 64, 64, 2))
    table[0, :, :, 0] = cosine
    table[0, :, :, 1] = -sine
    table[1, :, :, 0] = sine
    table[1, :, :, 1] = cosine
    high, low = split(table.reshape(128, 128))
    return np.concatenate([high, high, low], axis=1)


def row_twiddles():
    cosine, sine = circle(np.arange(128)[:, None] * np.arange(128)[None, :], N)
    return np.stack([cosine, sine]).astype(np.float32)


def row_second_table():
    cosine, sine = circle(np.arange(64)[:, None] * np.arange(128)[None, :], 64)
    table = np.block([[cosine, -sine], [sine, cosine]])
    high, low = split(table)
    return np.concatenate([high, low], axis=0)


def column_second_table():
    cosine, sine = circle(np.arange(128)[:, None] * np.arange(128)[None, :], 128)
    table = np.zeros((2, 128, 2, 2, 64))
    cosine = cosine.reshape(128, 2, 64) / N
    sine = sine.reshape(128, 2, 64) / N
    table[0, :, :, 0] = cosine
    table[0, :, :, 1] = -sine
    table[1, :, :, 0] = sine
    table[1, :, :, 1] = cosine
    high, low = split(table.reshape(256, 256))
    return np.concatenate([high, low], axis=1)


def pack_kernel(
    count_ref, band_ref, offset_ref, tiles_ref, out_ref, held_ref, rows_ref, done_ref, in_sems, out_sems,
    *, half
):
    groups = 8
    each = SLOTS // groups
    incoming = []
    for group in range(groups):
        where = pl.ds(each * group, each)
        copy = pltpu.make_async_copy(
            tiles_ref.at[where, :, pl.ds(64 * half, 64), :], held_ref.at[where], in_sems.at[group]
        )
        copy.start()
        incoming.append(copy)

    count = count_ref[0, 0]
    if half == 0:
        row = lax.broadcasted_iota(jnp.int32, (8, 128), 0)
        lane = lax.broadcasted_iota(jnp.int32, (8, 128), 1)

        def number(slot, values):
            column = offset_ref[1, slot]
            values = jnp.where((row == 0) & (lane == slot), band_ref[0, slot], values)
            values = jnp.where((row == 1) & (lane == slot), column >> 7, values)
            return jnp.where((row == 2) & (lane == slot), column & 127, values)

        values = lax.fori_loop(0, SLOTS, number, jnp.zeros((8, 128), jnp.int32), unroll=4)
        places = values.astype(F32).astype(BF16)

    def one(slot, carry):
        shift = offset_ref[1, slot] & 127
        keep = slot < count
        tile = pltpu.roll(held_ref[slot].astype(F32).reshape(128, 128), shift, 1)
        tile = jnp.where(keep, tile, 0.0)
        for part in range(2):
            where = pl.ds(slot * 2 + part, 64, stride=STRIDE)
            rows_ref[where, :] = tile[64 * part : 64 * part + 64]
        return carry

    for group in range(groups):
        incoming[group].wait()
        lax.fori_loop(each * group, each * group + each, one, 0, unroll=8)

    def cast(block, carry):
        done_ref[block, :128] = rows_ref[pl.ds(block * STRIDE, 128), :].astype(BF16)
        if half == 0:
            done_ref[block, 128:] = places
        return carry

    outgoing = []
    for group in range(4):
        lax.fori_loop(16 * group, 16 * group + 16, cast, 0, unroll=4)
        where = pl.ds(16 * group, 16)
        copy = pltpu.make_async_copy(done_ref.at[where], out_ref.at[where], out_sems.at[group])
        copy.start()
        outgoing.append(copy)
    for copy in outgoing:
        copy.wait()


def pack(count, bands, offsets, tiles, half):
    length = 128 if half else 136
    smem = pl.BlockSpec(memory_space=pltpu.SMEM)
    anywhere = pl.BlockSpec(memory_space=pl.ANY)
    return pl.pallas_call(
        functools.partial(pack_kernel, half=half),
        in_specs=[smem, smem, smem, anywhere],
        out_specs=anywhere,
        out_shape=jax.ShapeDtypeStruct((64, length, 128), BF16),
        scratch_shapes=[
            pltpu.VMEM((SLOTS, 2, 64, 128), BF16),
            pltpu.VMEM((64 * STRIDE, 128), F32),
            pltpu.VMEM((64, length, 128), BF16),
            pltpu.SemaphoreType.DMA((8,)),
            pltpu.SemaphoreType.DMA((4,)),
        ],
        compiler_params=pltpu.CompilerParams(vmem_limit_bytes=62 * MIB),
        cost_estimate=pl.CostEstimate(flops=8 << 20, bytes_accessed=4 << 20, transcendentals=0),
        name="pack_rows",
    )(count, bands, offsets, tiles)


def grid_kernel(
    place_ref, arrived_ref, first_ref, twiddle_ref, second_ref, bands_ref, out_ref,
    grid_a, grid_b, rows_ref, pieces_ref, done_ref, in_sem, out_sems,
):
    incoming = pltpu.make_async_copy(arrived_ref.at[:, pl.ds(0, 128), :], pieces_ref, in_sem)
    incoming.start()

    def clear(index, carry):
        where = pl.ds(pl.multiple_of(index * 64, 64), 64)
        grid_a[where, :] = jnp.zeros((64, 128), F32)
        grid_b[where, :] = jnp.zeros((64, 128), F32)
        return carry

    lax.fori_loop(0, ROWS // 64, clear, 0)
    grid_a[pl.ds(ROWS, 8), :] = jnp.zeros((8, 128), F32)
    grid_b[pl.ds(ROWS, 8), :] = jnp.zeros((8, 128), F32)

    incoming.wait()
    sublane = lax.broadcasted_iota(jnp.int32, (8, 128), 0)
    lane = lax.broadcasted_iota(jnp.int32, (8, 128), 1)
    position = lane + (sublane // 2) * 128
    upper = sublane < 2

    def place(index, carry):
        source = index >> 3
        slot = (index & 7) * 8
        pieces = pieces_ref[source, pl.ds(pl.multiple_of(slot * 2, 16), 16), :].astype(F32)
        for part in range(2):
            block = pieces[8 * part : 8 * part + 8]
            turned = [block] + [pltpu.roll(block, 8 - 2 * turn, 0) for turn in (1, 2, 3)]
            for piece in range(4):
                both = jnp.where(upper, turned[piece], turned[(piece + 3) % 4])
                packed = place_ref[source, slot + part * 4 + piece]
                shift = packed & 127
                row = packed >> 7
                offset = position - shift
                inside = (offset >= 0) & (offset < 128)
                grid = grid_a if piece % 2 == 0 else grid_b
                window = pl.ds(row, 8)
                grid[window, :] = grid[window, :] + jnp.where(inside, both, 0.0)
        return carry

    lax.fori_loop(0, BANDS * SLOTS // 8, place, 0, unroll=4)

    first = first_ref[...]
    second = second_ref[...]
    cosine = twiddle_ref[0]
    sine = twiddle_ref[1]

    def band_step(band, carry):
        where = pl.ds(pl.multiple_of(band * 128, 128), 128)
        cells = grid_a[where, :] + grid_b[where, :]
        high = cells.astype(BF16)
        low = (cells - high.astype(F32)).astype(BF16)
        section = jnp.dot(
            first, jnp.concatenate([high, low, high], axis=0), preferred_element_type=F32
        )
        real = jnp.concatenate([section[:64], section[:64]], axis=0)
        imag = jnp.concatenate([section[64:], section[64:]], axis=0)
        turned = jnp.concatenate(
            [real * cosine - imag * sine, real * sine + imag * cosine], axis=1
        )
        high = turned.astype(BF16)
        low = (turned - high.astype(F32)).astype(BF16)
        contract = (((1,), (1,)), ((), ()))
        main = lax.dot_general(second, high, contract, preferred_element_type=F32)
        rest = lax.dot_general(second[:128], low, contract, preferred_element_type=F32)
        spectrum = main[:128] + main[128:] + rest
        rows_ref[pl.ds(band, 64, stride=STRIDE), :] = spectrum[:64]
        rows_ref[pl.ds(64 + band, 64, stride=STRIDE), :] = spectrum[64:]
        return carry

    lax.fori_loop(0, BANDS, band_step, 0, unroll=4)

    table = bands_ref[...]

    def block_step(index, carry):
        rows = rows_ref[pl.ds(index * STRIDE, 128), :].astype(BF16)
        section = jnp.dot(table, jnp.concatenate([rows, rows], axis=0), preferred_element_type=F32)
        section = section.astype(BF16)
        parts, _, length, _ = done_ref.shape
        for part in range(parts):
            done_ref[part, index] = section[length * part : length * part + length]
        return carry

    outgoing = []
    for group in range(4):
        lax.fori_loop(16 * group, 16 * group + 16, block_step, 0, unroll=4)
        where = pl.ds(16 * group, 16)
        copy = pltpu.make_async_copy(
            done_ref.at[:, where], out_ref.at[:, where], out_sems.at[group]
        )
        copy.start()
        outgoing.append(copy)
    for copy in outgoing:
        copy.wait()


def grid_and_rows(places, arrived, first, twiddle, second, bands, parts):
    shape = (parts, 64, 128 // parts, 128)
    vmem = pl.BlockSpec(memory_space=pltpu.VMEM)
    anywhere = pl.BlockSpec(memory_space=pl.ANY)
    return pl.pallas_call(
        grid_kernel,
        in_specs=[pl.BlockSpec(memory_space=pltpu.SMEM), anywhere, vmem, vmem, vmem, vmem],
        out_specs=anywhere,
        out_shape=jax.ShapeDtypeStruct(shape, BF16),
        scratch_shapes=[
            pltpu.VMEM((ROWS + 8, 128), F32),
            pltpu.VMEM((ROWS + 8, 128), F32),
            pltpu.VMEM((64 * STRIDE, 128), F32),
            pltpu.VMEM((64, 128, 128), BF16),
            pltpu.VMEM(shape, BF16),
            pltpu.SemaphoreType.DMA,
            pltpu.SemaphoreType.DMA((4,)),
        ],
        compiler_params=pltpu.CompilerParams(vmem_limit_bytes=62 * MIB),
        cost_estimate=pl.CostEstimate(flops=20_000_000_000, bytes_accessed=4 << 20, transcendentals=0),
        name="place_and_transform",
    )(places, arrived, first, twiddle, second, bands)


def deal_kernel(turn_ref, columns_ref, *out_refs):
    for step, out_ref in enumerate(out_refs):
        begin = ((turn_ref[0] + step) & 3) * 32
        for group in range(2):
            where = pl.ds(pl.multiple_of(begin + 16 * group, 16), 16)
            rows = jnp.swapaxes(columns_ref[:, where, :], 0, 1).reshape(8, 128, 128)
            out_ref[8 * group : 8 * group + 8] = rows


def deal_rows(turn, columns):
    vmem = pl.BlockSpec(memory_space=pltpu.VMEM)
    return pl.pallas_call(
        deal_kernel,
        in_specs=[pl.BlockSpec(memory_space=pltpu.SMEM), vmem],
        out_specs=[vmem] * 4,
        out_shape=[jax.ShapeDtypeStruct((16, 128, 128), BF16)] * 4,
        compiler_params=pltpu.CompilerParams(vmem_limit_bytes=16 * MIB),
        cost_estimate=pl.CostEstimate(flops=1 << 20, bytes_accessed=4 << 20, transcendentals=0),
        name="deal_rows",
    )(turn, columns)


def base_phases(turn, me, w):
    k = jnp.arange(16, dtype=jnp.int32)[:, None, None]
    row = 64 * ((jnp.arange(128, dtype=jnp.int32)[:, None] + 32 * turn) % 128) + 16 * turn + k
    column = 128 * me + jnp.arange(128, dtype=jnp.int32)
    x = (row.astype(F32) - N // 2) / N
    y = (column.astype(F32) - N // 2) / N
    term = jnp.sqrt(1.0 - (x**2 + y**2)) - 1.0
    angle = (2.0 * math.pi) * w[:, None, None] * term[8]
    return jnp.stack([jnp.cos(angle), jnp.sin(angle)]), term - term[8]


def column_kernel(
    turn_ref, w_ref, early_0, early_1, early_2, early_3, late_ref, table_ref, base_hbm, change_hbm,
    own_ref, sent_1, sent_2, sent_3, early, late, rows, base_ref, change_ref, sems,
):
    arrivals = ([], [])

    def fetch(half, source, target):
        number = len(arrivals[0]) + len(arrivals[1])
        copy = pltpu.make_async_copy(source, target, sems.at[number])
        copy.start()
        arrivals[half].append(copy)

    for half in range(2):
        k = pl.ds(8 * half, 8)
        pairs = pl.ds(16 * half, 16)
        fetch(half, late_ref.at[:, :, pairs], late.at[:, :, pairs])
        for step, source in enumerate((early_0, early_1, early_2, early_3)):
            fetch(half, source.at[k], early.at[step, k])
        fetch(half, change_hbm.at[k], change_ref.at[k])
        if half == 0:
            fetch(half, base_hbm, base_ref)

    turn = turn_ref[0]
    table = table_ref[...]
    targets = (own_ref, sent_1, sent_2, sent_3)

    def one(k, carry):
        sky = []
        for pair in (0, 2):
            cells = jnp.concatenate(
                [
                    jnp.concatenate([early[step, k], rows[step, k]], axis=0)
                    for step in (pair, pair + 1)
                ],
                axis=1,
            )
            sky.append(
                jnp.dot(table, jnp.concatenate([cells, cells], axis=0), preferred_element_type=F32)
            )
        for block, target in enumerate(targets):
            where = slice(32 * block, 32 * block + 32)
            change = change_ref[k, where]
            image = jnp.zeros((32, 128), F32)
            for step in range(4):
                part = sky[step // 2][:, 128 * (step % 2) : 128 * (step % 2) + 128]
                real = part[:128][where]
                imag = part[128:][where]
                angle = (2.0 * math.pi * w_ref[step]) * change
                square = angle * angle
                sine = angle * (1.0 - square * (1.0 / 6.0))
                cosine = 1.0 - square * (0.5 - square * (1.0 / 24.0))
                image += (real * cosine - imag * sine) * base_ref[0, step, where]
                image -= (real * sine + imag * cosine) * base_ref[1, step, where]
            target[k] = image.astype(target.dtype)
        return carry

    for half in range(2):
        for copy in arrivals[half]:
            copy.wait()
        for step in range(4):
            block = late[(turn - step) & 3, :, 16 * half : 16 * half + 16]
            rows[step, 8 * half : 8 * half + 8] = jnp.swapaxes(block, 0, 1).reshape(8, 128, 128)
        lax.fori_loop(8 * half, 8 * half + 8, one, 0, unroll=4)


def column_transform(turn, w, early, late, table, base, change):
    smem = pl.BlockSpec(memory_space=pltpu.SMEM)
    vmem = pl.BlockSpec(memory_space=pltpu.VMEM)
    anywhere = pl.BlockSpec(memory_space=pl.ANY)
    return pl.pallas_call(
        column_kernel,
        in_specs=[smem] * 2 + [anywhere] * 5 + [vmem] + [anywhere] * 2,
        out_specs=[vmem] * 4,
        out_shape=[jax.ShapeDtypeStruct((16, 32, 128), F32)]
        + [jax.ShapeDtypeStruct((16, 32, 128), BF16)] * 3,
        scratch_shapes=[
            pltpu.VMEM((4, 16, 128, 128), BF16),
            pltpu.VMEM((4, 64, 32, 128), BF16),
            pltpu.VMEM((4, 16, 128, 128), BF16),
            pltpu.VMEM((2, 4, 128, 128), F32),
            pltpu.VMEM((16, 128, 128), F32),
            pltpu.SemaphoreType.DMA((13,)),
        ],
        compiler_params=pltpu.CompilerParams(vmem_limit_bytes=62 * MIB),
        cost_estimate=pl.CostEstimate(
            flops=4_300_000_000, bytes_accessed=5 << 20, transcendentals=0
        ),
        name="column_transform",
    )(turn, w, *early, late, table, base, change)


def place_kernel(turn_ref, *refs):
    out_ref = refs[-1]
    for step, block_ref in enumerate(refs[:-1]):
        begin = ((turn_ref[0] - step) & 3) * 16
        for group in (0, 8):
            rows = jnp.swapaxes(block_ref[group : group + 8].astype(F32), 0, 1)
            out_ref[:, pl.ds(pl.multiple_of(begin + group, 8), 8), :] = rows


def place_rows(turn, blocks):
    vmem = pl.BlockSpec(memory_space=pltpu.VMEM)
    return pl.pallas_call(
        place_kernel,
        in_specs=[pl.BlockSpec(memory_space=pltpu.SMEM)] + [vmem] * 4,
        out_specs=vmem,
        out_shape=jax.ShapeDtypeStruct((32, 64, 128), F32),
        compiler_params=pltpu.CompilerParams(vmem_limit_bytes=16 * MIB),
        cost_estimate=pl.CostEstimate(flops=1 << 20, bytes_accessed=2 << 20, transcendentals=0),
        name="place_image_rows",
    )(turn, *blocks)


def along_wp(block, step):
    pairs = [(plane, (plane + step) % 4) for plane in range(4)]
    return lax.ppermute(block, "wp", pairs)


def band_table(row):
    k = jnp.arange(64, dtype=jnp.int32)[:, None]
    band = jnp.arange(64, dtype=jnp.int32)[None, :]
    angle = (2.0 * math.pi / N) * ((k * (128 * band + row)) % N).astype(F32)
    cosine = jnp.cos(angle)
    sine = jnp.sin(angle)
    real = jnp.concatenate([cosine, -sine], axis=1)
    imag = jnp.concatenate([sine, cosine], axis=1)
    table = jnp.stack([real, imag], axis=1).reshape(128, 128)
    high = lax.reduce_precision(table, 8, 7)
    low = lax.reduce_precision(table - high, 8, 7)
    return jnp.concatenate([high, low], axis=1).astype(BF16)


def local(uv_tiles, target_bands, uv_offsets, tile_counts, plane_w):
    me = lax.axis_index("band")
    first = jnp.asarray(row_first_table())
    twiddle = jnp.asarray(row_twiddles())
    second = jnp.asarray(row_second_table())

    arrived = []
    for half in range(2):
        packed = pack(tile_counts, target_bands[0].T, uv_offsets[0].T, uv_tiles[0], half)
        arrived.append(
            lax.all_to_all(packed, "band", split_axis=0, concat_axis=0, tiled=True)
        )
    numbers = arrived[0][:, 128:131, :64].astype(jnp.int32)
    places = (numbers[:, 0] * 64 + numbers[:, 1]) * 256 + numbers[:, 2]
    turn = lax.axis_index("wp")[None]
    w = jnp.concatenate([plane_w, along_wp(plane_w, 1)])
    w = jnp.concatenate([w, along_wp(w, 2)])
    base, change = base_phases(turn[0], me, w)
    places, base, change = lax.optimization_barrier((places, base, change))

    early = late = None
    for half in range(2):
        spectrum = grid_and_rows(
            places, arrived[half], first, twiddle, second, band_table(me + 64 * half), 4 if half else 1
        )
        if half == 0:
            early = lax.all_to_all(
                spectrum.reshape(64, 128, 128), "band", split_axis=0, concat_axis=0, tiled=True
            )
        else:
            late = lax.all_to_all(
                spectrum.reshape(256, 32, 128), ("wp", "band"), split_axis=0, concat_axis=0, tiled=True
            ).reshape(4, 64, 32, 128)

    dealt = deal_rows(turn, early)
    dealt = [dealt[0]] + [along_wp(dealt[step], step) for step in (1, 2, 3)]
    table = jnp.roll(jnp.asarray(column_second_table()).reshape(2, 128, 512), -32 * turn[0], axis=1)
    own, *sent = column_transform(
        turn, w, dealt, late, table.reshape(256, 512), base, change
    )
    blocks = [own] + [along_wp(block, step + 1) for step, block in enumerate(sent)]
    return place_rows(turn, blocks).reshape(2048, 128)


def solution(mesh):
    placed = (
        P("wp", "band", None, None, None),
        P("wp", "band", None),
        P("wp", "band", None),
        P("wp", "band"),
        P("wp"),
    )
    return jax.shard_map(
        local, mesh=mesh, in_specs=placed, out_specs=P("wp", "band"), check_vma=False
    )
```

```python
import functools
import math

import jax
import jax.numpy as jnp
import ml_dtypes
import numpy as np
from jax import lax
from jax.experimental import pallas as pl
from jax.experimental.pallas import tpu as pltpu
from jax.sharding import PartitionSpec as P

N = 8192
BANDS = 64
EDGE = 128
SLOTS = 64
ROWS = 8192
STRIDE = 129
F32 = jnp.float32
BF16 = jnp.bfloat16
MIB = 1 << 20


def circle(numerator, length):
    angle = 2.0 * np.pi * (np.asarray(numerator) % length) / length
    return np.cos(angle), np.sin(angle)


def split(table):
    high = table.astype(ml_dtypes.bfloat16)
    low = (table - high.astype(np.float64)).astype(ml_dtypes.bfloat16)
    return high, low


def row_first_table():
    cosine, sine = circle(np.arange(64)[:, None] * np.arange(64)[None, :], 64)
    table = np.zeros((2, 64, 64, 2))
    table[0, :, :, 0] = cosine
    table[0, :, :, 1] = -sine
    table[1, :, :, 0] = sine
    table[1, :, :, 1] = cosine
    high, low = split(table.reshape(128, 128))
    return np.concatenate([high, high, low], axis=1)


def row_twiddles():
    cosine, sine = circle(np.arange(128)[:, None] * np.arange(128)[None, :], N)
    return np.stack([cosine, sine]).astype(np.float32)


def row_second_table():
    cosine, sine = circle(np.arange(64)[:, None] * np.arange(128)[None, :], 64)
    table = np.block([[cosine, -sine], [sine, cosine]])
    high, low = split(table)
    return np.concatenate([high, low], axis=0)


def column_second_table(half):
    cosine, sine = circle(np.arange(128)[:, None] * np.arange(128)[None, :], 128)
    table = np.zeros((2, 128, 2, 2, 64))
    cosine = cosine.reshape(128, 2, 64) / N
    sine = sine.reshape(128, 2, 64) / N
    table[0, :, :, 0] = cosine
    table[0, :, :, 1] = -sine
    table[1, :, :, 0] = sine
    table[1, :, :, 1] = cosine
    high, low = split(table[:, :, half].reshape(256, 128))
    return np.concatenate([high, low], axis=1)


def pack_kernel(
    count_ref, band_ref, offset_ref, tiles_ref, out_ref, held_ref, rows_ref, done_ref, in_sems, out_sems,
    *, half
):
    groups = 8
    each = SLOTS // groups
    incoming = []
    for group in range(groups):
        where = pl.ds(each * group, each)
        copy = pltpu.make_async_copy(
            tiles_ref.at[where, :, pl.ds(64 * half, 64), :], held_ref.at[where], in_sems.at[group]
        )
        copy.start()
        incoming.append(copy)

    count = count_ref[0, 0]
    if half == 0:
        row = lax.broadcasted_iota(jnp.int32, (8, 128), 0)
        lane = lax.broadcasted_iota(jnp.int32, (8, 128), 1)

        def number(slot, values):
            column = offset_ref[1, slot]
            values = jnp.where((row == 0) & (lane == slot), band_ref[0, slot], values)
            values = jnp.where((row == 1) & (lane == slot), column >> 7, values)
            return jnp.where((row == 2) & (lane == slot), column & 127, values)

        values = lax.fori_loop(0, SLOTS, number, jnp.zeros((8, 128), jnp.int32), unroll=4)
        places = values.astype(F32).astype(BF16)

    def one(slot, carry):
        shift = offset_ref[1, slot] & 127
        keep = slot < count
        tile = pltpu.roll(held_ref[slot].astype(F32).reshape(128, 128), shift, 1)
        tile = jnp.where(keep, tile, 0.0)
        for part in range(2):
            where = pl.ds(slot * 2 + part, 64, stride=STRIDE)
            rows_ref[where, :] = tile[64 * part : 64 * part + 64]
        return carry

    for group in range(groups):
        incoming[group].wait()
        lax.fori_loop(each * group, each * group + each, one, 0, unroll=8)

    def cast(block, carry):
        done_ref[block, :128] = rows_ref[pl.ds(block * STRIDE, 128), :].astype(BF16)
        if half == 0:
            done_ref[block, 128:] = places
        return carry

    outgoing = []
    for group in range(4):
        lax.fori_loop(16 * group, 16 * group + 16, cast, 0, unroll=4)
        where = pl.ds(16 * group, 16)
        copy = pltpu.make_async_copy(done_ref.at[where], out_ref.at[where], out_sems.at[group])
        copy.start()
        outgoing.append(copy)
    for copy in outgoing:
        copy.wait()


def pack(count, bands, offsets, tiles, half):
    length = 128 if half else 136
    smem = pl.BlockSpec(memory_space=pltpu.SMEM)
    anywhere = pl.BlockSpec(memory_space=pl.ANY)
    return pl.pallas_call(
        functools.partial(pack_kernel, half=half),
        in_specs=[smem, smem, smem, anywhere],
        out_specs=anywhere,
        out_shape=jax.ShapeDtypeStruct((64, length, 128), BF16),
        scratch_shapes=[
            pltpu.VMEM((SLOTS, 2, 64, 128), BF16),
            pltpu.VMEM((64 * STRIDE, 128), F32),
            pltpu.VMEM((64, length, 128), BF16),
            pltpu.SemaphoreType.DMA((8,)),
            pltpu.SemaphoreType.DMA((4,)),
        ],
        compiler_params=pltpu.CompilerParams(vmem_limit_bytes=62 * MIB),
        cost_estimate=pl.CostEstimate(flops=8 << 20, bytes_accessed=4 << 20, transcendentals=0),
        name="pack_rows",
    )(count, bands, offsets, tiles)


def grid_kernel(
    place_ref, arrived_ref, first_ref, twiddle_ref, second_ref, bands_ref, out_ref,
    grid_a, grid_b, rows_ref, pieces_ref, done_ref, in_sem, out_sems,
):
    incoming = pltpu.make_async_copy(arrived_ref.at[:, pl.ds(0, 128), :], pieces_ref, in_sem)
    incoming.start()

    def clear(index, carry):
        where = pl.ds(pl.multiple_of(index * 64, 64), 64)
        grid_a[where, :] = jnp.zeros((64, 128), F32)
        grid_b[where, :] = jnp.zeros((64, 128), F32)
        return carry

    lax.fori_loop(0, ROWS // 64, clear, 0)
    grid_a[pl.ds(ROWS, 8), :] = jnp.zeros((8, 128), F32)
    grid_b[pl.ds(ROWS, 8), :] = jnp.zeros((8, 128), F32)

    incoming.wait()
    sublane = lax.broadcasted_iota(jnp.int32, (8, 128), 0)
    lane = lax.broadcasted_iota(jnp.int32, (8, 128), 1)
    position = lane + (sublane // 2) * 128
    upper = sublane < 2

    def place(index, carry):
        source = index >> 3
        slot = (index & 7) * 8
        pieces = pieces_ref[source, pl.ds(pl.multiple_of(slot * 2, 16), 16), :].astype(F32)
        for part in range(2):
            block = pieces[8 * part : 8 * part + 8]
            turned = [block] + [pltpu.roll(block, 8 - 2 * turn, 0) for turn in (1, 2, 3)]
            for piece in range(4):
                both = jnp.where(upper, turned[piece], turned[(piece + 3) % 4])
                packed = place_ref[source, slot + part * 4 + piece]
                shift = packed & 127
                row = packed >> 7
                offset = position - shift
                inside = (offset >= 0) & (offset < 128)
                grid = grid_a if piece % 2 == 0 else grid_b
                window = pl.ds(row, 8)
                grid[window, :] = grid[window, :] + jnp.where(inside, both, 0.0)
        return carry

    lax.fori_loop(0, BANDS * SLOTS // 8, place, 0, unroll=4)

    first = first_ref[...]
    second = second_ref[...]
    cosine = twiddle_ref[0]
    sine = twiddle_ref[1]

    def band_step(band, carry):
        where = pl.ds(pl.multiple_of(band * 128, 128), 128)
        cells = grid_a[where, :] + grid_b[where, :]
        high = cells.astype(BF16)
        low = (cells - high.astype(F32)).astype(BF16)
        section = jnp.dot(
            first, jnp.concatenate([high, low, high], axis=0), preferred_element_type=F32
        )
        real = jnp.concatenate([section[:64], section[:64]], axis=0)
        imag = jnp.concatenate([section[64:], section[64:]], axis=0)
        turned = jnp.concatenate(
            [real * cosine - imag * sine, real * sine + imag * cosine], axis=1
        )
        high = turned.astype(BF16)
        low = (turned - high.astype(F32)).astype(BF16)
        contract = (((1,), (1,)), ((), ()))
        main = lax.dot_general(second, high, contract, preferred_element_type=F32)
        rest = lax.dot_general(second[:128], low, contract, preferred_element_type=F32)
        spectrum = main[:128] + main[128:] + rest
        rows_ref[pl.ds(band, 64, stride=STRIDE), :] = spectrum[:64]
        rows_ref[pl.ds(64 + band, 64, stride=STRIDE), :] = spectrum[64:]
        return carry

    lax.fori_loop(0, BANDS, band_step, 0, unroll=4)

    table = bands_ref[...]

    def block_step(index, carry):
        rows = rows_ref[pl.ds(index * STRIDE, 128), :].astype(BF16)
        section = jnp.dot(table, jnp.concatenate([rows, rows], axis=0), preferred_element_type=F32)
        section = section.astype(BF16)
        parts, _, length, _ = done_ref.shape
        for part in range(parts):
            done_ref[part, index] = section[length * part : length * part + length]
        return carry

    outgoing = []
    for group in range(4):
        lax.fori_loop(16 * group, 16 * group + 16, block_step, 0, unroll=4)
        where = pl.ds(16 * group, 16)
        copy = pltpu.make_async_copy(
            done_ref.at[:, where], out_ref.at[:, where], out_sems.at[group]
        )
        copy.start()
        outgoing.append(copy)
    for copy in outgoing:
        copy.wait()


def grid_and_rows(places, arrived, first, twiddle, second, bands, parts):
    shape = (parts, 64, 128 // parts, 128)
    vmem = pl.BlockSpec(memory_space=pltpu.VMEM)
    anywhere = pl.BlockSpec(memory_space=pl.ANY)
    return pl.pallas_call(
        grid_kernel,
        in_specs=[pl.BlockSpec(memory_space=pltpu.SMEM), anywhere, vmem, vmem, vmem, vmem],
        out_specs=anywhere,
        out_shape=jax.ShapeDtypeStruct(shape, BF16),
        scratch_shapes=[
            pltpu.VMEM((ROWS + 8, 128), F32),
            pltpu.VMEM((ROWS + 8, 128), F32),
            pltpu.VMEM((64 * STRIDE, 128), F32),
            pltpu.VMEM((64, 128, 128), BF16),
            pltpu.VMEM(shape, BF16),
            pltpu.SemaphoreType.DMA,
            pltpu.SemaphoreType.DMA((4,)),
        ],
        compiler_params=pltpu.CompilerParams(vmem_limit_bytes=62 * MIB),
        cost_estimate=pl.CostEstimate(flops=20_000_000_000, bytes_accessed=4 << 20, transcendentals=0),
        name="place_and_transform",
    )(places, arrived, first, twiddle, second, bands)


def deal_kernel(turn_ref, columns_ref, *out_refs):
    for step, out_ref in enumerate(out_refs):
        begin = ((turn_ref[0] + step) & 3) * 32
        for group in range(2):
            where = pl.ds(pl.multiple_of(begin + 16 * group, 16), 16)
            rows = jnp.swapaxes(columns_ref[:, where, :], 0, 1).reshape(8, 128, 128)
            out_ref[8 * group : 8 * group + 8] = rows


def deal_rows(turn, columns):
    vmem = pl.BlockSpec(memory_space=pltpu.VMEM)
    return pl.pallas_call(
        deal_kernel,
        in_specs=[pl.BlockSpec(memory_space=pltpu.SMEM), vmem],
        out_specs=[vmem] * 4,
        out_shape=[jax.ShapeDtypeStruct((16, 128, 128), BF16)] * 4,
        compiler_params=pltpu.CompilerParams(vmem_limit_bytes=16 * MIB),
        cost_estimate=pl.CostEstimate(flops=1 << 20, bytes_accessed=4 << 20, transcendentals=0),
        name="deal_rows",
    )(turn, columns)


def base_phases(turn, me, w):
    k = jnp.arange(16, dtype=jnp.int32)[:, None, None]
    row = 64 * ((jnp.arange(128, dtype=jnp.int32)[:, None] + 32 * turn) % 128) + 16 * turn + k
    column = 128 * me + jnp.arange(128, dtype=jnp.int32)
    x = (row.astype(F32) - N // 2) / N
    y = (column.astype(F32) - N // 2) / N
    term = jnp.sqrt(1.0 - (x**2 + y**2)) - 1.0
    angle = (2.0 * math.pi) * w[:, None, None] * term[8]
    return jnp.stack([jnp.cos(angle), jnp.sin(angle)]), (term - term[8]).astype(BF16)


def transform_planes(table_ref, cells):
    sky = []
    for pair in (0, 2):
        both = jnp.concatenate([cells[pair], cells[pair + 1]], axis=1)
        sky.append(
            jnp.dot(
                table_ref[...], jnp.concatenate([both, both], axis=0), preferred_element_type=F32
            )
        )
    return sky


def add_planes(image, sky, where, change, w_ref, base_ref):
    for step in range(4):
        part = sky[step // 2][:, 128 * (step % 2) : 128 * (step % 2) + 128]
        real = part[:128][where]
        imag = part[128:][where]
        angle = (2.0 * math.pi * w_ref[step]) * change
        square = angle * angle
        sine = angle * (1.0 - square * (1.0 / 6.0))
        cosine = 1.0 - square * (0.5 - square * (1.0 / 24.0))
        image += (real * cosine - imag * sine) * base_ref[0, step, where]
        image -= (real * sine + imag * cosine) * base_ref[1, step, where]
    return image


def early_kernel(w_ref, early_0, early_1, early_2, early_3, table_ref, base_ref, change_ref, out_ref):
    def one(k, carry):
        sky = transform_planes(table_ref, [ref[k] for ref in (early_0, early_1, early_2, early_3)])
        for block in range(4):
            where = slice(32 * block, 32 * block + 32)
            change = change_ref[k, where].astype(F32)
            out_ref[k, where] = add_planes(
                jnp.zeros((32, 128), F32), sky, where, change, w_ref, base_ref
            )
        return carry

    lax.fori_loop(0, 16, one, 0, unroll=2)


def early_image(w, early, table, base, change):
    vmem = pl.BlockSpec(memory_space=pltpu.VMEM)
    return pl.pallas_call(
        early_kernel,
        in_specs=[pl.BlockSpec(memory_space=pltpu.SMEM)] + [vmem] * 7,
        out_specs=vmem,
        out_shape=jax.ShapeDtypeStruct((16, 128, 128), F32),
        compiler_params=pltpu.CompilerParams(vmem_limit_bytes=62 * MIB),
        cost_estimate=pl.CostEstimate(
            flops=2_200_000_000, bytes_accessed=5 << 20, transcendentals=0
        ),
        name="early_column_transform",
    )(w, *early, table, base, change)


def late_kernel(
    turn_ref, w_ref, early_hbm, late_hbm, table_hbm, base_hbm, change_hbm,
    own_hbm, sent_1, sent_2, sent_3, early_ref, late_ref, rows_ref, table_ref, base_ref, change_ref,
    own_ref, sent_ref, in_sems, out_sems,
):
    def fetch(half):
        k = pl.ds(8 * half, 8)
        pairs = pl.ds(16 * half, 16)
        moves = [
            (late_hbm.at[:, :, pairs], late_ref.at[:, :, pairs]),
            (early_hbm.at[k], early_ref.at[k]),
            (change_hbm.at[k], change_ref.at[k]),
        ]
        if half == 0:
            moves += [(table_hbm, table_ref), (base_hbm, base_ref)]
        copies = []
        for number, (source, target) in enumerate(moves):
            copy = pltpu.make_async_copy(source, target, in_sems.at[5 * half + number])
            copy.start()
            copies.append(copy)
        return copies

    def one(k, carry):
        sky = transform_planes(table_ref, [rows_ref[step, k] for step in range(4)])
        for block in range(4):
            where = slice(32 * block, 32 * block + 32)
            change = change_ref[k, where].astype(F32)
            image = add_planes(early_ref[k, where], sky, where, change, w_ref, base_ref)
            if block == 0:
                own_ref[k] = image
            else:
                sent_ref[block - 1, k] = image.astype(BF16)
        return carry

    turn = turn_ref[0]
    incoming = fetch(0)
    outgoing = []
    for half in range(2):
        for copy in incoming:
            copy.wait()
        if half == 0:
            incoming = fetch(1)
        for step in range(4):
            block = late_ref[(turn - step) & 3, :, 16 * half : 16 * half + 16]
            rows_ref[step, 8 * half : 8 * half + 8] = jnp.swapaxes(block, 0, 1).reshape(8, 128, 128)
        lax.fori_loop(8 * half, 8 * half + 8, one, 0, unroll=4)
        k = pl.ds(8 * half, 8)
        moves = [(sent_ref.at[0, k], sent_1.at[k]), (sent_ref.at[1, k], sent_2.at[k])]
        moves += [(sent_ref.at[2, k], sent_3.at[k]), (own_ref.at[k], own_hbm.at[k])]
        for number, (source, target) in enumerate(moves):
            copy = pltpu.make_async_copy(source, target, out_sems.at[4 * half + number])
            copy.start()
            outgoing.append(copy)
    for copy in outgoing:
        copy.wait()


def late_image(turn, w, early, late, table, base, change):
    smem = pl.BlockSpec(memory_space=pltpu.SMEM)
    anywhere = pl.BlockSpec(memory_space=pl.ANY)
    return pl.pallas_call(
        late_kernel,
        in_specs=[smem] * 2 + [anywhere] * 5,
        out_specs=[anywhere] * 4,
        out_shape=[jax.ShapeDtypeStruct((16, 32, 128), F32)]
        + [jax.ShapeDtypeStruct((16, 32, 128), BF16)] * 3,
        scratch_shapes=[
            pltpu.VMEM((16, 128, 128), F32),
            pltpu.VMEM((4, 64, 32, 128), BF16),
            pltpu.VMEM((4, 16, 128, 128), BF16),
            pltpu.VMEM((256, 256), BF16),
            pltpu.VMEM((2, 4, 128, 128), F32),
            pltpu.VMEM((16, 128, 128), BF16),
            pltpu.VMEM((16, 32, 128), F32),
            pltpu.VMEM((3, 16, 32, 128), BF16),
            pltpu.SemaphoreType.DMA((10,)),
            pltpu.SemaphoreType.DMA((8,)),
        ],
        compiler_params=pltpu.CompilerParams(vmem_limit_bytes=62 * MIB),
        cost_estimate=pl.CostEstimate(
            flops=2_200_000_000, bytes_accessed=5 << 20, transcendentals=0
        ),
        name="late_column_transform",
    )(turn, w, early, late, table, base, change)


def place_kernel(turn_ref, *refs):
    out_ref = refs[-1]
    for step, block_ref in enumerate(refs[:-1]):
        begin = ((turn_ref[0] - step) & 3) * 16
        for group in (0, 8):
            rows = jnp.swapaxes(block_ref[group : group + 8].astype(F32), 0, 1)
            out_ref[:, pl.ds(pl.multiple_of(begin + group, 8), 8), :] = rows


def place_rows(turn, blocks):
    vmem = pl.BlockSpec(memory_space=pltpu.VMEM)
    return pl.pallas_call(
        place_kernel,
        in_specs=[pl.BlockSpec(memory_space=pltpu.SMEM)] + [vmem] * 4,
        out_specs=vmem,
        out_shape=jax.ShapeDtypeStruct((32, 64, 128), F32),
        compiler_params=pltpu.CompilerParams(vmem_limit_bytes=62 * MIB),
        cost_estimate=pl.CostEstimate(flops=1 << 20, bytes_accessed=2 << 20, transcendentals=0),
        name="place_image_rows",
    )(turn, *blocks)


def along_wp(block, step):
    pairs = [(plane, (plane + step) % 4) for plane in range(4)]
    return lax.ppermute(block, "wp", pairs)


def band_table(row):
    k = jnp.arange(64, dtype=jnp.int32)[:, None]
    band = jnp.arange(64, dtype=jnp.int32)[None, :]
    angle = (2.0 * math.pi / N) * ((k * (128 * band + row)) % N).astype(F32)
    cosine = jnp.cos(angle)
    sine = jnp.sin(angle)
    real = jnp.concatenate([cosine, -sine], axis=1)
    imag = jnp.concatenate([sine, cosine], axis=1)
    table = jnp.stack([real, imag], axis=1).reshape(128, 128)
    high = lax.reduce_precision(table, 8, 7)
    low = lax.reduce_precision(table - high, 8, 7)
    return jnp.concatenate([high, low], axis=1).astype(BF16)


def local(uv_tiles, target_bands, uv_offsets, tile_counts, plane_w):
    me = lax.axis_index("band")
    first = jnp.asarray(row_first_table())
    twiddle = jnp.asarray(row_twiddles())
    second = jnp.asarray(row_second_table())

    arrived = []
    for half in range(2):
        packed = pack(tile_counts, target_bands[0].T, uv_offsets[0].T, uv_tiles[0], half)
        arrived.append(
            lax.all_to_all(packed, "band", split_axis=0, concat_axis=0, tiled=True)
        )
    numbers = arrived[0][:, 128:131, :64].astype(jnp.int32)
    places = (numbers[:, 0] * 64 + numbers[:, 1]) * 256 + numbers[:, 2]
    turn = lax.axis_index("wp")[None]
    w = jnp.concatenate([plane_w, along_wp(plane_w, 1)])
    w = jnp.concatenate([w, along_wp(w, 2)])
    base, change = base_phases(turn[0], me, w)
    places, base, change = lax.optimization_barrier((places, base, change))

    early = late = None
    for half in range(2):
        spectrum = grid_and_rows(
            places, arrived[half], first, twiddle, second, band_table(me + 64 * half), 4 if half else 1
        )
        if half == 0:
            early = lax.all_to_all(
                spectrum.reshape(64, 128, 128), "band", split_axis=0, concat_axis=0, tiled=True
            )
        else:
            late = lax.all_to_all(
                spectrum.reshape(256, 32, 128), ("wp", "band"), split_axis=0, concat_axis=0, tiled=True
            ).reshape(4, 64, 32, 128)

    dealt = deal_rows(turn, early)
    dealt = [dealt[0]] + [along_wp(dealt[step], step) for step in (1, 2, 3)]
    tables = [
        jnp.roll(jnp.asarray(column_second_table(half)).reshape(2, 128, 256), -32 * turn[0], axis=1)
        for half in range(2)
    ]
    tables = [table.reshape(256, 256) for table in tables]
    early = early_image(w, dealt, tables[0], base, change)
    own, *sent = late_image(turn, w, early, late, tables[1], base, change)
    blocks = [own] + [along_wp(block, step + 1) for step, block in enumerate(sent)]
    return place_rows(turn, blocks).reshape(2048, 128)


def solution(mesh):
    placed = (
        P("wp", "band", None, None, None),
        P("wp", "band", None),
        P("wp", "band", None),
        P("wp", "band"),
        P("wp"),
    )
    return jax.shard_map(
        local, mesh=mesh, in_specs=placed, out_specs=P("wp", "band"), check_vma=False
    )
```

```python
import functools
import math

import jax
import jax.numpy as jnp
import ml_dtypes
import numpy as np
from jax import lax
from jax.experimental import pallas as pl
from jax.experimental.pallas import tpu as pltpu
from jax.sharding import PartitionSpec as P

N = 8192
BANDS = 64
EDGE = 128
SLOTS = 64
ROWS = 8192
STRIDE = 129
F32 = jnp.float32
BF16 = jnp.bfloat16
MIB = 1 << 20


def circle(numerator, length):
    angle = 2.0 * np.pi * (np.asarray(numerator) % length) / length
    return np.cos(angle), np.sin(angle)


def split(table):
    high = table.astype(ml_dtypes.bfloat16)
    low = (table - high.astype(np.float64)).astype(ml_dtypes.bfloat16)
    return high, low


def row_first_table():
    cosine, sine = circle(np.arange(64)[:, None] * np.arange(64)[None, :], 64)
    table = np.zeros((2, 64, 64, 2))
    table[0, :, :, 0] = cosine
    table[0, :, :, 1] = -sine
    table[1, :, :, 0] = sine
    table[1, :, :, 1] = cosine
    high, low = split(table.reshape(128, 128))
    return np.concatenate([high, high, low], axis=1)


def row_twiddles():
    cosine, sine = circle(np.arange(128)[:, None] * np.arange(128)[None, :], N)
    return np.stack([cosine, sine]).astype(np.float32)


def row_second_table():
    cosine, sine = circle(np.arange(64)[:, None] * np.arange(128)[None, :], 64)
    table = np.block([[cosine, -sine], [sine, cosine]])
    high, low = split(table)
    return np.concatenate([high, low], axis=0)


def column_second_table(half):
    cosine, sine = circle(np.arange(128)[:, None] * np.arange(128)[None, :], 128)
    table = np.zeros((2, 128, 2, 2, 64))
    cosine = cosine.reshape(128, 2, 64) / N
    sine = sine.reshape(128, 2, 64) / N
    table[0, :, :, 0] = cosine
    table[0, :, :, 1] = -sine
    table[1, :, :, 0] = sine
    table[1, :, :, 1] = cosine
    high, low = split(table[:, :, half].reshape(256, 128))
    return np.concatenate([high, low], axis=1)


def pack_kernel(
    count_ref, band_ref, offset_ref, tiles_ref, out_ref, held_ref, rows_ref, done_ref, in_sems, out_sems,
    *, half
):
    groups = 8
    each = SLOTS // groups
    incoming = []
    for group in range(groups):
        where = pl.ds(each * group, each)
        copy = pltpu.make_async_copy(
            tiles_ref.at[where, :, pl.ds(64 * half, 64), :], held_ref.at[where], in_sems.at[group]
        )
        copy.start()
        incoming.append(copy)

    count = count_ref[0, 0]
    if half == 0:
        row = lax.broadcasted_iota(jnp.int32, (8, 128), 0)
        lane = lax.broadcasted_iota(jnp.int32, (8, 128), 1)

        def number(slot, values):
            column = offset_ref[1, slot]
            values = jnp.where((row == 0) & (lane == slot), band_ref[0, slot], values)
            values = jnp.where((row == 1) & (lane == slot), column >> 7, values)
            return jnp.where((row == 2) & (lane == slot), column & 127, values)

        values = lax.fori_loop(0, SLOTS, number, jnp.zeros((8, 128), jnp.int32), unroll=4)
        places = values.astype(F32).astype(BF16)

    def one(slot, carry):
        shift = offset_ref[1, slot] & 127
        keep = slot < count
        tile = pltpu.roll(held_ref[slot].astype(F32).reshape(128, 128), shift, 1)
        tile = jnp.where(keep, tile, 0.0)
        for part in range(2):
            where = pl.ds(slot * 2 + part, 64, stride=STRIDE)
            rows_ref[where, :] = tile[64 * part : 64 * part + 64]
        return carry

    for group in range(groups):
        incoming[group].wait()
        lax.fori_loop(each * group, each * group + each, one, 0, unroll=8)

    def cast(block, carry):
        done_ref[block, :128] = rows_ref[pl.ds(block * STRIDE, 128), :].astype(BF16)
        if half == 0:
            done_ref[block, 128:] = places
        return carry

    outgoing = []
    for group in range(4):
        lax.fori_loop(16 * group, 16 * group + 16, cast, 0, unroll=4)
        where = pl.ds(16 * group, 16)
        copy = pltpu.make_async_copy(done_ref.at[where], out_ref.at[where], out_sems.at[group])
        copy.start()
        outgoing.append(copy)
    for copy in outgoing:
        copy.wait()


def pack(count, bands, offsets, tiles, half):
    length = 128 if half else 136
    smem = pl.BlockSpec(memory_space=pltpu.SMEM)
    anywhere = pl.BlockSpec(memory_space=pl.ANY)
    return pl.pallas_call(
        functools.partial(pack_kernel, half=half),
        in_specs=[smem, smem, smem, anywhere],
        out_specs=anywhere,
        out_shape=jax.ShapeDtypeStruct((64, length, 128), BF16),
        scratch_shapes=[
            pltpu.VMEM((SLOTS, 2, 64, 128), BF16),
            pltpu.VMEM((64 * STRIDE, 128), F32),
            pltpu.VMEM((64, length, 128), BF16),
            pltpu.SemaphoreType.DMA((8,)),
            pltpu.SemaphoreType.DMA((4,)),
        ],
        compiler_params=pltpu.CompilerParams(vmem_limit_bytes=62 * MIB),
        cost_estimate=pl.CostEstimate(flops=8 << 20, bytes_accessed=4 << 20, transcendentals=0),
        name="pack_rows",
    )(count, bands, offsets, tiles)


def grid_kernel(
    place_ref, arrived_ref, first_ref, twiddle_ref, second_ref, bands_ref, out_ref,
    grid_a, grid_b, rows_ref, pieces_ref, done_ref, in_sem, out_sems,
):
    incoming = pltpu.make_async_copy(arrived_ref.at[:, pl.ds(0, 128), :], pieces_ref, in_sem)
    incoming.start()

    def clear(index, carry):
        where = pl.ds(pl.multiple_of(index * 64, 64), 64)
        grid_a[where, :] = jnp.zeros((64, 128), F32)
        grid_b[where, :] = jnp.zeros((64, 128), F32)
        return carry

    lax.fori_loop(0, ROWS // 64, clear, 0)
    grid_a[pl.ds(ROWS, 8), :] = jnp.zeros((8, 128), F32)
    grid_b[pl.ds(ROWS, 8), :] = jnp.zeros((8, 128), F32)

    incoming.wait()
    sublane = lax.broadcasted_iota(jnp.int32, (8, 128), 0)
    lane = lax.broadcasted_iota(jnp.int32, (8, 128), 1)
    position = lane + (sublane // 2) * 128
    upper = sublane < 2

    def place(index, carry):
        source = index >> 3
        slot = (index & 7) * 8
        pieces = pieces_ref[source, pl.ds(pl.multiple_of(slot * 2, 16), 16), :].astype(F32)
        for part in range(2):
            block = pieces[8 * part : 8 * part + 8]
            turned = [block] + [pltpu.roll(block, 8 - 2 * turn, 0) for turn in (1, 2, 3)]
            for piece in range(4):
                both = jnp.where(upper, turned[piece], turned[(piece + 3) % 4])
                packed = place_ref[source, slot + part * 4 + piece]
                shift = packed & 127
                row = packed >> 7
                offset = position - shift
                inside = (offset >= 0) & (offset < 128)
                grid = grid_a if piece % 2 == 0 else grid_b
                window = pl.ds(row, 8)
                grid[window, :] = grid[window, :] + jnp.where(inside, both, 0.0)
        return carry

    lax.fori_loop(0, BANDS * SLOTS // 8, place, 0, unroll=4)

    first = first_ref[...]
    second = second_ref[...]
    cosine = twiddle_ref[0]
    sine = twiddle_ref[1]

    def band_step(band, carry):
        where = pl.ds(pl.multiple_of(band * 128, 128), 128)
        cells = grid_a[where, :] + grid_b[where, :]
        high = cells.astype(BF16)
        low = (cells - high.astype(F32)).astype(BF16)
        section = jnp.dot(
            first, jnp.concatenate([high, low, high], axis=0), preferred_element_type=F32
        )
        real = jnp.concatenate([section[:64], section[:64]], axis=0)
        imag = jnp.concatenate([section[64:], section[64:]], axis=0)
        turned = jnp.concatenate(
            [real * cosine - imag * sine, real * sine + imag * cosine], axis=1
        )
        high = turned.astype(BF16)
        low = (turned - high.astype(F32)).astype(BF16)
        contract = (((1,), (1,)), ((), ()))
        main = lax.dot_general(second, high, contract, preferred_element_type=F32)
        rest = lax.dot_general(second[:128], low, contract, preferred_element_type=F32)
        spectrum = main[:128] + main[128:] + rest
        rows_ref[pl.ds(band, 64, stride=STRIDE), :] = spectrum[:64]
        rows_ref[pl.ds(64 + band, 64, stride=STRIDE), :] = spectrum[64:]
        return carry

    lax.fori_loop(0, BANDS, band_step, 0, unroll=4)

    table = bands_ref[...]

    def block_step(index, carry):
        rows = rows_ref[pl.ds(index * STRIDE, 128), :].astype(BF16)
        section = jnp.dot(table, jnp.concatenate([rows, rows], axis=0), preferred_element_type=F32)
        section = section.astype(BF16)
        parts, _, length, _ = done_ref.shape
        for part in range(parts):
            done_ref[part, index] = section[length * part : length * part + length]
        return carry

    outgoing = []
    for group in range(4):
        lax.fori_loop(16 * group, 16 * group + 16, block_step, 0, unroll=4)
        where = pl.ds(16 * group, 16)
        copy = pltpu.make_async_copy(
            done_ref.at[:, where], out_ref.at[:, where], out_sems.at[group]
        )
        copy.start()
        outgoing.append(copy)
    for copy in outgoing:
        copy.wait()


def grid_and_rows(places, arrived, first, twiddle, second, bands):
    shape = (4, 64, 32, 128)
    vmem = pl.BlockSpec(memory_space=pltpu.VMEM)
    anywhere = pl.BlockSpec(memory_space=pl.ANY)
    return pl.pallas_call(
        grid_kernel,
        in_specs=[pl.BlockSpec(memory_space=pltpu.SMEM), anywhere, vmem, vmem, vmem, vmem],
        out_specs=anywhere,
        out_shape=jax.ShapeDtypeStruct(shape, BF16),
        scratch_shapes=[
            pltpu.VMEM((ROWS + 8, 128), F32),
            pltpu.VMEM((ROWS + 8, 128), F32),
            pltpu.VMEM((64 * STRIDE, 128), F32),
            pltpu.VMEM((64, 128, 128), BF16),
            pltpu.VMEM(shape, BF16),
            pltpu.SemaphoreType.DMA,
            pltpu.SemaphoreType.DMA((4,)),
        ],
        compiler_params=pltpu.CompilerParams(vmem_limit_bytes=62 * MIB),
        cost_estimate=pl.CostEstimate(flops=20_000_000_000, bytes_accessed=4 << 20, transcendentals=0),
        name="place_and_transform",
    )(places, arrived, first, twiddle, second, bands)


def base_phases(turn, me, w):
    k = jnp.arange(16, dtype=jnp.int32)[:, None, None]
    row = 64 * ((jnp.arange(128, dtype=jnp.int32)[:, None] + 32 * turn) % 128) + 16 * turn + k
    column = 128 * me + jnp.arange(128, dtype=jnp.int32)
    x = (row.astype(F32) - N // 2) / N
    y = (column.astype(F32) - N // 2) / N
    term = jnp.sqrt(1.0 - (x**2 + y**2)) - 1.0
    angle = (2.0 * math.pi) * w[:, None, None] * term[8]
    return jnp.stack([jnp.cos(angle), jnp.sin(angle)]), (term - term[8]).astype(BF16)


def transform_planes(table_ref, cells):
    sky = []
    for pair in (0, 2):
        both = jnp.concatenate([cells[pair], cells[pair + 1]], axis=1)
        sky.append(
            jnp.dot(
                table_ref[...], jnp.concatenate([both, both], axis=0), preferred_element_type=F32
            )
        )
    return sky


def add_planes(image, sky, where, change, w_ref, base_ref):
    for step in range(4):
        part = sky[step // 2][:, 128 * (step % 2) : 128 * (step % 2) + 128]
        real = part[:128][where]
        imag = part[128:][where]
        angle = (2.0 * math.pi * w_ref[step]) * change
        square = angle * angle
        sine = angle * (1.0 - square * (1.0 / 6.0))
        cosine = 1.0 - square * (0.5 - square * (1.0 / 24.0))
        image += (real * cosine - imag * sine) * base_ref[0, step, where]
        image -= (real * sine + imag * cosine) * base_ref[1, step, where]
    return image


def turn_rows(turn, rows_ref, columns_ref, half):
    for step in range(4):
        block = columns_ref[(turn - step) & 3, :, 16 * half : 16 * half + 16]
        rows_ref[step, 8 * half : 8 * half + 8] = jnp.swapaxes(block, 0, 1).reshape(8, 128, 128)


def early_kernel(turn_ref, w_ref, early_ref, table_ref, base_ref, change_ref, out_ref, rows_ref):
    for half in range(2):
        turn_rows(turn_ref[0], rows_ref, early_ref, half)

    def one(k, carry):
        sky = transform_planes(table_ref, [rows_ref[step, k] for step in range(4)])
        for block in range(4):
            where = slice(32 * block, 32 * block + 32)
            change = change_ref[k, where].astype(F32)
            out_ref[k, where] = add_planes(
                jnp.zeros((32, 128), F32), sky, where, change, w_ref, base_ref
            )
        return carry

    lax.fori_loop(0, 16, one, 0, unroll=2)


def early_image(turn, w, early, table, base, change):
    smem = pl.BlockSpec(memory_space=pltpu.SMEM)
    vmem = pl.BlockSpec(memory_space=pltpu.VMEM)
    return pl.pallas_call(
        early_kernel,
        in_specs=[smem] * 2 + [vmem] * 4,
        out_specs=vmem,
        out_shape=jax.ShapeDtypeStruct((16, 128, 128), F32),
        scratch_shapes=[pltpu.VMEM((4, 16, 128, 128), BF16)],
        compiler_params=pltpu.CompilerParams(vmem_limit_bytes=62 * MIB),
        cost_estimate=pl.CostEstimate(
            flops=2_200_000_000, bytes_accessed=5 << 20, transcendentals=0
        ),
        name="early_column_transform",
    )(turn, w, early, table, base, change)


def late_kernel(
    turn_ref, w_ref, early_hbm, late_hbm, table_hbm, base_hbm, change_hbm,
    own_hbm, sent_1, sent_2, sent_3, early_ref, late_ref, rows_ref, table_ref, base_ref, change_ref,
    own_ref, sent_ref, in_sems, out_sems,
):
    def fetch(half):
        k = pl.ds(8 * half, 8)
        pairs = pl.ds(16 * half, 16)
        moves = [
            (late_hbm.at[:, :, pairs], late_ref.at[:, :, pairs]),
            (early_hbm.at[k], early_ref.at[k]),
            (change_hbm.at[k], change_ref.at[k]),
        ]
        if half == 0:
            moves += [(table_hbm, table_ref), (base_hbm, base_ref)]
        copies = []
        for number, (source, target) in enumerate(moves):
            copy = pltpu.make_async_copy(source, target, in_sems.at[5 * half + number])
            copy.start()
            copies.append(copy)
        return copies

    def one(k, carry):
        sky = transform_planes(table_ref, [rows_ref[step, k] for step in range(4)])
        for block in range(4):
            where = slice(32 * block, 32 * block + 32)
            change = change_ref[k, where].astype(F32)
            image = add_planes(early_ref[k, where], sky, where, change, w_ref, base_ref)
            if block == 0:
                own_ref[k] = image
            else:
                sent_ref[block - 1, k] = image.astype(BF16)
        return carry

    turn = turn_ref[0]
    incoming = fetch(0)
    outgoing = []
    for half in range(2):
        for copy in incoming:
            copy.wait()
        if half == 0:
            incoming = fetch(1)
        turn_rows(turn, rows_ref, late_ref, half)
        lax.fori_loop(8 * half, 8 * half + 8, one, 0, unroll=4)
        k = pl.ds(8 * half, 8)
        moves = [(sent_ref.at[0, k], sent_1.at[k]), (sent_ref.at[1, k], sent_2.at[k])]
        moves += [(sent_ref.at[2, k], sent_3.at[k]), (own_ref.at[k], own_hbm.at[k])]
        for number, (source, target) in enumerate(moves):
            copy = pltpu.make_async_copy(source, target, out_sems.at[4 * half + number])
            copy.start()
            outgoing.append(copy)
    for copy in outgoing:
        copy.wait()


def late_image(turn, w, early, late, table, base, change):
    smem = pl.BlockSpec(memory_space=pltpu.SMEM)
    anywhere = pl.BlockSpec(memory_space=pl.ANY)
    return pl.pallas_call(
        late_kernel,
        in_specs=[smem] * 2 + [anywhere] * 5,
        out_specs=[anywhere] * 4,
        out_shape=[jax.ShapeDtypeStruct((16, 32, 128), F32)]
        + [jax.ShapeDtypeStruct((16, 32, 128), BF16)] * 3,
        scratch_shapes=[
            pltpu.VMEM((16, 128, 128), F32),
            pltpu.VMEM((4, 64, 32, 128), BF16),
            pltpu.VMEM((4, 16, 128, 128), BF16),
            pltpu.VMEM((256, 256), BF16),
            pltpu.VMEM((2, 4, 128, 128), F32),
            pltpu.VMEM((16, 128, 128), BF16),
            pltpu.VMEM((16, 32, 128), F32),
            pltpu.VMEM((3, 16, 32, 128), BF16),
            pltpu.SemaphoreType.DMA((10,)),
            pltpu.SemaphoreType.DMA((8,)),
        ],
        compiler_params=pltpu.CompilerParams(vmem_limit_bytes=62 * MIB),
        cost_estimate=pl.CostEstimate(
            flops=2_200_000_000, bytes_accessed=5 << 20, transcendentals=0
        ),
        name="late_column_transform",
    )(turn, w, early, late, table, base, change)


def place_kernel(turn_ref, *refs):
    out_ref = refs[-1]
    for step, block_ref in enumerate(refs[:-1]):
        begin = ((turn_ref[0] - step) & 3) * 16
        for group in (0, 8):
            rows = jnp.swapaxes(block_ref[group : group + 8].astype(F32), 0, 1)
            out_ref[:, pl.ds(pl.multiple_of(begin + group, 8), 8), :] = rows


def place_rows(turn, blocks):
    vmem = pl.BlockSpec(memory_space=pltpu.VMEM)
    return pl.pallas_call(
        place_kernel,
        in_specs=[pl.BlockSpec(memory_space=pltpu.SMEM)] + [vmem] * 4,
        out_specs=vmem,
        out_shape=jax.ShapeDtypeStruct((32, 64, 128), F32),
        compiler_params=pltpu.CompilerParams(vmem_limit_bytes=16 * MIB),
        cost_estimate=pl.CostEstimate(flops=1 << 20, bytes_accessed=2 << 20, transcendentals=0),
        name="place_image_rows",
    )(turn, *blocks)


def along_wp(block, step):
    pairs = [(plane, (plane + step) % 4) for plane in range(4)]
    return lax.ppermute(block, "wp", pairs)


def band_table(row):
    k = jnp.arange(64, dtype=jnp.int32)[:, None]
    band = jnp.arange(64, dtype=jnp.int32)[None, :]
    angle = (2.0 * math.pi / N) * ((k * (128 * band + row)) % N).astype(F32)
    cosine = jnp.cos(angle)
    sine = jnp.sin(angle)
    real = jnp.concatenate([cosine, -sine], axis=1)
    imag = jnp.concatenate([sine, cosine], axis=1)
    table = jnp.stack([real, imag], axis=1).reshape(128, 128)
    high = lax.reduce_precision(table, 8, 7)
    low = lax.reduce_precision(table - high, 8, 7)
    return jnp.concatenate([high, low], axis=1).astype(BF16)


def local(uv_tiles, target_bands, uv_offsets, tile_counts, plane_w):
    me = lax.axis_index("band")
    first = jnp.asarray(row_first_table())
    twiddle = jnp.asarray(row_twiddles())
    second = jnp.asarray(row_second_table())

    arrived = []
    for half in range(2):
        packed = pack(tile_counts, target_bands[0].T, uv_offsets[0].T, uv_tiles[0], half)
        arrived.append(
            lax.all_to_all(packed, "band", split_axis=0, concat_axis=0, tiled=True)
        )
    numbers = arrived[0][:, 128:131, :64].astype(jnp.int32)
    places = (numbers[:, 0] * 64 + numbers[:, 1]) * 256 + numbers[:, 2]
    turn = lax.axis_index("wp")[None]
    w = jnp.concatenate([plane_w, along_wp(plane_w, 1)])
    w = jnp.concatenate([w, along_wp(w, 2)])
    base, change = base_phases(turn[0], me, w)
    places, base, change = lax.optimization_barrier((places, base, change))

    columns = []
    for half in range(2):
        spectrum = grid_and_rows(
            places, arrived[half], first, twiddle, second, band_table(me + 64 * half)
        )
        columns.append(
            lax.all_to_all(
                spectrum.reshape(256, 32, 128), ("wp", "band"), split_axis=0, concat_axis=0, tiled=True
            ).reshape(4, 64, 32, 128)
        )

    tables = [
        jnp.roll(jnp.asarray(column_second_table(half)).reshape(2, 128, 256), -32 * turn[0], axis=1)
        for half in range(2)
    ]
    tables = [table.reshape(256, 256) for table in tables]
    early = early_image(turn, w, columns[0], tables[0], base, change)
    own, *sent = late_image(turn, w, early, columns[1], tables[1], base, change)
    blocks = [own] + [along_wp(block, step + 1) for step, block in enumerate(sent)]
    return place_rows(turn, blocks).reshape(2048, 128)


def solution(mesh):
    placed = (
        P("wp", "band", None, None, None),
        P("wp", "band", None),
        P("wp", "band", None),
        P("wp", "band"),
        P("wp"),
    )
    return jax.shard_map(
        local, mesh=mesh, in_specs=placed, out_specs=P("wp", "band"), check_vma=False
    )
```

```python
import functools
import math

import jax
import jax.numpy as jnp
import ml_dtypes
import numpy as np
from jax import lax
from jax.experimental import pallas as pl
from jax.experimental.pallas import tpu as pltpu
from jax.sharding import PartitionSpec as P

N = 8192
BANDS = 64
EDGE = 128
SLOTS = 64
ROWS = 8192
STRIDE = 129
F32 = jnp.float32
BF16 = jnp.bfloat16
MIB = 1 << 20


def circle(numerator, length):
    angle = 2.0 * np.pi * (np.asarray(numerator) % length) / length
    return np.cos(angle), np.sin(angle)


def split(table):
    high = table.astype(ml_dtypes.bfloat16)
    low = (table - high.astype(np.float64)).astype(ml_dtypes.bfloat16)
    return high, low


def row_first_table():
    cosine, sine = circle(np.arange(64)[:, None] * np.arange(64)[None, :], 64)
    table = np.zeros((2, 64, 64, 2))
    table[0, :, :, 0] = cosine
    table[0, :, :, 1] = -sine
    table[1, :, :, 0] = sine
    table[1, :, :, 1] = cosine
    high, low = split(table.reshape(128, 128))
    return np.concatenate([high, high, low], axis=1)


def row_twiddles():
    cosine, sine = circle(np.arange(128)[:, None] * np.arange(128)[None, :], N)
    return np.stack([cosine, sine]).astype(np.float32)


def row_second_table():
    cosine, sine = circle(np.arange(64)[:, None] * np.arange(128)[None, :], 64)
    table = np.block([[cosine, -sine], [sine, cosine]])
    high, low = split(table)
    return np.concatenate([high, low], axis=0)


def column_second_table():
    cosine, sine = circle(np.arange(128)[:, None] * np.arange(128)[None, :], 128)
    table = np.zeros((2, 128, 2, 2, 64))
    cosine = cosine.reshape(128, 2, 64) / N
    sine = sine.reshape(128, 2, 64) / N
    table[0, :, :, 0] = cosine
    table[0, :, :, 1] = -sine
    table[1, :, :, 0] = sine
    table[1, :, :, 1] = cosine
    high, low = split(table.reshape(256, 256))
    return np.concatenate([high, low], axis=1)


def pack_kernel(
    count_ref, band_ref, offset_ref, tiles_ref, out_ref, held_ref, rows_ref, done_ref, in_sems, out_sems,
    *, half
):
    groups = 8
    each = SLOTS // groups
    incoming = []
    for group in range(groups):
        where = pl.ds(each * group, each)
        copy = pltpu.make_async_copy(
            tiles_ref.at[where, :, pl.ds(64 * half, 64), :], held_ref.at[where], in_sems.at[group]
        )
        copy.start()
        incoming.append(copy)

    count = count_ref[0, 0]
    if half == 0:
        row = lax.broadcasted_iota(jnp.int32, (8, 128), 0)
        lane = lax.broadcasted_iota(jnp.int32, (8, 128), 1)

        def number(slot, values):
            column = offset_ref[1, slot]
            values = jnp.where((row == 0) & (lane == slot), band_ref[0, slot], values)
            values = jnp.where((row == 1) & (lane == slot), column >> 7, values)
            return jnp.where((row == 2) & (lane == slot), column & 127, values)

        values = lax.fori_loop(0, SLOTS, number, jnp.zeros((8, 128), jnp.int32), unroll=4)
        places = values.astype(F32).astype(BF16)

    def one(slot, carry):
        shift = offset_ref[1, slot] & 127
        keep = slot < count
        tile = pltpu.roll(held_ref[slot].astype(F32).reshape(128, 128), shift, 1)
        tile = jnp.where(keep, tile, 0.0)
        for part in range(2):
            where = pl.ds(slot * 2 + part, 64, stride=STRIDE)
            rows_ref[where, :] = tile[64 * part : 64 * part + 64]
        return carry

    for group in range(groups):
        incoming[group].wait()
        lax.fori_loop(each * group, each * group + each, one, 0, unroll=8)

    def cast(block, carry):
        done_ref[block, :128] = rows_ref[pl.ds(block * STRIDE, 128), :].astype(BF16)
        if half == 0:
            done_ref[block, 128:] = places
        return carry

    outgoing = []
    for group in range(4):
        lax.fori_loop(16 * group, 16 * group + 16, cast, 0, unroll=4)
        where = pl.ds(16 * group, 16)
        copy = pltpu.make_async_copy(done_ref.at[where], out_ref.at[where], out_sems.at[group])
        copy.start()
        outgoing.append(copy)
    for copy in outgoing:
        copy.wait()


def pack(count, bands, offsets, tiles, half):
    length = 128 if half else 136
    smem = pl.BlockSpec(memory_space=pltpu.SMEM)
    anywhere = pl.BlockSpec(memory_space=pl.ANY)
    return pl.pallas_call(
        functools.partial(pack_kernel, half=half),
        in_specs=[smem, smem, smem, anywhere],
        out_specs=anywhere,
        out_shape=jax.ShapeDtypeStruct((64, length, 128), BF16),
        scratch_shapes=[
            pltpu.VMEM((SLOTS, 2, 64, 128), BF16),
            pltpu.VMEM((64 * STRIDE, 128), F32),
            pltpu.VMEM((64, length, 128), BF16),
            pltpu.SemaphoreType.DMA((8,)),
            pltpu.SemaphoreType.DMA((4,)),
        ],
        compiler_params=pltpu.CompilerParams(vmem_limit_bytes=62 * MIB),
        cost_estimate=pl.CostEstimate(flops=8 << 20, bytes_accessed=4 << 20, transcendentals=0),
        name="pack_rows",
    )(count, bands, offsets, tiles)


def grid_kernel(
    place_ref, arrived_ref, first_ref, twiddle_ref, second_ref, bands_ref, out_ref,
    grid_a, grid_b, rows_ref, pieces_ref, done_ref, in_sem, out_sems,
):
    incoming = pltpu.make_async_copy(arrived_ref.at[:, pl.ds(0, 128), :], pieces_ref, in_sem)
    incoming.start()

    def clear(index, carry):
        where = pl.ds(pl.multiple_of(index * 64, 64), 64)
        grid_a[where, :] = jnp.zeros((64, 128), F32)
        grid_b[where, :] = jnp.zeros((64, 128), F32)
        return carry

    lax.fori_loop(0, ROWS // 64, clear, 0)
    grid_a[pl.ds(ROWS, 8), :] = jnp.zeros((8, 128), F32)
    grid_b[pl.ds(ROWS, 8), :] = jnp.zeros((8, 128), F32)

    incoming.wait()
    sublane = lax.broadcasted_iota(jnp.int32, (8, 128), 0)
    lane = lax.broadcasted_iota(jnp.int32, (8, 128), 1)
    position = lane + (sublane // 2) * 128
    upper = sublane < 2

    def place(index, carry):
        source = index >> 3
        slot = (index & 7) * 8
        pieces = pieces_ref[source, pl.ds(pl.multiple_of(slot * 2, 16), 16), :].astype(F32)
        for part in range(2):
            block = pieces[8 * part : 8 * part + 8]
            turned = [block] + [pltpu.roll(block, 8 - 2 * turn, 0) for turn in (1, 2, 3)]
            for piece in range(4):
                both = jnp.where(upper, turned[piece], turned[(piece + 3) % 4])
                packed = place_ref[source, slot + part * 4 + piece]
                shift = packed & 127
                row = packed >> 7
                offset = position - shift
                inside = (offset >= 0) & (offset < 128)
                grid = grid_a if piece % 2 == 0 else grid_b
                window = pl.ds(row, 8)
                grid[window, :] = grid[window, :] + jnp.where(inside, both, 0.0)
        return carry

    lax.fori_loop(0, BANDS * SLOTS // 8, place, 0, unroll=4)

    first = first_ref[...]
    second = second_ref[...]
    cosine = twiddle_ref[0]
    sine = twiddle_ref[1]

    def band_step(band, carry):
        where = pl.ds(pl.multiple_of(band * 128, 128), 128)
        cells = grid_a[where, :] + grid_b[where, :]
        high = cells.astype(BF16)
        low = (cells - high.astype(F32)).astype(BF16)
        section = jnp.dot(
            first, jnp.concatenate([high, low, high], axis=0), preferred_element_type=F32
        )
        real = jnp.concatenate([section[:64], section[:64]], axis=0)
        imag = jnp.concatenate([section[64:], section[64:]], axis=0)
        turned = jnp.concatenate(
            [real * cosine - imag * sine, real * sine + imag * cosine], axis=1
        )
        high = turned.astype(BF16)
        low = (turned - high.astype(F32)).astype(BF16)
        contract = (((1,), (1,)), ((), ()))
        main = lax.dot_general(second, high, contract, preferred_element_type=F32)
        rest = lax.dot_general(second[:128], low, contract, preferred_element_type=F32)
        spectrum = main[:128] + main[128:] + rest
        rows_ref[pl.ds(band, 64, stride=STRIDE), :] = spectrum[:64]
        rows_ref[pl.ds(64 + band, 64, stride=STRIDE), :] = spectrum[64:]
        return carry

    lax.fori_loop(0, BANDS, band_step, 0, unroll=4)

    table = bands_ref[...]

    def block_step(index, carry):
        rows = rows_ref[pl.ds(index * STRIDE, 128), :].astype(BF16)
        section = jnp.dot(table, jnp.concatenate([rows, rows], axis=0), preferred_element_type=F32)
        section = section.astype(BF16)
        parts, _, length, _ = done_ref.shape
        for part in range(parts):
            done_ref[part, index] = section[length * part : length * part + length]
        return carry

    outgoing = []
    for group in range(4):
        lax.fori_loop(16 * group, 16 * group + 16, block_step, 0, unroll=4)
        where = pl.ds(16 * group, 16)
        copy = pltpu.make_async_copy(
            done_ref.at[:, where], out_ref.at[:, where], out_sems.at[group]
        )
        copy.start()
        outgoing.append(copy)
    for copy in outgoing:
        copy.wait()


def grid_and_rows(places, arrived, first, twiddle, second, bands, parts):
    shape = (parts, 64, 128 // parts, 128)
    vmem = pl.BlockSpec(memory_space=pltpu.VMEM)
    anywhere = pl.BlockSpec(memory_space=pl.ANY)
    return pl.pallas_call(
        grid_kernel,
        in_specs=[pl.BlockSpec(memory_space=pltpu.SMEM), anywhere, vmem, vmem, vmem, vmem],
        out_specs=anywhere,
        out_shape=jax.ShapeDtypeStruct(shape, BF16),
        scratch_shapes=[
            pltpu.VMEM((ROWS + 8, 128), F32),
            pltpu.VMEM((ROWS + 8, 128), F32),
            pltpu.VMEM((64 * STRIDE, 128), F32),
            pltpu.VMEM((64, 128, 128), BF16),
            pltpu.VMEM(shape, BF16),
            pltpu.SemaphoreType.DMA,
            pltpu.SemaphoreType.DMA((4,)),
        ],
        compiler_params=pltpu.CompilerParams(vmem_limit_bytes=62 * MIB),
        cost_estimate=pl.CostEstimate(flops=20_000_000_000, bytes_accessed=4 << 20, transcendentals=0),
        name="place_and_transform",
    )(places, arrived, first, twiddle, second, bands)


def deal_kernel(turn_ref, columns_ref, *out_refs):
    for step, out_ref in enumerate(out_refs):
        begin = ((turn_ref[0] + step) & 3) * 32
        for group in range(2):
            where = pl.ds(pl.multiple_of(begin + 16 * group, 16), 16)
            rows = jnp.swapaxes(columns_ref[:, where, :], 0, 1).reshape(8, 128, 128)
            out_ref[8 * group : 8 * group + 8] = rows


def deal_rows(turn, columns):
    vmem = pl.BlockSpec(memory_space=pltpu.VMEM)
    return pl.pallas_call(
        deal_kernel,
        in_specs=[pl.BlockSpec(memory_space=pltpu.SMEM), vmem],
        out_specs=[vmem] * 4,
        out_shape=[jax.ShapeDtypeStruct((16, 128, 128), BF16)] * 4,
        compiler_params=pltpu.CompilerParams(vmem_limit_bytes=16 * MIB),
        cost_estimate=pl.CostEstimate(flops=1 << 20, bytes_accessed=4 << 20, transcendentals=0),
        name="deal_rows",
    )(turn, columns)


def base_phases(turn, me, w):
    k = jnp.arange(16, dtype=jnp.int32)[:, None, None]
    row = 64 * ((jnp.arange(128, dtype=jnp.int32)[:, None] + 32 * turn) % 128) + 16 * turn + k
    column = 128 * me + jnp.arange(128, dtype=jnp.int32)
    x = (row.astype(F32) - N // 2) / N
    y = (column.astype(F32) - N // 2) / N
    term = jnp.sqrt(1.0 - (x**2 + y**2)) - 1.0
    angle = (2.0 * math.pi) * w[:, None, None] * term[8]
    return jnp.stack([jnp.cos(angle), jnp.sin(angle)]), (term - term[8]).astype(BF16)


def column_kernel(
    turn_ref, w_ref, early_0, early_1, early_2, early_3, late_ref, table_ref, base_ref, change_ref,
    own_ref, sent_1, sent_2, sent_3, rows,
):
    turn = turn_ref[0]
    early = (early_0, early_1, early_2, early_3)
    targets = (own_ref, sent_1, sent_2, sent_3)

    def one(k, carry):
        sky = []
        for pair in (0, 2):
            cells = jnp.concatenate(
                [
                    jnp.concatenate([early[step][k], rows[step, k]], axis=0)
                    for step in (pair, pair + 1)
                ],
                axis=1,
            )
            sky.append(
                jnp.dot(
                    table_ref[...],
                    jnp.concatenate([cells, cells], axis=0),
                    preferred_element_type=F32,
                )
            )
        for block, target in enumerate(targets):
            where = slice(32 * block, 32 * block + 32)
            change = change_ref[k, where].astype(F32)
            image = jnp.zeros((32, 128), F32)
            for step in range(4):
                part = sky[step // 2][:, 128 * (step % 2) : 128 * (step % 2) + 128]
                real = part[:128][where]
                imag = part[128:][where]
                angle = (2.0 * math.pi * w_ref[step]) * change
                square = angle * angle
                sine = angle * (1.0 - square * (1.0 / 6.0))
                cosine = 1.0 - square * (0.5 - square * (1.0 / 24.0))
                image += (real * cosine - imag * sine) * base_ref[0, step, where]
                image -= (real * sine + imag * cosine) * base_ref[1, step, where]
            target[k] = image.astype(target.dtype)
        return carry

    for half in range(2):
        for step in range(4):
            block = late_ref[(turn - step) & 3, :, 16 * half : 16 * half + 16]
            rows[step, 8 * half : 8 * half + 8] = jnp.swapaxes(block, 0, 1).reshape(8, 128, 128)
        lax.fori_loop(8 * half, 8 * half + 8, one, 0, unroll=4)


def column_transform(turn, w, early, late, table, base, change):
    smem = pl.BlockSpec(memory_space=pltpu.SMEM)
    vmem = pl.BlockSpec(memory_space=pltpu.VMEM)
    return pl.pallas_call(
        column_kernel,
        in_specs=[smem] * 2 + [vmem] * 8,
        out_specs=[vmem] * 4,
        out_shape=[jax.ShapeDtypeStruct((16, 32, 128), F32)]
        + [jax.ShapeDtypeStruct((16, 32, 128), BF16)] * 3,
        scratch_shapes=[pltpu.VMEM((4, 16, 128, 128), BF16)],
        compiler_params=pltpu.CompilerParams(vmem_limit_bytes=16 * MIB),
        cost_estimate=pl.CostEstimate(
            flops=4_300_000_000, bytes_accessed=5 << 20, transcendentals=0
        ),
        name="column_transform",
    )(turn, w, *early, late, table, base, change)


def place_kernel(turn_ref, *refs):
    out_ref = refs[-1]
    for step, block_ref in enumerate(refs[:-1]):
        begin = ((turn_ref[0] - step) & 3) * 16
        for group in (0, 8):
            rows = jnp.swapaxes(block_ref[group : group + 8].astype(F32), 0, 1)
            out_ref[:, pl.ds(pl.multiple_of(begin + group, 8), 8), :] = rows


def place_rows(turn, blocks):
    vmem = pl.BlockSpec(memory_space=pltpu.VMEM)
    return pl.pallas_call(
        place_kernel,
        in_specs=[pl.BlockSpec(memory_space=pltpu.SMEM)] + [vmem] * 4,
        out_specs=vmem,
        out_shape=jax.ShapeDtypeStruct((32, 64, 128), F32),
        compiler_params=pltpu.CompilerParams(vmem_limit_bytes=16 * MIB),
        cost_estimate=pl.CostEstimate(flops=1 << 20, bytes_accessed=2 << 20, transcendentals=0),
        name="place_image_rows",
    )(turn, *blocks)


def along_wp(block, step):
    pairs = [(plane, (plane + step) % 4) for plane in range(4)]
    return lax.ppermute(block, "wp", pairs)


def band_table(row):
    k = jnp.arange(64, dtype=jnp.int32)[:, None]
    band = jnp.arange(64, dtype=jnp.int32)[None, :]
    angle = (2.0 * math.pi / N) * ((k * (128 * band + row)) % N).astype(F32)
    cosine = jnp.cos(angle)
    sine = jnp.sin(angle)
    real = jnp.concatenate([cosine, -sine], axis=1)
    imag = jnp.concatenate([sine, cosine], axis=1)
    table = jnp.stack([real, imag], axis=1).reshape(128, 128)
    high = lax.reduce_precision(table, 8, 7)
    low = lax.reduce_precision(table - high, 8, 7)
    return jnp.concatenate([high, low], axis=1).astype(BF16)


def local(uv_tiles, target_bands, uv_offsets, tile_counts, plane_w):
    me = lax.axis_index("band")
    first = jnp.asarray(row_first_table())
    twiddle = jnp.asarray(row_twiddles())
    second = jnp.asarray(row_second_table())

    arrived = []
    for half in range(2):
        packed = pack(tile_counts, target_bands[0].T, uv_offsets[0].T, uv_tiles[0], half)
        arrived.append(
            lax.all_to_all(packed, "band", split_axis=0, concat_axis=0, tiled=True)
        )
    numbers = arrived[0][:, 128:131, :64].astype(jnp.int32)
    places = (numbers[:, 0] * 64 + numbers[:, 1]) * 256 + numbers[:, 2]
    turn = lax.axis_index("wp")[None]
    w = jnp.concatenate([plane_w, along_wp(plane_w, 1)])
    w = jnp.concatenate([w, along_wp(w, 2)])
    base, change = base_phases(turn[0], me, w)
    places, base, change = lax.optimization_barrier((places, base, change))

    early = late = None
    for half in range(2):
        spectrum = grid_and_rows(
            places, arrived[half], first, twiddle, second, band_table(me + 64 * half), 4 if half else 1
        )
        if half == 0:
            early = lax.all_to_all(
                spectrum.reshape(64, 128, 128), "band", split_axis=0, concat_axis=0, tiled=True
            )
        else:
            late = lax.all_to_all(
                spectrum.reshape(256, 32, 128), ("wp", "band"), split_axis=0, concat_axis=0, tiled=True
            ).reshape(4, 64, 32, 128)

    dealt = deal_rows(turn, early)
    dealt = [dealt[0]] + [along_wp(dealt[step], step) for step in (1, 2, 3)]
    table = jnp.roll(jnp.asarray(column_second_table()).reshape(2, 128, 512), -32 * turn[0], axis=1)
    own, *sent = column_transform(
        turn, w, dealt, late, table.reshape(256, 512), base, change
    )
    blocks = [own] + [along_wp(block, step + 1) for step, block in enumerate(sent)]
    return place_rows(turn, blocks).reshape(2048, 128)


def solution(mesh):
    placed = (
        P("wp", "band", None, None, None),
        P("wp", "band", None),
        P("wp", "band", None),
        P("wp", "band"),
        P("wp"),
    )
    return jax.shard_map(
        local, mesh=mesh, in_specs=placed, out_specs=P("wp", "band"), check_vma=False
    )
```

```python
import functools
import math

import jax
import jax.numpy as jnp
import ml_dtypes
import numpy as np
from jax import lax
from jax.experimental import pallas as pl
from jax.experimental.pallas import tpu as pltpu
from jax.sharding import PartitionSpec as P

N = 8192
BANDS = 64
EDGE = 128
SLOTS = 64
ROWS = 8192
STRIDE = 129
F32 = jnp.float32
BF16 = jnp.bfloat16
MIB = 1 << 20


def circle(numerator, length):
    angle = 2.0 * np.pi * (np.asarray(numerator) % length) / length
    return np.cos(angle), np.sin(angle)


def split(table):
    high = table.astype(ml_dtypes.bfloat16)
    low = (table - high.astype(np.float64)).astype(ml_dtypes.bfloat16)
    return high, low


def row_first_table():
    cosine, sine = circle(np.arange(64)[:, None] * np.arange(64)[None, :], 64)
    table = np.zeros((2, 64, 64, 2))
    table[0, :, :, 0] = cosine
    table[0, :, :, 1] = -sine
    table[1, :, :, 0] = sine
    table[1, :, :, 1] = cosine
    high, low = split(table.reshape(128, 128))
    return np.concatenate([high, high, low], axis=1)


def row_twiddles():
    cosine, sine = circle(np.arange(128)[:, None] * np.arange(128)[None, :], N)
    return np.stack([cosine, sine]).astype(np.float32)


def row_second_table():
    cosine, sine = circle(np.arange(64)[:, None] * np.arange(128)[None, :], 64)
    table = np.block([[cosine, -sine], [sine, cosine]])
    high, low = split(table)
    return np.concatenate([high, low], axis=0)


def column_second_table():
    cosine, sine = circle(np.arange(128)[:, None] * np.arange(128)[None, :], 128)
    table = np.zeros((2, 128, 2, 2, 64))
    cosine = cosine.reshape(128, 2, 64) / N
    sine = sine.reshape(128, 2, 64) / N
    table[0, :, :, 0] = cosine
    table[0, :, :, 1] = -sine
    table[1, :, :, 0] = sine
    table[1, :, :, 1] = cosine
    high, low = split(table.reshape(256, 256))
    return np.concatenate([high, low], axis=1)


def pack_kernel(
    count_ref, band_ref, offset_ref, tiles_ref, out_ref, held_ref, rows_ref, done_ref, in_sems, out_sems,
    *, half
):
    groups = 8
    each = SLOTS // groups
    incoming = []
    for group in range(groups):
        where = pl.ds(each * group, each)
        copy = pltpu.make_async_copy(
            tiles_ref.at[where, :, pl.ds(64 * half, 64), :], held_ref.at[where], in_sems.at[group]
        )
        copy.start()
        incoming.append(copy)

    count = count_ref[0, 0]
    if half == 0:
        row = lax.broadcasted_iota(jnp.int32, (8, 128), 0)
        lane = lax.broadcasted_iota(jnp.int32, (8, 128), 1)

        def number(slot, values):
            column = offset_ref[1, slot]
            values = jnp.where((row == 0) & (lane == slot), band_ref[0, slot], values)
            values = jnp.where((row == 1) & (lane == slot), column >> 7, values)
            return jnp.where((row == 2) & (lane == slot), column & 127, values)

        values = lax.fori_loop(0, SLOTS, number, jnp.zeros((8, 128), jnp.int32), unroll=4)
        places = values.astype(F32).astype(BF16)

    def one(slot, carry):
        shift = offset_ref[1, slot] & 127
        keep = slot < count
        tile = pltpu.roll(held_ref[slot].astype(F32).reshape(128, 128), shift, 1)
        tile = jnp.where(keep, tile, 0.0)
        for part in range(2):
            where = pl.ds(slot * 2 + part, 64, stride=STRIDE)
            rows_ref[where, :] = tile[64 * part : 64 * part + 64]
        return carry

    for group in range(groups):
        incoming[group].wait()
        lax.fori_loop(each * group, each * group + each, one, 0, unroll=8)

    def cast(block, carry):
        done_ref[block, :128] = rows_ref[pl.ds(block * STRIDE, 128), :].astype(BF16)
        if half == 0:
            done_ref[block, 128:] = places
        return carry

    outgoing = []
    for group in range(4):
        lax.fori_loop(16 * group, 16 * group + 16, cast, 0, unroll=4)
        where = pl.ds(16 * group, 16)
        copy = pltpu.make_async_copy(done_ref.at[where], out_ref.at[where], out_sems.at[group])
        copy.start()
        outgoing.append(copy)
    for copy in outgoing:
        copy.wait()


def pack(count, bands, offsets, tiles, half):
    length = 128 if half else 136
    smem = pl.BlockSpec(memory_space=pltpu.SMEM)
    anywhere = pl.BlockSpec(memory_space=pl.ANY)
    return pl.pallas_call(
        functools.partial(pack_kernel, half=half),
        in_specs=[smem, smem, smem, anywhere],
        out_specs=anywhere,
        out_shape=jax.ShapeDtypeStruct((64, length, 128), BF16),
        scratch_shapes=[
            pltpu.VMEM((SLOTS, 2, 64, 128), BF16),
            pltpu.VMEM((65 * STRIDE + 7, 128), F32),
            pltpu.VMEM((64, length, 128), BF16),
            pltpu.SemaphoreType.DMA((8,)),
            pltpu.SemaphoreType.DMA((4,)),
        ],
        compiler_params=pltpu.CompilerParams(vmem_limit_bytes=62 * MIB),
        cost_estimate=pl.CostEstimate(flops=8 << 20, bytes_accessed=4 << 20, transcendentals=0),
        name="pack_rows",
    )(count, bands, offsets, tiles)


def grid_kernel(
    place_ref, arrived_ref, first_ref, twiddle_ref, second_ref, bands_ref, out_ref,
    grid_a, grid_b, rows_ref, pieces_ref, done_ref, in_sem, out_sems,
):
    incoming = pltpu.make_async_copy(arrived_ref.at[:, pl.ds(0, 128), :], pieces_ref, in_sem)
    incoming.start()

    def clear(index, carry):
        where = pl.ds(pl.multiple_of(index * 64, 64), 64)
        grid_a[where, :] = jnp.zeros((64, 128), F32)
        grid_b[where, :] = jnp.zeros((64, 128), F32)
        return carry

    lax.fori_loop(0, ROWS // 64, clear, 0)
    grid_a[pl.ds(ROWS, 8), :] = jnp.zeros((8, 128), F32)
    grid_b[pl.ds(ROWS, 8), :] = jnp.zeros((8, 128), F32)

    incoming.wait()
    sublane = lax.broadcasted_iota(jnp.int32, (8, 128), 0)
    lane = lax.broadcasted_iota(jnp.int32, (8, 128), 1)
    position = lane + (sublane // 2) * 128
    upper = sublane < 2

    def place(index, carry):
        source = index >> 3
        slot = (index & 7) * 8
        pieces = pieces_ref[source, pl.ds(pl.multiple_of(slot * 2, 16), 16), :].astype(F32)
        for part in range(2):
            block = pieces[8 * part : 8 * part + 8]
            turned = [block] + [pltpu.roll(block, 8 - 2 * turn, 0) for turn in (1, 2, 3)]
            for piece in range(4):
                both = jnp.where(upper, turned[piece], turned[(piece + 3) % 4])
                packed = place_ref[source, slot + part * 4 + piece]
                shift = packed & 127
                row = packed >> 7
                offset = position - shift
                inside = (offset >= 0) & (offset < 128)
                grid = grid_a if piece % 2 == 0 else grid_b
                window = pl.ds(row, 8)
                grid[window, :] = grid[window, :] + jnp.where(inside, both, 0.0)
        return carry

    lax.fori_loop(0, BANDS * SLOTS // 8, place, 0, unroll=4)

    first = first_ref[...]
    second = second_ref[...]
    cosine = twiddle_ref[0]
    sine = twiddle_ref[1]

    def band_step(band, carry):
        where = pl.ds(pl.multiple_of(band * 128, 128), 128)
        cells = grid_a[where, :] + grid_b[where, :]
        high = cells.astype(BF16)
        low = (cells - high.astype(F32)).astype(BF16)
        section = jnp.dot(
            first, jnp.concatenate([high, low, high], axis=0), preferred_element_type=F32
        )
        real = jnp.concatenate([section[:64], section[:64]], axis=0)
        imag = jnp.concatenate([section[64:], section[64:]], axis=0)
        turned = jnp.concatenate(
            [real * cosine - imag * sine, real * sine + imag * cosine], axis=1
        )
        high = turned.astype(BF16)
        low = (turned - high.astype(F32)).astype(BF16)
        contract = (((1,), (1,)), ((), ()))
        main = lax.dot_general(second, high, contract, preferred_element_type=F32)
        rest = lax.dot_general(second[:128], low, contract, preferred_element_type=F32)
        spectrum = main[:128] + main[128:] + rest
        rows_ref[pl.ds(band, 64, stride=STRIDE), :] = spectrum[:64]
        rows_ref[pl.ds(64 + band, 64, stride=STRIDE), :] = spectrum[64:]
        return carry

    lax.fori_loop(0, BANDS, band_step, 0, unroll=4)

    table = bands_ref[...]

    def block_step(index, carry):
        rows = rows_ref[pl.ds(index * STRIDE, 128), :].astype(BF16)
        section = jnp.dot(table, jnp.concatenate([rows, rows], axis=0), preferred_element_type=F32)
        section = section.astype(BF16)
        parts, _, length, _ = done_ref.shape
        for part in range(parts):
            done_ref[part, index] = section[length * part : length * part + length]
        return carry

    outgoing = []
    for group in range(4):
        lax.fori_loop(16 * group, 16 * group + 16, block_step, 0, unroll=4)
        where = pl.ds(16 * group, 16)
        copy = pltpu.make_async_copy(
            done_ref.at[:, where], out_ref.at[:, where], out_sems.at[group]
        )
        copy.start()
        outgoing.append(copy)
    for copy in outgoing:
        copy.wait()


def grid_and_rows(places, arrived, first, twiddle, second, bands, parts):
    shape = (parts, 64, 128 // parts, 128)
    vmem = pl.BlockSpec(memory_space=pltpu.VMEM)
    anywhere = pl.BlockSpec(memory_space=pl.ANY)
    return pl.pallas_call(
        grid_kernel,
        in_specs=[pl.BlockSpec(memory_space=pltpu.SMEM), anywhere, vmem, vmem, vmem, vmem],
        out_specs=anywhere,
        out_shape=jax.ShapeDtypeStruct(shape, BF16),
        scratch_shapes=[
            pltpu.VMEM((ROWS + 8, 128), F32),
            pltpu.VMEM((ROWS + 8, 128), F32),
            pltpu.VMEM((65 * STRIDE + 7, 128), F32),
            pltpu.VMEM((64, 128, 128), BF16),
            pltpu.VMEM(shape, BF16),
            pltpu.SemaphoreType.DMA,
            pltpu.SemaphoreType.DMA((4,)),
        ],
        compiler_params=pltpu.CompilerParams(vmem_limit_bytes=62 * MIB),
        cost_estimate=pl.CostEstimate(flops=20_000_000_000, bytes_accessed=4 << 20, transcendentals=0),
        name="place_and_transform",
    )(places, arrived, first, twiddle, second, bands)


def deal_kernel(turn_ref, columns_ref, *refs):
    out_refs = refs[:4]
    rows_ref, sems = refs[4:]
    copies = []
    for step, out_ref in enumerate(out_refs):
        begin = ((turn_ref[0] + step) & 3) * 32
        for group in range(2):
            where = pl.ds(pl.multiple_of(begin + 16 * group, 16), 16)
            rows = jnp.swapaxes(columns_ref[:, where, :], 0, 1).reshape(8, 128, 128)
            rows_ref[step, 8 * group : 8 * group + 8] = rows
        copy = pltpu.make_async_copy(rows_ref.at[step], out_ref, sems.at[step])
        copy.start()
        copies.append(copy)
    for copy in copies:
        copy.wait()


def deal_rows(turn, columns):
    return pl.pallas_call(
        deal_kernel,
        in_specs=[pl.BlockSpec(memory_space=pltpu.SMEM), pl.BlockSpec(memory_space=pltpu.VMEM)],
        out_specs=[pl.BlockSpec(memory_space=pl.ANY)] * 4,
        out_shape=[jax.ShapeDtypeStruct((16, 128, 128), BF16)] * 4,
        scratch_shapes=[pltpu.VMEM((4, 16, 128, 128), BF16), pltpu.SemaphoreType.DMA((4,))],
        compiler_params=pltpu.CompilerParams(vmem_limit_bytes=62 * MIB),
        cost_estimate=pl.CostEstimate(flops=1 << 20, bytes_accessed=4 << 20, transcendentals=0),
        name="deal_rows",
    )(turn, columns)


def base_phases(turn, me, w):
    k = jnp.arange(16, dtype=jnp.int32)[:, None, None]
    row = 64 * ((jnp.arange(128, dtype=jnp.int32)[:, None] + 32 * turn) % 128) + 16 * turn + k
    column = 128 * me + jnp.arange(128, dtype=jnp.int32)
    x = (row.astype(F32) - N // 2) / N
    y = (column.astype(F32) - N // 2) / N
    term = jnp.sqrt(1.0 - (x**2 + y**2)) - 1.0
    angle = (2.0 * math.pi) * w[:, None, None] * term[8]
    return jnp.stack([jnp.cos(angle), jnp.sin(angle)]), (term - term[8]).astype(BF16)


def column_kernel(
    turn_ref, w_ref, early_0, early_1, early_2, early_3, late_ref, table_ref, base_ref, change_ref,
    own_ref, sent_1, sent_2, sent_3, rows, early, sems,
):
    incoming = []
    for half in range(2):
        where = pl.ds(8 * half, 8)
        for step, source in enumerate((early_0, early_1, early_2, early_3)):
            copy = pltpu.make_async_copy(
                source.at[where], early.at[step, where], sems.at[4 * half + step]
            )
            copy.start()
            incoming.append(copy)

    turn = turn_ref[0]
    targets = (own_ref, sent_1, sent_2, sent_3)

    def one(k, carry):
        sky = []
        for pair in (0, 2):
            cells = jnp.concatenate(
                [
                    jnp.concatenate([early[step, k], rows[step, k]], axis=0)
                    for step in (pair, pair + 1)
                ],
                axis=1,
            )
            sky.append(
                jnp.dot(
                    table_ref[...],
                    jnp.concatenate([cells, cells], axis=0),
                    preferred_element_type=F32,
                )
            )
        for block, target in enumerate(targets):
            where = slice(32 * block, 32 * block + 32)
            change = change_ref[k, where].astype(F32)
            image = jnp.zeros((32, 128), F32)
            for step in range(4):
                part = sky[step // 2][:, 128 * (step % 2) : 128 * (step % 2) + 128]
                real = part[:128][where]
                imag = part[128:][where]
                angle = (2.0 * math.pi * w_ref[step]) * change
                square = angle * angle
                sine = angle * (1.0 - square * (1.0 / 6.0))
                cosine = 1.0 - square * (0.5 - square * (1.0 / 24.0))
                image += (real * cosine - imag * sine) * base_ref[0, step, where]
                image -= (real * sine + imag * cosine) * base_ref[1, step, where]
            target[k] = image.astype(target.dtype)
        return carry

    for half in range(2):
        for step in range(4):
            block = late_ref[(turn - step) & 3, :, 16 * half : 16 * half + 16]
            rows[step, 8 * half : 8 * half + 8] = jnp.swapaxes(block, 0, 1).reshape(8, 128, 128)
        for copy in incoming[4 * half : 4 * half + 4]:
            copy.wait()
        lax.fori_loop(8 * half, 8 * half + 8, one, 0, unroll=4)


def column_transform(turn, w, early, late, table, base, change):
    smem = pl.BlockSpec(memory_space=pltpu.SMEM)
    vmem = pl.BlockSpec(memory_space=pltpu.VMEM)
    anywhere = pl.BlockSpec(memory_space=pl.ANY)
    return pl.pallas_call(
        column_kernel,
        in_specs=[smem] * 2 + [anywhere] * 4 + [vmem] * 4,
        out_specs=[vmem] * 4,
        out_shape=[jax.ShapeDtypeStruct((16, 32, 128), F32)]
        + [jax.ShapeDtypeStruct((16, 32, 128), BF16)] * 3,
        scratch_shapes=[
            pltpu.VMEM((4, 16, 128, 128), BF16),
            pltpu.VMEM((4, 16, 128, 128), BF16),
            pltpu.SemaphoreType.DMA((8,)),
        ],
        compiler_params=pltpu.CompilerParams(vmem_limit_bytes=16 * MIB),
        cost_estimate=pl.CostEstimate(
            flops=4_300_000_000, bytes_accessed=5 << 20, transcendentals=0
        ),
        name="column_transform",
    )(turn, w, *early, late, table, base, change)


def place_kernel(turn_ref, *refs):
    out_ref = refs[-1]
    for step, block_ref in enumerate(refs[:-1]):
        begin = ((turn_ref[0] - step) & 3) * 16
        for group in (0, 8):
            rows = jnp.swapaxes(block_ref[group : group + 8].astype(F32), 0, 1)
            out_ref[:, pl.ds(pl.multiple_of(begin + group, 8), 8), :] = rows


def place_rows(turn, blocks):
    vmem = pl.BlockSpec(memory_space=pltpu.VMEM)
    return pl.pallas_call(
        place_kernel,
        in_specs=[pl.BlockSpec(memory_space=pltpu.SMEM)] + [vmem] * 4,
        out_specs=vmem,
        out_shape=jax.ShapeDtypeStruct((32, 64, 128), F32),
        compiler_params=pltpu.CompilerParams(vmem_limit_bytes=16 * MIB),
        cost_estimate=pl.CostEstimate(flops=1 << 20, bytes_accessed=2 << 20, transcendentals=0),
        name="place_image_rows",
    )(turn, *blocks)


def along_wp(block, step):
    pairs = [(plane, (plane + step) % 4) for plane in range(4)]
    return lax.ppermute(block, "wp", pairs)


def band_table(row):
    k = jnp.arange(64, dtype=jnp.int32)[:, None]
    band = jnp.arange(64, dtype=jnp.int32)[None, :]
    angle = (2.0 * math.pi / N) * ((k * (128 * band + row)) % N).astype(F32)
    cosine = jnp.cos(angle)
    sine = jnp.sin(angle)
    real = jnp.concatenate([cosine, -sine], axis=1)
    imag = jnp.concatenate([sine, cosine], axis=1)
    table = jnp.stack([real, imag], axis=1).reshape(128, 128)
    high = lax.reduce_precision(table, 8, 7)
    low = lax.reduce_precision(table - high, 8, 7)
    return jnp.concatenate([high, low], axis=1).astype(BF16)


def local(uv_tiles, target_bands, uv_offsets, tile_counts, plane_w):
    me = lax.axis_index("band")
    first = jnp.asarray(row_first_table())
    twiddle = jnp.asarray(row_twiddles())
    second = jnp.asarray(row_second_table())

    arrived = []
    for half in range(2):
        packed = pack(tile_counts, target_bands[0].T, uv_offsets[0].T, uv_tiles[0], half)
        arrived.append(
            lax.all_to_all(packed, "band", split_axis=0, concat_axis=0, tiled=True)
        )
    numbers = arrived[0][:, 128:131, :64].astype(jnp.int32)
    places = (numbers[:, 0] * 64 + numbers[:, 1]) * 256 + numbers[:, 2]
    turn = lax.axis_index("wp")[None]
    w = jnp.concatenate([plane_w, along_wp(plane_w, 1)])
    w = jnp.concatenate([w, along_wp(w, 2)])
    base, change = base_phases(turn[0], me, w)
    places, base, change = lax.optimization_barrier((places, base, change))

    early = late = None
    for half in range(2):
        spectrum = grid_and_rows(
            places, arrived[half], first, twiddle, second, band_table(me + 64 * half), 4 if half else 1
        )
        if half == 0:
            early = lax.all_to_all(
                spectrum.reshape(64, 128, 128), "band", split_axis=0, concat_axis=0, tiled=True
            )
        else:
            late = lax.all_to_all(
                spectrum.reshape(256, 32, 128), ("wp", "band"), split_axis=0, concat_axis=0, tiled=True
            ).reshape(4, 64, 32, 128)

    dealt = deal_rows(turn, early)
    dealt = [dealt[0]] + [along_wp(dealt[step], step) for step in (1, 2, 3)]
    table = jnp.roll(jnp.asarray(column_second_table()).reshape(2, 128, 512), -32 * turn[0], axis=1)
    own, *sent = column_transform(
        turn, w, dealt, late, table.reshape(256, 512), base, change
    )
    blocks = [own] + [along_wp(block, step + 1) for step, block in enumerate(sent)]
    return place_rows(turn, blocks).reshape(2048, 128)


def solution(mesh):
    placed = (
        P("wp", "band", None, None, None),
        P("wp", "band", None),
        P("wp", "band", None),
        P("wp", "band"),
        P("wp"),
    )
    return jax.shard_map(
        local, mesh=mesh, in_specs=placed, out_specs=P("wp", "band"), check_vma=False
    )
```

```python
import functools
import math

import jax
import jax.numpy as jnp
import ml_dtypes
import numpy as np
from jax import lax
from jax.experimental import pallas as pl
from jax.experimental.pallas import tpu as pltpu
from jax.sharding import PartitionSpec as P

N = 8192
BANDS = 64
EDGE = 128
SLOTS = 64
ROWS = 8192
STRIDE = 129
F32 = jnp.float32
BF16 = jnp.bfloat16
MIB = 1 << 20


def circle(numerator, length):
    angle = 2.0 * np.pi * (np.asarray(numerator) % length) / length
    return np.cos(angle), np.sin(angle)


def split(table):
    high = table.astype(ml_dtypes.bfloat16)
    low = (table - high.astype(np.float64)).astype(ml_dtypes.bfloat16)
    return high, low


def row_first_table():
    cosine, sine = circle(np.arange(64)[:, None] * np.arange(64)[None, :], 64)
    table = np.zeros((2, 64, 64, 2))
    table[0, :, :, 0] = cosine
    table[0, :, :, 1] = -sine
    table[1, :, :, 0] = sine
    table[1, :, :, 1] = cosine
    high, low = split(table.reshape(128, 128))
    return np.concatenate([high, high, low], axis=1)


def row_twiddles():
    cosine, sine = circle(np.arange(128)[:, None] * np.arange(128)[None, :], N)
    return np.stack([cosine, sine]).astype(np.float32)


def row_second_table():
    cosine, sine = circle(np.arange(64)[:, None] * np.arange(128)[None, :], 64)
    table = np.block([[cosine, -sine], [sine, cosine]])
    high, low = split(table)
    return np.concatenate([high, low], axis=0)


def column_second_table():
    cosine, sine = circle(np.arange(128)[:, None] * np.arange(128)[None, :], 128)
    table = np.zeros((2, 128, 2, 2, 64))
    cosine = cosine.reshape(128, 2, 64) / N
    sine = sine.reshape(128, 2, 64) / N
    table[0, :, :, 0] = cosine
    table[0, :, :, 1] = -sine
    table[1, :, :, 0] = sine
    table[1, :, :, 1] = cosine
    high, low = split(table.reshape(256, 256))
    return np.concatenate([high, low], axis=1)


def pack_kernel(
    count_ref, band_ref, offset_ref, tiles_ref, out_ref, held_ref, rows_ref, done_ref, in_sems, out_sems,
    *, half
):
    groups = 8
    each = SLOTS // groups
    incoming = []
    for group in range(groups):
        where = pl.ds(each * group, each)
        copy = pltpu.make_async_copy(
            tiles_ref.at[where, :, pl.ds(64 * half, 64), :], held_ref.at[where], in_sems.at[group]
        )
        copy.start()
        incoming.append(copy)

    count = count_ref[0, 0]
    if half == 0:
        row = lax.broadcasted_iota(jnp.int32, (8, 128), 0)
        lane = lax.broadcasted_iota(jnp.int32, (8, 128), 1)

        def number(slot, values):
            column = offset_ref[1, slot]
            values = jnp.where((row == 0) & (lane == slot), band_ref[0, slot], values)
            values = jnp.where((row == 1) & (lane == slot), column >> 7, values)
            return jnp.where((row == 2) & (lane == slot), column & 127, values)

        values = lax.fori_loop(0, SLOTS, number, jnp.zeros((8, 128), jnp.int32), unroll=4)
        places = values.astype(F32).astype(BF16)

    def one(slot, carry):
        shift = offset_ref[1, slot] & 127
        keep = slot < count
        tile = pltpu.roll(held_ref[slot].astype(F32).reshape(128, 128), shift, 1)
        tile = jnp.where(keep, tile, 0.0)
        for part in range(2):
            where = pl.ds(slot * 2 + part, 64, stride=STRIDE)
            rows_ref[where, :] = tile[64 * part : 64 * part + 64]
        return carry

    for group in range(groups):
        incoming[group].wait()
        lax.fori_loop(each * group, each * group + each, one, 0, unroll=8)

    def cast(block, carry):
        done_ref[block, :128] = rows_ref[pl.ds(block * STRIDE, 128), :].astype(BF16)
        if half == 0:
            done_ref[block, 128:] = places
        return carry

    outgoing = []
    for group in range(4):
        lax.fori_loop(16 * group, 16 * group + 16, cast, 0, unroll=4)
        where = pl.ds(16 * group, 16)
        copy = pltpu.make_async_copy(done_ref.at[where], out_ref.at[where], out_sems.at[group])
        copy.start()
        outgoing.append(copy)
    for copy in outgoing:
        copy.wait()


def pack(count, bands, offsets, tiles, half):
    length = 128 if half else 136
    smem = pl.BlockSpec(memory_space=pltpu.SMEM)
    anywhere = pl.BlockSpec(memory_space=pl.ANY)
    return pl.pallas_call(
        functools.partial(pack_kernel, half=half),
        in_specs=[smem, smem, smem, anywhere],
        out_specs=anywhere,
        out_shape=jax.ShapeDtypeStruct((64, length, 128), BF16),
        scratch_shapes=[
            pltpu.VMEM((SLOTS, 2, 64, 128), BF16),
            pltpu.VMEM((65 * STRIDE + 7, 128), F32),
            pltpu.VMEM((64, length, 128), BF16),
            pltpu.SemaphoreType.DMA((8,)),
            pltpu.SemaphoreType.DMA((4,)),
        ],
        compiler_params=pltpu.CompilerParams(vmem_limit_bytes=62 * MIB),
        cost_estimate=pl.CostEstimate(flops=8 << 20, bytes_accessed=4 << 20, transcendentals=0),
        name="pack_rows",
    )(count, bands, offsets, tiles)


def grid_kernel(
    place_ref, arrived_ref, first_ref, twiddle_ref, second_ref, bands_ref, out_ref,
    grid_a, grid_b, rows_ref, pieces_ref, done_ref, in_sem, out_sems,
):
    incoming = pltpu.make_async_copy(arrived_ref.at[:, pl.ds(0, 128), :], pieces_ref, in_sem)
    incoming.start()

    def clear(index, carry):
        where = pl.ds(pl.multiple_of(index * 64, 64), 64)
        grid_a[where, :] = jnp.zeros((64, 128), F32)
        grid_b[where, :] = jnp.zeros((64, 128), F32)
        return carry

    lax.fori_loop(0, ROWS // 64, clear, 0)
    grid_a[pl.ds(ROWS, 8), :] = jnp.zeros((8, 128), F32)
    grid_b[pl.ds(ROWS, 8), :] = jnp.zeros((8, 128), F32)

    incoming.wait()
    sublane = lax.broadcasted_iota(jnp.int32, (8, 128), 0)
    lane = lax.broadcasted_iota(jnp.int32, (8, 128), 1)
    position = lane + (sublane // 2) * 128
    upper = sublane < 2

    def place(index, carry):
        source = index >> 3
        slot = (index & 7) * 8
        pieces = pieces_ref[source, pl.ds(pl.multiple_of(slot * 2, 16), 16), :].astype(F32)
        for part in range(2):
            block = pieces[8 * part : 8 * part + 8]
            turned = [block] + [pltpu.roll(block, 8 - 2 * turn, 0) for turn in (1, 2, 3)]
            for piece in range(4):
                both = jnp.where(upper, turned[piece], turned[(piece + 3) % 4])
                packed = place_ref[source, slot + part * 4 + piece]
                shift = packed & 127
                row = packed >> 7
                offset = position - shift
                inside = (offset >= 0) & (offset < 128)
                grid = grid_a if piece % 2 == 0 else grid_b
                window = pl.ds(row, 8)
                grid[window, :] = grid[window, :] + jnp.where(inside, both, 0.0)
        return carry

    lax.fori_loop(0, BANDS * SLOTS // 8, place, 0, unroll=4)

    first = first_ref[...]
    second = second_ref[...]
    cosine = twiddle_ref[0]
    sine = twiddle_ref[1]

    def band_step(band, carry):
        where = pl.ds(pl.multiple_of(band * 128, 128), 128)
        cells = grid_a[where, :] + grid_b[where, :]
        high = cells.astype(BF16)
        low = (cells - high.astype(F32)).astype(BF16)
        section = jnp.dot(
            first, jnp.concatenate([high, low, high], axis=0), preferred_element_type=F32
        )
        real = jnp.concatenate([section[:64], section[:64]], axis=0)
        imag = jnp.concatenate([section[64:], section[64:]], axis=0)
        turned = jnp.concatenate(
            [real * cosine - imag * sine, real * sine + imag * cosine], axis=1
        )
        high = turned.astype(BF16)
        low = (turned - high.astype(F32)).astype(BF16)
        contract = (((1,), (1,)), ((), ()))
        main = lax.dot_general(second, high, contract, preferred_element_type=F32)
        rest = lax.dot_general(second[:128], low, contract, preferred_element_type=F32)
        spectrum = main[:128] + main[128:] + rest
        rows_ref[pl.ds(band, 64, stride=STRIDE), :] = spectrum[:64]
        rows_ref[pl.ds(64 + band, 64, stride=STRIDE), :] = spectrum[64:]
        return carry

    lax.fori_loop(0, BANDS, band_step, 0, unroll=4)

    table = bands_ref[...]

    def block_step(index, carry):
        rows = rows_ref[pl.ds(index * STRIDE, 128), :].astype(BF16)
        section = jnp.dot(table, jnp.concatenate([rows, rows], axis=0), preferred_element_type=F32)
        section = section.astype(BF16)
        parts, _, length, _ = done_ref.shape
        for part in range(parts):
            done_ref[part, index] = section[length * part : length * part + length]
        return carry

    outgoing = []
    for group in range(4):
        lax.fori_loop(16 * group, 16 * group + 16, block_step, 0, unroll=4)
        where = pl.ds(16 * group, 16)
        copy = pltpu.make_async_copy(
            done_ref.at[:, where], out_ref.at[:, where], out_sems.at[group]
        )
        copy.start()
        outgoing.append(copy)
    for copy in outgoing:
        copy.wait()


def grid_and_rows(places, arrived, first, twiddle, second, bands, parts):
    shape = (parts, 64, 128 // parts, 128)
    vmem = pl.BlockSpec(memory_space=pltpu.VMEM)
    anywhere = pl.BlockSpec(memory_space=pl.ANY)
    return pl.pallas_call(
        grid_kernel,
        in_specs=[pl.BlockSpec(memory_space=pltpu.SMEM), anywhere, vmem, vmem, vmem, vmem],
        out_specs=anywhere,
        out_shape=jax.ShapeDtypeStruct(shape, BF16),
        scratch_shapes=[
            pltpu.VMEM((ROWS + 8, 128), F32),
            pltpu.VMEM((ROWS + 8, 128), F32),
            pltpu.VMEM((65 * STRIDE + 7, 128), F32),
            pltpu.VMEM((64, 128, 128), BF16),
            pltpu.VMEM(shape, BF16),
            pltpu.SemaphoreType.DMA,
            pltpu.SemaphoreType.DMA((4,)),
        ],
        compiler_params=pltpu.CompilerParams(vmem_limit_bytes=62 * MIB),
        cost_estimate=pl.CostEstimate(flops=20_000_000_000, bytes_accessed=4 << 20, transcendentals=0),
        name="place_and_transform",
    )(places, arrived, first, twiddle, second, bands)


def deal_kernel(turn_ref, columns_ref, *refs):
    out_refs = refs[:4]
    rows_ref, sems = refs[4:]
    copies = []
    for step, out_ref in enumerate(out_refs):
        begin = ((turn_ref[0] + step) & 3) * 32
        for group in range(2):
            where = pl.ds(pl.multiple_of(begin + 16 * group, 16), 16)
            rows = jnp.swapaxes(columns_ref[:, where, :], 0, 1).reshape(8, 128, 128)
            rows_ref[step, 8 * group : 8 * group + 8] = rows
        copy = pltpu.make_async_copy(rows_ref.at[step], out_ref, sems.at[step])
        copy.start()
        copies.append(copy)
    for copy in copies:
        copy.wait()


def deal_rows(turn, columns):
    return pl.pallas_call(
        deal_kernel,
        in_specs=[pl.BlockSpec(memory_space=pltpu.SMEM), pl.BlockSpec(memory_space=pltpu.VMEM)],
        out_specs=[pl.BlockSpec(memory_space=pl.ANY)] * 4,
        out_shape=[jax.ShapeDtypeStruct((16, 128, 128), BF16)] * 4,
        scratch_shapes=[pltpu.VMEM((4, 16, 128, 128), BF16), pltpu.SemaphoreType.DMA((4,))],
        compiler_params=pltpu.CompilerParams(vmem_limit_bytes=62 * MIB),
        cost_estimate=pl.CostEstimate(flops=1 << 20, bytes_accessed=4 << 20, transcendentals=0),
        name="deal_rows",
    )(turn, columns)


def base_phases(turn, me, w):
    k = jnp.arange(16, dtype=jnp.int32)[:, None, None]
    row = 64 * ((jnp.arange(128, dtype=jnp.int32)[:, None] + 32 * turn) % 128) + 16 * turn + k
    column = 128 * me + jnp.arange(128, dtype=jnp.int32)
    x = (row.astype(F32) - N // 2) / N
    y = (column.astype(F32) - N // 2) / N
    term = jnp.sqrt(1.0 - (x**2 + y**2)) - 1.0
    angle = (2.0 * math.pi) * w[:, None, None] * term[8]
    return jnp.stack([jnp.cos(angle), jnp.sin(angle)]), (term - term[8]).astype(BF16)


def column_kernel(
    turn_ref, w_ref, early_0, early_1, early_2, early_3, late_ref, table_ref, base_ref, change_ref,
    own_ref, sent_1, sent_2, sent_3, rows,
):
    turn = turn_ref[0]
    early = (early_0, early_1, early_2, early_3)
    targets = (own_ref, sent_1, sent_2, sent_3)

    def one(k, carry):
        sky = []
        for pair in (0, 2):
            cells = jnp.concatenate(
                [
                    jnp.concatenate([early[step][k], rows[step, k]], axis=0)
                    for step in (pair, pair + 1)
                ],
                axis=1,
            )
            sky.append(
                jnp.dot(
                    table_ref[...],
                    jnp.concatenate([cells, cells], axis=0),
                    preferred_element_type=F32,
                )
            )
        for block, target in enumerate(targets):
            where = slice(32 * block, 32 * block + 32)
            change = change_ref[k, where].astype(F32)
            image = jnp.zeros((32, 128), F32)
            for step in range(4):
                part = sky[step // 2][:, 128 * (step % 2) : 128 * (step % 2) + 128]
                real = part[:128][where]
                imag = part[128:][where]
                angle = (2.0 * math.pi * w_ref[step]) * change
                square = angle * angle
                sine = angle * (1.0 - square * (1.0 / 6.0))
                cosine = 1.0 - square * (0.5 - square * (1.0 / 24.0))
                image += (real * cosine - imag * sine) * base_ref[0, step, where]
                image -= (real * sine + imag * cosine) * base_ref[1, step, where]
            target[k] = image.astype(target.dtype)
        return carry

    for half in range(2):
        for step in range(4):
            block = late_ref[(turn - step) & 3, :, 16 * half : 16 * half + 16]
            rows[step, 8 * half : 8 * half + 8] = jnp.swapaxes(block, 0, 1).reshape(8, 128, 128)
        lax.fori_loop(8 * half, 8 * half + 8, one, 0, unroll=4)


def column_transform(turn, w, early, late, table, base, change):
    smem = pl.BlockSpec(memory_space=pltpu.SMEM)
    vmem = pl.BlockSpec(memory_space=pltpu.VMEM)
    return pl.pallas_call(
        column_kernel,
        in_specs=[smem] * 2 + [vmem] * 8,
        out_specs=[vmem] * 4,
        out_shape=[jax.ShapeDtypeStruct((16, 32, 128), F32)]
        + [jax.ShapeDtypeStruct((16, 32, 128), BF16)] * 3,
        scratch_shapes=[pltpu.VMEM((4, 16, 128, 128), BF16)],
        compiler_params=pltpu.CompilerParams(vmem_limit_bytes=16 * MIB),
        cost_estimate=pl.CostEstimate(
            flops=4_300_000_000, bytes_accessed=5 << 20, transcendentals=0
        ),
        name="column_transform",
    )(turn, w, *early, late, table, base, change)


def place_kernel(turn_ref, *refs):
    out_ref = refs[-1]
    for step, block_ref in enumerate(refs[:-1]):
        begin = ((turn_ref[0] - step) & 3) * 16
        for group in (0, 8):
            rows = jnp.swapaxes(block_ref[group : group + 8].astype(F32), 0, 1)
            out_ref[:, pl.ds(pl.multiple_of(begin + group, 8), 8), :] = rows


def place_rows(turn, blocks):
    vmem = pl.BlockSpec(memory_space=pltpu.VMEM)
    return pl.pallas_call(
        place_kernel,
        in_specs=[pl.BlockSpec(memory_space=pltpu.SMEM)] + [vmem] * 4,
        out_specs=vmem,
        out_shape=jax.ShapeDtypeStruct((32, 64, 128), F32),
        compiler_params=pltpu.CompilerParams(vmem_limit_bytes=16 * MIB),
        cost_estimate=pl.CostEstimate(flops=1 << 20, bytes_accessed=2 << 20, transcendentals=0),
        name="place_image_rows",
    )(turn, *blocks)


def along_wp(block, step):
    pairs = [(plane, (plane + step) % 4) for plane in range(4)]
    return lax.ppermute(block, "wp", pairs)


def band_table(row):
    k = jnp.arange(64, dtype=jnp.int32)[:, None]
    band = jnp.arange(64, dtype=jnp.int32)[None, :]
    angle = (2.0 * math.pi / N) * ((k * (128 * band + row)) % N).astype(F32)
    cosine = jnp.cos(angle)
    sine = jnp.sin(angle)
    real = jnp.concatenate([cosine, -sine], axis=1)
    imag = jnp.concatenate([sine, cosine], axis=1)
    table = jnp.stack([real, imag], axis=1).reshape(128, 128)
    high = lax.reduce_precision(table, 8, 7)
    low = lax.reduce_precision(table - high, 8, 7)
    return jnp.concatenate([high, low], axis=1).astype(BF16)


def local(uv_tiles, target_bands, uv_offsets, tile_counts, plane_w):
    me = lax.axis_index("band")
    first = jnp.asarray(row_first_table())
    twiddle = jnp.asarray(row_twiddles())
    second = jnp.asarray(row_second_table())

    arrived = []
    for half in range(2):
        packed = pack(tile_counts, target_bands[0].T, uv_offsets[0].T, uv_tiles[0], half)
        arrived.append(
            lax.all_to_all(packed, "band", split_axis=0, concat_axis=0, tiled=True)
        )
    numbers = arrived[0][:, 128:131, :64].astype(jnp.int32)
    places = (numbers[:, 0] * 64 + numbers[:, 1]) * 256 + numbers[:, 2]
    turn = lax.axis_index("wp")[None]
    w = jnp.concatenate([plane_w, along_wp(plane_w, 1)])
    w = jnp.concatenate([w, along_wp(w, 2)])
    base, change = base_phases(turn[0], me, w)
    places, base, change = lax.optimization_barrier((places, base, change))

    early = late = None
    for half in range(2):
        spectrum = grid_and_rows(
            places, arrived[half], first, twiddle, second, band_table(me + 64 * half), 4 if half else 1
        )
        if half == 0:
            early = lax.all_to_all(
                spectrum.reshape(64, 128, 128), "band", split_axis=0, concat_axis=0, tiled=True
            )
        else:
            late = lax.all_to_all(
                spectrum.reshape(256, 32, 128), ("wp", "band"), split_axis=0, concat_axis=0, tiled=True
            ).reshape(4, 64, 32, 128)

    dealt = deal_rows(turn, early)
    dealt = [dealt[0]] + [along_wp(dealt[step], step) for step in (1, 2, 3)]
    table = jnp.roll(jnp.asarray(column_second_table()).reshape(2, 128, 512), -32 * turn[0], axis=1)
    own, *sent = column_transform(
        turn, w, dealt, late, table.reshape(256, 512), base, change
    )
    blocks = [own] + [along_wp(block, step + 1) for step, block in enumerate(sent)]
    return place_rows(turn, blocks).reshape(2048, 128)


def solution(mesh):
    placed = (
        P("wp", "band", None, None, None),
        P("wp", "band", None),
        P("wp", "band", None),
        P("wp", "band"),
        P("wp"),
    )
    return jax.shard_map(
        local, mesh=mesh, in_specs=placed, out_specs=P("wp", "band"), check_vma=False
    )
```

```python
import functools
import math

import jax
import jax.numpy as jnp
import ml_dtypes
import numpy as np
from jax import lax
from jax.experimental import pallas as pl
from jax.experimental.pallas import tpu as pltpu
from jax.sharding import PartitionSpec as P

N = 8192
BANDS = 64
EDGE = 128
SLOTS = 64
ROWS = 8192
STRIDE = 129
F32 = jnp.float32
BF16 = jnp.bfloat16
MIB = 1 << 20


def circle(numerator, length):
    angle = 2.0 * np.pi * (np.asarray(numerator) % length) / length
    return np.cos(angle), np.sin(angle)


def split(table):
    high = table.astype(ml_dtypes.bfloat16)
    low = (table - high.astype(np.float64)).astype(ml_dtypes.bfloat16)
    return high, low


def row_first_table():
    cosine, sine = circle(np.arange(64)[:, None] * np.arange(64)[None, :], 64)
    table = np.zeros((2, 64, 64, 2))
    table[0, :, :, 0] = cosine
    table[0, :, :, 1] = -sine
    table[1, :, :, 0] = sine
    table[1, :, :, 1] = cosine
    high, low = split(table.reshape(128, 128))
    return np.concatenate([high, high, low], axis=1)


def row_twiddles():
    cosine, sine = circle(np.arange(128)[:, None] * np.arange(128)[None, :], N)
    return np.stack([cosine, sine]).astype(np.float32)


def row_second_table():
    cosine, sine = circle(np.arange(64)[:, None] * np.arange(128)[None, :], 64)
    table = np.block([[cosine, -sine], [sine, cosine]])
    high, low = split(table)
    return np.concatenate([high, low], axis=0)


def column_second_table():
    cosine, sine = circle(np.arange(128)[:, None] * np.arange(128)[None, :], 128)
    table = np.zeros((2, 128, 2, 2, 64))
    cosine = cosine.reshape(128, 2, 64) / N
    sine = sine.reshape(128, 2, 64) / N
    table[0, :, :, 0] = cosine
    table[0, :, :, 1] = -sine
    table[1, :, :, 0] = sine
    table[1, :, :, 1] = cosine
    high, low = split(table.reshape(256, 256))
    return np.concatenate([high, low], axis=1)


def pack_kernel(
    count_ref, band_ref, offset_ref, tiles_ref, out_ref, held_ref, rows_ref, done_ref, in_sems, out_sems,
    *, half
):
    groups = 8
    each = SLOTS // groups
    incoming = []
    for group in range(groups):
        where = pl.ds(each * group, each)
        copy = pltpu.make_async_copy(
            tiles_ref.at[where, :, pl.ds(64 * half, 64), :], held_ref.at[where], in_sems.at[group]
        )
        copy.start()
        incoming.append(copy)

    count = count_ref[0, 0]
    if half == 0:
        row = lax.broadcasted_iota(jnp.int32, (8, 128), 0)
        lane = lax.broadcasted_iota(jnp.int32, (8, 128), 1)

        def number(slot, values):
            column = offset_ref[1, slot]
            values = jnp.where((row == 0) & (lane == slot), band_ref[0, slot], values)
            values = jnp.where((row == 1) & (lane == slot), column >> 7, values)
            return jnp.where((row == 2) & (lane == slot), column & 127, values)

        values = lax.fori_loop(0, SLOTS, number, jnp.zeros((8, 128), jnp.int32), unroll=4)
        places = values.astype(F32).astype(BF16)

    def one(slot, carry):
        shift = offset_ref[1, slot] & 127
        keep = slot < count
        tile = pltpu.roll(held_ref[slot].astype(F32).reshape(128, 128), shift, 1)
        tile = jnp.where(keep, tile, 0.0)
        for part in range(2):
            where = pl.ds(slot * 2 + part, 64, stride=STRIDE)
            rows_ref[where, :] = tile[64 * part : 64 * part + 64]
        return carry

    for group in range(groups):
        incoming[group].wait()
        lax.fori_loop(each * group, each * group + each, one, 0, unroll=8)

    def cast(block, carry):
        done_ref[block, :128] = rows_ref[pl.ds(block * STRIDE, 128), :].astype(BF16)
        if half == 0:
            done_ref[block, 128:] = places
        return carry

    outgoing = []
    for group in range(4):
        lax.fori_loop(16 * group, 16 * group + 16, cast, 0, unroll=4)
        where = pl.ds(16 * group, 16)
        copy = pltpu.make_async_copy(done_ref.at[where], out_ref.at[where], out_sems.at[group])
        copy.start()
        outgoing.append(copy)
    for copy in outgoing:
        copy.wait()


def pack(count, bands, offsets, tiles, half):
    length = 128 if half else 136
    smem = pl.BlockSpec(memory_space=pltpu.SMEM)
    anywhere = pl.BlockSpec(memory_space=pl.ANY)
    return pl.pallas_call(
        functools.partial(pack_kernel, half=half),
        in_specs=[smem, smem, smem, anywhere],
        out_specs=anywhere,
        out_shape=jax.ShapeDtypeStruct((64, length, 128), BF16),
        scratch_shapes=[
            pltpu.VMEM((SLOTS, 2, 64, 128), BF16),
            pltpu.VMEM((65 * STRIDE + 7, 128), F32),
            pltpu.VMEM((64, length, 128), BF16),
            pltpu.SemaphoreType.DMA((8,)),
            pltpu.SemaphoreType.DMA((4,)),
        ],
        compiler_params=pltpu.CompilerParams(vmem_limit_bytes=62 * MIB),
        cost_estimate=pl.CostEstimate(flops=8 << 20, bytes_accessed=4 << 20, transcendentals=0),
        name="pack_rows",
    )(count, bands, offsets, tiles)


def grid_kernel(
    place_ref, arrived_ref, first_ref, twiddle_ref, second_ref, bands_ref, out_ref,
    grid_a, grid_b, rows_ref, pieces_ref, done_ref, in_sem, out_sems,
):
    incoming = pltpu.make_async_copy(arrived_ref.at[:, pl.ds(0, 128), :], pieces_ref, in_sem)
    incoming.start()

    def clear(index, carry):
        where = pl.ds(pl.multiple_of(index * 64, 64), 64)
        grid_a[where, :] = jnp.zeros((64, 128), F32)
        grid_b[where, :] = jnp.zeros((64, 128), F32)
        return carry

    lax.fori_loop(0, ROWS // 64, clear, 0)
    grid_a[pl.ds(ROWS, 8), :] = jnp.zeros((8, 128), F32)
    grid_b[pl.ds(ROWS, 8), :] = jnp.zeros((8, 128), F32)

    incoming.wait()
    sublane = lax.broadcasted_iota(jnp.int32, (8, 128), 0)
    lane = lax.broadcasted_iota(jnp.int32, (8, 128), 1)
    position = lane + (sublane // 2) * 128
    upper = sublane < 2

    def place(index, carry):
        source = index >> 3
        slot = (index & 7) * 8
        pieces = pieces_ref[source, pl.ds(pl.multiple_of(slot * 2, 16), 16), :].astype(F32)
        for part in range(2):
            block = pieces[8 * part : 8 * part + 8]
            turned = [block] + [pltpu.roll(block, 8 - 2 * turn, 0) for turn in (1, 2, 3)]
            for piece in range(4):
                both = jnp.where(upper, turned[piece], turned[(piece + 3) % 4])
                packed = place_ref[source, slot + part * 4 + piece]
                shift = packed & 127
                row = packed >> 7
                offset = position - shift
                inside = (offset >= 0) & (offset < 128)
                grid = grid_a if piece % 2 == 0 else grid_b
                window = pl.ds(row, 8)
                grid[window, :] = grid[window, :] + jnp.where(inside, both, 0.0)
        return carry

    lax.fori_loop(0, BANDS * SLOTS // 8, place, 0, unroll=4)

    first = first_ref[...]
    second = second_ref[...]
    cosine = twiddle_ref[0]
    sine = twiddle_ref[1]

    def band_step(band, carry):
        where = pl.ds(pl.multiple_of(band * 128, 128), 128)
        cells = grid_a[where, :] + grid_b[where, :]
        high = cells.astype(BF16)
        low = (cells - high.astype(F32)).astype(BF16)
        section = jnp.dot(
            first, jnp.concatenate([high, low, high], axis=0), preferred_element_type=F32
        )
        real = jnp.concatenate([section[:64], section[:64]], axis=0)
        imag = jnp.concatenate([section[64:], section[64:]], axis=0)
        turned = jnp.concatenate(
            [real * cosine - imag * sine, real * sine + imag * cosine], axis=1
        )
        high = turned.astype(BF16)
        low = (turned - high.astype(F32)).astype(BF16)
        contract = (((1,), (1,)), ((), ()))
        main = lax.dot_general(second, high, contract, preferred_element_type=F32)
        rest = lax.dot_general(second[:128], low, contract, preferred_element_type=F32)
        spectrum = main[:128] + main[128:] + rest
        rows_ref[pl.ds(band, 64, stride=STRIDE), :] = spectrum[:64]
        rows_ref[pl.ds(64 + band, 64, stride=STRIDE), :] = spectrum[64:]
        return carry

    lax.fori_loop(0, BANDS, band_step, 0, unroll=4)

    table = bands_ref[...]

    def block_step(index, carry):
        rows = rows_ref[pl.ds(index * STRIDE, 128), :].astype(BF16)
        section = jnp.dot(table, jnp.concatenate([rows, rows], axis=0), preferred_element_type=F32)
        section = section.astype(BF16)
        parts, _, length, _ = done_ref.shape
        for part in range(parts):
            done_ref[part, index] = section[length * part : length * part + length]
        return carry

    outgoing = []
    for group in range(4):
        lax.fori_loop(16 * group, 16 * group + 16, block_step, 0, unroll=4)
        where = pl.ds(16 * group, 16)
        copy = pltpu.make_async_copy(
            done_ref.at[:, where], out_ref.at[:, where], out_sems.at[group]
        )
        copy.start()
        outgoing.append(copy)
    for copy in outgoing:
        copy.wait()


def grid_and_rows(places, arrived, first, twiddle, second, bands, parts):
    shape = (parts, 64, 128 // parts, 128)
    vmem = pl.BlockSpec(memory_space=pltpu.VMEM)
    anywhere = pl.BlockSpec(memory_space=pl.ANY)
    return pl.pallas_call(
        grid_kernel,
        in_specs=[pl.BlockSpec(memory_space=pltpu.SMEM), anywhere, vmem, vmem, vmem, vmem],
        out_specs=anywhere,
        out_shape=jax.ShapeDtypeStruct(shape, BF16),
        scratch_shapes=[
            pltpu.VMEM((ROWS + 8, 128), F32),
            pltpu.VMEM((ROWS + 8, 128), F32),
            pltpu.VMEM((65 * STRIDE + 7, 128), F32),
            pltpu.VMEM((64, 128, 128), BF16),
            pltpu.VMEM(shape, BF16),
            pltpu.SemaphoreType.DMA,
            pltpu.SemaphoreType.DMA((4,)),
        ],
        compiler_params=pltpu.CompilerParams(vmem_limit_bytes=62 * MIB),
        cost_estimate=pl.CostEstimate(flops=20_000_000_000, bytes_accessed=4 << 20, transcendentals=0),
        name="place_and_transform",
    )(places, arrived, first, twiddle, second, bands)


def deal_kernel(turn_ref, columns_ref, *refs):
    out_refs = refs[:4]
    rows_ref, sems = refs[4:]
    copies = []
    for step, out_ref in enumerate(out_refs):
        begin = ((turn_ref[0] + step) & 3) * 32
        for group in range(2):
            where = pl.ds(pl.multiple_of(begin + 16 * group, 16), 16)
            rows = jnp.swapaxes(columns_ref[:, where, :], 0, 1).reshape(8, 128, 128)
            rows_ref[step, 8 * group : 8 * group + 8] = rows
        copy = pltpu.make_async_copy(rows_ref.at[step], out_ref, sems.at[step])
        copy.start()
        copies.append(copy)
    for copy in copies:
        copy.wait()


def deal_rows(turn, columns):
    return pl.pallas_call(
        deal_kernel,
        in_specs=[pl.BlockSpec(memory_space=pltpu.SMEM), pl.BlockSpec(memory_space=pltpu.VMEM)],
        out_specs=[pl.BlockSpec(memory_space=pl.ANY)] * 4,
        out_shape=[jax.ShapeDtypeStruct((16, 128, 128), BF16)] * 4,
        scratch_shapes=[pltpu.VMEM((4, 16, 128, 128), BF16), pltpu.SemaphoreType.DMA((4,))],
        compiler_params=pltpu.CompilerParams(vmem_limit_bytes=62 * MIB),
        cost_estimate=pl.CostEstimate(flops=1 << 20, bytes_accessed=4 << 20, transcendentals=0),
        name="deal_rows",
    )(turn, columns)


def base_phases(turn, me, w):
    k = jnp.arange(16, dtype=jnp.int32)[:, None, None]
    row = 64 * ((jnp.arange(128, dtype=jnp.int32)[:, None] + 32 * turn) % 128) + 16 * turn + k
    column = 128 * me + jnp.arange(128, dtype=jnp.int32)
    x = (row.astype(F32) - N // 2) / N
    y = (column.astype(F32) - N // 2) / N
    term = jnp.sqrt(1.0 - (x**2 + y**2)) - 1.0
    angle = (2.0 * math.pi) * w[:, None, None] * term[8]
    return jnp.stack([jnp.cos(angle), jnp.sin(angle)]), (term - term[8]).astype(BF16)


def column_kernel(
    turn_ref, w_ref, early_0, early_1, early_2, early_3, late_ref, table_ref, base_ref, change_ref,
    *refs, blocks,
):
    turn = turn_ref[0]
    *targets, rows = refs
    early = (early_0, early_1, early_2, early_3)
    height = 32 * len(blocks)

    def one(k, carry):
        sky = []
        for pair in (0, 2):
            cells = jnp.concatenate(
                [
                    jnp.concatenate([early[step][k], rows[step, k]], axis=0)
                    for step in (pair, pair + 1)
                ],
                axis=1,
            )
            sky.append(
                jnp.dot(
                    table_ref[...],
                    jnp.concatenate([cells, cells], axis=0),
                    preferred_element_type=F32,
                )
            )
        for place, (block, target) in enumerate(zip(blocks, targets)):
            where = slice(32 * block, 32 * block + 32)
            change = change_ref[k, where].astype(F32)
            image = jnp.zeros((32, 128), F32)
            for step in range(4):
                part = sky[step // 2][:, 128 * (step % 2) : 128 * (step % 2) + 128]
                real = part[32 * place : 32 * place + 32]
                imag = part[height + 32 * place : height + 32 * place + 32]
                angle = (2.0 * math.pi * w_ref[step]) * change
                square = angle * angle
                sine = angle * (1.0 - square * (1.0 / 6.0))
                cosine = 1.0 - square * (0.5 - square * (1.0 / 24.0))
                image += (real * cosine - imag * sine) * base_ref[0, step, where]
                image -= (real * sine + imag * cosine) * base_ref[1, step, where]
            target[k] = image.astype(target.dtype)
        return carry

    for half in range(2):
        for step in range(4):
            block = late_ref[(turn - step) & 3, :, 16 * half : 16 * half + 16]
            rows[step, 8 * half : 8 * half + 8] = jnp.swapaxes(block, 0, 1).reshape(8, 128, 128)
        lax.fori_loop(8 * half, 8 * half + 8, one, 0, unroll=4)


def column_transform(turn, w, early, late, table, base, change, blocks):
    table = table[:, 32 * blocks[0] : 32 * blocks[-1] + 32].reshape(64 * len(blocks), 512)
    smem = pl.BlockSpec(memory_space=pltpu.SMEM)
    vmem = pl.BlockSpec(memory_space=pltpu.VMEM)
    return pl.pallas_call(
        functools.partial(column_kernel, blocks=blocks),
        in_specs=[smem] * 2 + [vmem] * 8,
        out_specs=[vmem] * len(blocks),
        out_shape=[
            jax.ShapeDtypeStruct((16, 32, 128), BF16 if block else F32) for block in blocks
        ],
        scratch_shapes=[pltpu.VMEM((4, 16, 128, 128), BF16)],
        compiler_params=pltpu.CompilerParams(vmem_limit_bytes=16 * MIB),
        cost_estimate=pl.CostEstimate(
            flops=1_080_000_000 * len(blocks), bytes_accessed=5 << 20, transcendentals=0
        ),
        name="column_transform",
    )(turn, w, *early, late, table, base, change)


def place_kernel(turn_ref, *refs):
    out_ref = refs[-1]
    for step, block_ref in enumerate(refs[:-1]):
        begin = ((turn_ref[0] - step) & 3) * 16
        for group in (0, 8):
            rows = jnp.swapaxes(block_ref[group : group + 8].astype(F32), 0, 1)
            out_ref[:, pl.ds(pl.multiple_of(begin + group, 8), 8), :] = rows


def place_rows(turn, blocks):
    vmem = pl.BlockSpec(memory_space=pltpu.VMEM)
    return pl.pallas_call(
        place_kernel,
        in_specs=[pl.BlockSpec(memory_space=pltpu.SMEM)] + [vmem] * 4,
        out_specs=vmem,
        out_shape=jax.ShapeDtypeStruct((32, 64, 128), F32),
        compiler_params=pltpu.CompilerParams(vmem_limit_bytes=16 * MIB),
        cost_estimate=pl.CostEstimate(flops=1 << 20, bytes_accessed=2 << 20, transcendentals=0),
        name="place_image_rows",
    )(turn, *blocks)


def along_wp(block, step):
    pairs = [(plane, (plane + step) % 4) for plane in range(4)]
    return lax.ppermute(block, "wp", pairs)


def band_table(row):
    k = jnp.arange(64, dtype=jnp.int32)[:, None]
    band = jnp.arange(64, dtype=jnp.int32)[None, :]
    angle = (2.0 * math.pi / N) * ((k * (128 * band + row)) % N).astype(F32)
    cosine = jnp.cos(angle)
    sine = jnp.sin(angle)
    real = jnp.concatenate([cosine, -sine], axis=1)
    imag = jnp.concatenate([sine, cosine], axis=1)
    table = jnp.stack([real, imag], axis=1).reshape(128, 128)
    high = lax.reduce_precision(table, 8, 7)
    low = lax.reduce_precision(table - high, 8, 7)
    return jnp.concatenate([high, low], axis=1).astype(BF16)


def local(uv_tiles, target_bands, uv_offsets, tile_counts, plane_w):
    me = lax.axis_index("band")
    first = jnp.asarray(row_first_table())
    twiddle = jnp.asarray(row_twiddles())
    second = jnp.asarray(row_second_table())

    arrived = []
    for half in range(2):
        packed = pack(tile_counts, target_bands[0].T, uv_offsets[0].T, uv_tiles[0], half)
        arrived.append(
            lax.all_to_all(packed, "band", split_axis=0, concat_axis=0, tiled=True)
        )
    numbers = arrived[0][:, 128:131, :64].astype(jnp.int32)
    places = (numbers[:, 0] * 64 + numbers[:, 1]) * 256 + numbers[:, 2]
    turn = lax.axis_index("wp")[None]
    w = jnp.concatenate([plane_w, along_wp(plane_w, 1)])
    w = jnp.concatenate([w, along_wp(w, 2)])
    base, change = base_phases(turn[0], me, w)
    places, base, change = lax.optimization_barrier((places, base, change))

    early = late = None
    for half in range(2):
        spectrum = grid_and_rows(
            places, arrived[half], first, twiddle, second, band_table(me + 64 * half), 4 if half else 1
        )
        if half == 0:
            early = lax.all_to_all(
                spectrum.reshape(64, 128, 128), "band", split_axis=0, concat_axis=0, tiled=True
            )
        else:
            late = lax.all_to_all(
                spectrum.reshape(256, 32, 128), ("wp", "band"), split_axis=0, concat_axis=0, tiled=True
            ).reshape(4, 64, 32, 128)

    dealt = deal_rows(turn, early)
    dealt = [dealt[0]] + [along_wp(dealt[step], step) for step in (1, 2, 3)]
    table = jnp.roll(jnp.asarray(column_second_table()).reshape(2, 128, 512), -32 * turn[0], axis=1)
    operands = (turn, w, dealt, late, table, base, change)
    sent = column_transform(*operands, (1, 2, 3))
    blocks = [along_wp(block, step + 1) for step, block in enumerate(sent)]
    blocks = [*column_transform(*operands, (0,)), *blocks]
    return place_rows(turn, blocks).reshape(2048, 128)


def solution(mesh):
    placed = (
        P("wp", "band", None, None, None),
        P("wp", "band", None),
        P("wp", "band", None),
        P("wp", "band"),
        P("wp"),
    )
    return jax.shard_map(
        local, mesh=mesh, in_specs=placed, out_specs=P("wp", "band"), check_vma=False
    )
```

```python
import functools
import math

import jax
import jax.numpy as jnp
import ml_dtypes
import numpy as np
from jax import lax
from jax.experimental import pallas as pl
from jax.experimental.pallas import tpu as pltpu
from jax.sharding import PartitionSpec as P

N = 8192
BANDS = 64
EDGE = 128
SLOTS = 64
ROWS = 8192
STRIDE = 129
F32 = jnp.float32
BF16 = jnp.bfloat16
MIB = 1 << 20


def circle(numerator, length):
    angle = 2.0 * np.pi * (np.asarray(numerator) % length) / length
    return np.cos(angle), np.sin(angle)


def split(table):
    high = table.astype(ml_dtypes.bfloat16)
    low = (table - high.astype(np.float64)).astype(ml_dtypes.bfloat16)
    return high, low


def row_first_table():
    cosine, sine = circle(np.arange(64)[:, None] * np.arange(64)[None, :], 64)
    table = np.zeros((2, 64, 64, 2))
    table[0, :, :, 0] = cosine
    table[0, :, :, 1] = -sine
    table[1, :, :, 0] = sine
    table[1, :, :, 1] = cosine
    high, low = split(table.reshape(128, 128))
    return np.concatenate([high, high, low], axis=1)


def row_twiddles():
    cosine, sine = circle(np.arange(128)[:, None] * np.arange(128)[None, :], N)
    return np.stack([cosine, sine]).astype(np.float32)


def row_second_table():
    cosine, sine = circle(np.arange(64)[:, None] * np.arange(128)[None, :], 64)
    table = np.block([[cosine, -sine], [sine, cosine]])
    high, low = split(table)
    return np.concatenate([high, low], axis=0)


def column_second_table():
    cosine, sine = circle(np.arange(128)[:, None] * np.arange(128)[None, :], 128)
    table = np.zeros((2, 128, 2, 2, 64))
    cosine = cosine.reshape(128, 2, 64) / N
    sine = sine.reshape(128, 2, 64) / N
    table[0, :, :, 0] = cosine
    table[0, :, :, 1] = -sine
    table[1, :, :, 0] = sine
    table[1, :, :, 1] = cosine
    high, low = split(table.reshape(256, 256))
    return np.concatenate([high, low], axis=1)


def pack_kernel(
    count_ref, band_ref, offset_ref, tiles_ref, out_ref, held_ref, rows_ref, done_ref, in_sems, out_sems,
    *, half
):
    groups = 8
    each = SLOTS // groups
    incoming = []
    for group in range(groups):
        where = pl.ds(each * group, each)
        copy = pltpu.make_async_copy(
            tiles_ref.at[where, :, pl.ds(64 * half, 64), :], held_ref.at[where], in_sems.at[group]
        )
        copy.start()
        incoming.append(copy)

    count = count_ref[0, 0]
    if half == 0:
        row = lax.broadcasted_iota(jnp.int32, (8, 128), 0)
        lane = lax.broadcasted_iota(jnp.int32, (8, 128), 1)

        def number(slot, values):
            column = offset_ref[1, slot]
            values = jnp.where((row == 0) & (lane == slot), band_ref[0, slot], values)
            values = jnp.where((row == 1) & (lane == slot), column >> 7, values)
            return jnp.where((row == 2) & (lane == slot), column & 127, values)

        values = lax.fori_loop(0, SLOTS, number, jnp.zeros((8, 128), jnp.int32), unroll=4)
        places = values.astype(F32).astype(BF16)

    def one(slot, carry):
        shift = offset_ref[1, slot] & 127
        keep = slot < count
        tile = pltpu.roll(held_ref[slot].astype(F32).reshape(128, 128), shift, 1)
        tile = jnp.where(keep, tile, 0.0)
        for part in range(2):
            where = pl.ds(slot * 2 + part, 64, stride=STRIDE)
            rows_ref[where, :] = tile[64 * part : 64 * part + 64]
        return carry

    for group in range(groups):
        incoming[group].wait()
        lax.fori_loop(each * group, each * group + each, one, 0, unroll=8)

    def cast(block, carry):
        done_ref[block, :128] = rows_ref[pl.ds(block * STRIDE, 128), :].astype(BF16)
        if half == 0:
            done_ref[block, 128:] = places
        return carry

    outgoing = []
    for group in range(4):
        lax.fori_loop(16 * group, 16 * group + 16, cast, 0, unroll=4)
        where = pl.ds(16 * group, 16)
        copy = pltpu.make_async_copy(done_ref.at[where], out_ref.at[where], out_sems.at[group])
        copy.start()
        outgoing.append(copy)
    for copy in outgoing:
        copy.wait()


def pack(count, bands, offsets, tiles, half):
    length = 128 if half else 136
    smem = pl.BlockSpec(memory_space=pltpu.SMEM)
    anywhere = pl.BlockSpec(memory_space=pl.ANY)
    return pl.pallas_call(
        functools.partial(pack_kernel, half=half),
        in_specs=[smem, smem, smem, anywhere],
        out_specs=anywhere,
        out_shape=jax.ShapeDtypeStruct((64, length, 128), BF16),
        scratch_shapes=[
            pltpu.VMEM((SLOTS, 2, 64, 128), BF16),
            pltpu.VMEM((65 * STRIDE + 7, 128), F32),
            pltpu.VMEM((64, length, 128), BF16),
            pltpu.SemaphoreType.DMA((8,)),
            pltpu.SemaphoreType.DMA((4,)),
        ],
        compiler_params=pltpu.CompilerParams(vmem_limit_bytes=62 * MIB),
        cost_estimate=pl.CostEstimate(flops=8 << 20, bytes_accessed=4 << 20, transcendentals=0),
        name="pack_rows",
    )(count, bands, offsets, tiles)


def grid_kernel(
    place_ref, arrived_ref, first_ref, twiddle_ref, second_ref, bands_ref, out_ref,
    grid_a, grid_b, rows_ref, pieces_ref, done_ref, in_sem, out_sems,
):
    incoming = pltpu.make_async_copy(arrived_ref.at[:, pl.ds(0, 128), :], pieces_ref, in_sem)
    incoming.start()

    def clear(index, carry):
        where = pl.ds(pl.multiple_of(index * 64, 64), 64)
        grid_a[where, :] = jnp.zeros((64, 128), F32)
        grid_b[where, :] = jnp.zeros((64, 128), F32)
        return carry

    lax.fori_loop(0, ROWS // 64, clear, 0)
    grid_a[pl.ds(ROWS, 8), :] = jnp.zeros((8, 128), F32)
    grid_b[pl.ds(ROWS, 8), :] = jnp.zeros((8, 128), F32)

    incoming.wait()
    sublane = lax.broadcasted_iota(jnp.int32, (8, 128), 0)
    lane = lax.broadcasted_iota(jnp.int32, (8, 128), 1)
    position = lane + (sublane // 2) * 128
    upper = sublane < 2

    def place(index, carry):
        source = index >> 3
        slot = (index & 7) * 8
        pieces = pieces_ref[source, pl.ds(pl.multiple_of(slot * 2, 16), 16), :].astype(F32)
        for part in range(2):
            block = pieces[8 * part : 8 * part + 8]
            turned = [block] + [pltpu.roll(block, 8 - 2 * turn, 0) for turn in (1, 2, 3)]
            for piece in range(4):
                both = jnp.where(upper, turned[piece], turned[(piece + 3) % 4])
                packed = place_ref[source, slot + part * 4 + piece]
                shift = packed & 127
                row = packed >> 7
                offset = position - shift
                inside = (offset >= 0) & (offset < 128)
                grid = grid_a if piece % 2 == 0 else grid_b
                window = pl.ds(row, 8)
                grid[window, :] = grid[window, :] + jnp.where(inside, both, 0.0)
        return carry

    lax.fori_loop(0, BANDS * SLOTS // 8, place, 0, unroll=4)

    first = first_ref[...]
    second = second_ref[...]
    cosine = twiddle_ref[0]
    sine = twiddle_ref[1]

    def band_step(band, carry):
        where = pl.ds(pl.multiple_of(band * 128, 128), 128)
        cells = grid_a[where, :] + grid_b[where, :]
        high = cells.astype(BF16)
        low = (cells - high.astype(F32)).astype(BF16)
        section = jnp.dot(
            first, jnp.concatenate([high, low, high], axis=0), preferred_element_type=F32
        )
        real = jnp.concatenate([section[:64], section[:64]], axis=0)
        imag = jnp.concatenate([section[64:], section[64:]], axis=0)
        turned = jnp.concatenate(
            [real * cosine - imag * sine, real * sine + imag * cosine], axis=1
        )
        high = turned.astype(BF16)
        low = (turned - high.astype(F32)).astype(BF16)
        contract = (((1,), (1,)), ((), ()))
        main = lax.dot_general(second, high, contract, preferred_element_type=F32)
        rest = lax.dot_general(second[:128], low, contract, preferred_element_type=F32)
        spectrum = main[:128] + main[128:] + rest
        rows_ref[pl.ds(band, 64, stride=STRIDE), :] = spectrum[:64]
        rows_ref[pl.ds(64 + band, 64, stride=STRIDE), :] = spectrum[64:]
        return carry

    lax.fori_loop(0, BANDS, band_step, 0, unroll=4)

    table = bands_ref[...]

    def block_step(index, carry):
        rows = rows_ref[pl.ds(index * STRIDE, 128), :].astype(BF16)
        section = jnp.dot(table, jnp.concatenate([rows, rows], axis=0), preferred_element_type=F32)
        section = section.astype(BF16)
        parts, _, length, _ = done_ref.shape
        for part in range(parts):
            done_ref[part, index] = section[length * part : length * part + length]
        return carry

    outgoing = []
    for group in range(4):
        lax.fori_loop(16 * group, 16 * group + 16, block_step, 0, unroll=4)
        where = pl.ds(16 * group, 16)
        copy = pltpu.make_async_copy(
            done_ref.at[:, where], out_ref.at[:, where], out_sems.at[group]
        )
        copy.start()
        outgoing.append(copy)
    for copy in outgoing:
        copy.wait()


def grid_and_rows(places, arrived, first, twiddle, second, bands, parts):
    shape = (parts, 64, 128 // parts, 128)
    vmem = pl.BlockSpec(memory_space=pltpu.VMEM)
    anywhere = pl.BlockSpec(memory_space=pl.ANY)
    return pl.pallas_call(
        grid_kernel,
        in_specs=[pl.BlockSpec(memory_space=pltpu.SMEM), anywhere, vmem, vmem, vmem, vmem],
        out_specs=anywhere,
        out_shape=jax.ShapeDtypeStruct(shape, BF16),
        scratch_shapes=[
            pltpu.VMEM((ROWS + 8, 128), F32),
            pltpu.VMEM((ROWS + 8, 128), F32),
            pltpu.VMEM((65 * STRIDE + 7, 128), F32),
            pltpu.VMEM((64, 128, 128), BF16),
            pltpu.VMEM(shape, BF16),
            pltpu.SemaphoreType.DMA,
            pltpu.SemaphoreType.DMA((4,)),
        ],
        compiler_params=pltpu.CompilerParams(vmem_limit_bytes=62 * MIB),
        cost_estimate=pl.CostEstimate(flops=20_000_000_000, bytes_accessed=4 << 20, transcendentals=0),
        name="place_and_transform",
    )(places, arrived, first, twiddle, second, bands)


def deal_kernel(turn_ref, columns_ref, *refs):
    out_refs = refs[:4]
    rows_ref, sems = refs[4:]
    copies = []
    for step, out_ref in enumerate(out_refs):
        begin = ((turn_ref[0] + step) & 3) * 32
        for group in range(2):
            where = pl.ds(pl.multiple_of(begin + 16 * group, 16), 16)
            rows = jnp.swapaxes(columns_ref[:, where, :], 0, 1).reshape(8, 128, 128)
            rows_ref[step, 8 * group : 8 * group + 8] = rows
        copy = pltpu.make_async_copy(rows_ref.at[step], out_ref, sems.at[step])
        copy.start()
        copies.append(copy)
    for copy in copies:
        copy.wait()


def deal_rows(turn, columns):
    return pl.pallas_call(
        deal_kernel,
        in_specs=[pl.BlockSpec(memory_space=pltpu.SMEM), pl.BlockSpec(memory_space=pltpu.VMEM)],
        out_specs=[pl.BlockSpec(memory_space=pl.ANY)] * 4,
        out_shape=[jax.ShapeDtypeStruct((16, 128, 128), BF16)] * 4,
        scratch_shapes=[pltpu.VMEM((4, 16, 128, 128), BF16), pltpu.SemaphoreType.DMA((4,))],
        compiler_params=pltpu.CompilerParams(vmem_limit_bytes=62 * MIB),
        cost_estimate=pl.CostEstimate(flops=1 << 20, bytes_accessed=4 << 20, transcendentals=0),
        name="deal_rows",
    )(turn, columns)


def base_phases(turn, me, w):
    k = jnp.arange(16, dtype=jnp.int32)[:, None, None]
    row = 64 * ((jnp.arange(128, dtype=jnp.int32)[:, None] + 32 * turn) % 128) + 16 * turn + k
    column = 128 * me + jnp.arange(128, dtype=jnp.int32)
    x = (row.astype(F32) - N // 2) / N
    y = (column.astype(F32) - N // 2) / N
    term = jnp.sqrt(1.0 - (x**2 + y**2)) - 1.0
    angle = (2.0 * math.pi) * w[:, None, None] * term[8]
    return jnp.stack([jnp.cos(angle), jnp.sin(angle)]), (term - term[8]).astype(BF16)


def column_kernel(
    turn_ref, w_ref, early_0, early_1, early_2, early_3, late_ref, table_ref, base_ref, change_ref,
    *refs, blocks,
):
    turn = turn_ref[0]
    *targets, rows = refs
    early = (early_0, early_1, early_2, early_3)
    height = 32 * len(blocks)

    def one(k, carry):
        sky = []
        for pair in (0, 2):
            cells = jnp.concatenate(
                [
                    jnp.concatenate([early[step][k], rows[step, k]], axis=0)
                    for step in (pair, pair + 1)
                ],
                axis=1,
            )
            sky.append(
                jnp.dot(
                    table_ref[...],
                    jnp.concatenate([cells, cells], axis=0),
                    preferred_element_type=F32,
                )
            )
        for place, (block, target) in enumerate(zip(blocks, targets)):
            where = slice(32 * block, 32 * block + 32)
            change = change_ref[k, where].astype(F32)
            image = jnp.zeros((32, 128), F32)
            for step in range(4):
                part = sky[step // 2][:, 128 * (step % 2) : 128 * (step % 2) + 128]
                real = part[32 * place : 32 * place + 32]
                imag = part[height + 32 * place : height + 32 * place + 32]
                angle = (2.0 * math.pi * w_ref[step]) * change
                square = angle * angle
                sine = angle * (1.0 - square * (1.0 / 6.0))
                cosine = 1.0 - square * (0.5 - square * (1.0 / 24.0))
                image += (real * cosine - imag * sine) * base_ref[0, step, where]
                image -= (real * sine + imag * cosine) * base_ref[1, step, where]
            target[k] = image.astype(target.dtype)
        return carry

    for half in range(2):
        for step in range(4):
            block = late_ref[(turn - step) & 3, :, 16 * half : 16 * half + 16]
            rows[step, 8 * half : 8 * half + 8] = jnp.swapaxes(block, 0, 1).reshape(8, 128, 128)
        lax.fori_loop(8 * half, 8 * half + 8, one, 0, unroll=4)


def column_transform(turn, w, early, late, table, base, change, blocks):
    table = table[:, 32 * blocks[0] : 32 * blocks[-1] + 32].reshape(64 * len(blocks), 512)
    smem = pl.BlockSpec(memory_space=pltpu.SMEM)
    vmem = pl.BlockSpec(memory_space=pltpu.VMEM)
    return pl.pallas_call(
        functools.partial(column_kernel, blocks=blocks),
        in_specs=[smem] * 2 + [vmem] * 8,
        out_specs=[vmem] * len(blocks),
        out_shape=[
            jax.ShapeDtypeStruct((16, 32, 128), BF16 if block else F32) for block in blocks
        ],
        scratch_shapes=[pltpu.VMEM((4, 16, 128, 128), BF16)],
        compiler_params=pltpu.CompilerParams(vmem_limit_bytes=58 * MIB),
        cost_estimate=pl.CostEstimate(
            flops=1_080_000_000 * len(blocks), bytes_accessed=5 << 20, transcendentals=0
        ),
        name="column_transform",
    )(turn, w, *early, late, table, base, change)


def place_kernel(turn_ref, *refs):
    out_ref = refs[-1]
    for step, block_ref in enumerate(refs[:-1]):
        begin = ((turn_ref[0] - step) & 3) * 16
        for group in (0, 8):
            rows = jnp.swapaxes(block_ref[group : group + 8].astype(F32), 0, 1)
            out_ref[:, pl.ds(pl.multiple_of(begin + group, 8), 8), :] = rows


def place_rows(turn, blocks):
    vmem = pl.BlockSpec(memory_space=pltpu.VMEM)
    return pl.pallas_call(
        place_kernel,
        in_specs=[pl.BlockSpec(memory_space=pltpu.SMEM)] + [vmem] * 4,
        out_specs=vmem,
        out_shape=jax.ShapeDtypeStruct((32, 64, 128), F32),
        compiler_params=pltpu.CompilerParams(vmem_limit_bytes=16 * MIB),
        cost_estimate=pl.CostEstimate(flops=1 << 20, bytes_accessed=2 << 20, transcendentals=0),
        name="place_image_rows",
    )(turn, *blocks)


def along_wp(block, step):
    pairs = [(plane, (plane + step) % 4) for plane in range(4)]
    return lax.ppermute(block, "wp", pairs)


def band_table(row):
    k = jnp.arange(64, dtype=jnp.int32)[:, None]
    band = jnp.arange(64, dtype=jnp.int32)[None, :]
    angle = (2.0 * math.pi / N) * ((k * (128 * band + row)) % N).astype(F32)
    cosine = jnp.cos(angle)
    sine = jnp.sin(angle)
    real = jnp.concatenate([cosine, -sine], axis=1)
    imag = jnp.concatenate([sine, cosine], axis=1)
    table = jnp.stack([real, imag], axis=1).reshape(128, 128)
    high = lax.reduce_precision(table, 8, 7)
    low = lax.reduce_precision(table - high, 8, 7)
    return jnp.concatenate([high, low], axis=1).astype(BF16)


def local(uv_tiles, target_bands, uv_offsets, tile_counts, plane_w):
    me = lax.axis_index("band")
    first = jnp.asarray(row_first_table())
    twiddle = jnp.asarray(row_twiddles())
    second = jnp.asarray(row_second_table())

    arrived = []
    for half in range(2):
        packed = pack(tile_counts, target_bands[0].T, uv_offsets[0].T, uv_tiles[0], half)
        arrived.append(
            lax.all_to_all(packed, "band", split_axis=0, concat_axis=0, tiled=True)
        )
    numbers = arrived[0][:, 128:131, :64].astype(jnp.int32)
    places = (numbers[:, 0] * 64 + numbers[:, 1]) * 256 + numbers[:, 2]
    turn = lax.axis_index("wp")[None]
    w = jnp.concatenate([plane_w, along_wp(plane_w, 1)])
    w = jnp.concatenate([w, along_wp(w, 2)])
    base, change = base_phases(turn[0], me, w)
    places, base, change = lax.optimization_barrier((places, base, change))

    early = late = None
    for half in range(2):
        spectrum = grid_and_rows(
            places, arrived[half], first, twiddle, second, band_table(me + 64 * half), 4 if half else 1
        )
        if half == 0:
            early = lax.all_to_all(
                spectrum.reshape(64, 128, 128), "band", split_axis=0, concat_axis=0, tiled=True
            )
        else:
            late = lax.all_to_all(
                spectrum.reshape(256, 32, 128), ("wp", "band"), split_axis=0, concat_axis=0, tiled=True
            ).reshape(4, 64, 32, 128)

    dealt = deal_rows(turn, early)
    dealt = [dealt[0]] + [along_wp(dealt[step], step) for step in (1, 2, 3)]
    table = jnp.roll(jnp.asarray(column_second_table()).reshape(2, 128, 512), -32 * turn[0], axis=1)
    operands = (turn, w, dealt, late, table, base, change)
    sent = column_transform(*operands, (1, 2, 3))
    blocks = [along_wp(block, step + 1) for step, block in enumerate(sent)]
    blocks = [*column_transform(*operands, (0,)), *blocks]
    return place_rows(turn, blocks).reshape(2048, 128)


def solution(mesh):
    placed = (
        P("wp", "band", None, None, None),
        P("wp", "band", None),
        P("wp", "band", None),
        P("wp", "band"),
        P("wp"),
    )
    return jax.shard_map(
        local, mesh=mesh, in_specs=placed, out_specs=P("wp", "band"), check_vma=False
    )
```
